32 devices in a mesh: dp: 16 (over z, y, core), tensor: 2 (over x).
Axes of the slice: x: 2, y: 2, z: 4, core: 2. Of those that a mesh axis runs over, the one named last changes fastest.
Arguments:
- tokens: bfloat16 [16384, 1024], P(('dp', 'tensor')), may hold values from -6 to 6
- positions: int32 [16384], P('dp'), may hold values from 0 to 1023, as said below
- cotangent: bfloat16 [16384, 1024], P(('dp', 'tensor')), may hold values from -6 to 6
- w_qkv: bfloat16 [1024, 3072], P('dp', 'tensor'), may hold values from -0.1875 to 0.1875
- b_qkv: float32 [3072], P('tensor'), may hold values from -3 to 3
- w_dense: bfloat16 [1024, 1024], P('dp', 'tensor'), may hold values from -0.75 to 0.75
- b_dense: float32 [1024], replicated, may hold values from -3 to 3
- w_fc1: bfloat16 [1024, 4096], P('dp', 'tensor'), may hold values from -0.1875 to 0.1875
- b_fc1: float32 [4096], P('tensor'), may hold values from -3 to 3
- w_fc2: bfloat16 [1024, 4096], P('dp', 'tensor'), may hold values from -0.09375 to 0.09375
- b_fc2: float32 [1024], replicated, may hold values from -3 to 3
- norm1_gain: float32 [1024], replicated, may hold values from 0.25 to 1.75
- norm1_shift: float32 [1024], replicated, may hold values from -3 to 3
- norm2_gain: float32 [1024], replicated, may hold values from 0.25 to 1.75
- norm2_shift: float32 [1024], replicated, may hold values from -3 to 3
Outputs:
- output: bfloat16 [16384, 1024], P(('dp', 'tensor'))
- grad_tokens: bfloat16 [16384, 1024], P(('dp', 'tensor'))
- grad_w_qkv: float32 [1024, 3072], P('dp', 'tensor')
- grad_b_qkv: float32 [3072], P('tensor')
- grad_w_dense: float32 [1024, 1024], P('dp', 'tensor')
- grad_b_dense: float32 [1024], replicated
- grad_w_fc1: float32 [1024, 4096], P('dp', 'tensor')
- grad_b_fc1: float32 [4096], P('tensor')
- grad_w_fc2: float32 [1024, 4096], P('dp', 'tensor')
- grad_b_fc2: float32 [1024], replicated
- grad_norm1_gain: float32 [1024], replicated
- grad_norm1_shift: float32 [1024], replicated
- grad_norm2_gain: float32 [1024], replicated
- grad_norm2_shift: float32 [1024], replicated
The draws below stay inside these ranges and needn't reach their ends.
Inputs may be any that keep to these rules, and one draw needn't show every extreme that they name: `positions`: positions count up by one within a document and are 0 at each document's start; every sequence of 1024 tokens begins a document, and documents start at random places inside sequences; in one sequence, drawn from the seed, a single document fills all 1024 tokens.
All inputs are finite; a program needn't handle non-finite values.
Results may differ from the reference program's by a relative error of at most 0.0099.
Values may be sent and summed in bfloat16 or wider, within the bound.
No kernel may reach another device: no remote copies, remote signals or barrier semaphores. Data moves between devices by JAX's collectives and lax.ppermute only.
A program may use at most 192 MiB of HBM per device.

```python
import jax
import jax.numpy as jnp
from jax import lax

D = 1024
HEADS = 16
HEAD = 64
ROT = 16
FF = 4096
SEQ_LEN = 1024
TOKENS = 16384


def draw_positions(key, part):
    key = jax.random.fold_in(key, 11)
    mark_key = jax.random.fold_in(key, 1)
    pick_key = jax.random.fold_in(key, 2)
    seq_total = TOKENS // SEQ_LEN
    marks = jax.random.randint(mark_key, (seq_total, SEQ_LEN), 0, max(SEQ_LEN // 4, 2))
    chosen = jax.random.randint(pick_key, (), 0, seq_total)
    places = jnp.broadcast_to(jnp.arange(SEQ_LEN, dtype=jnp.int32)[None, :], (seq_total, SEQ_LEN))
    rows_index = jnp.broadcast_to(jnp.arange(seq_total, dtype=jnp.int32)[:, None], (seq_total, SEQ_LEN))
    breaks = (marks == 0) & (rows_index != chosen) | (places == 0)
    starts = jnp.where(breaks, places, 0).astype(jnp.int32)
    return (places - lax.cummax(starts, axis=1)).reshape(TOKENS).astype(jnp.int32)


def raised(drawn, stream_key, source, target, blocks, factor):
    owner, partner = [(jnp.arange(drawn.shape[axis_at]) // (drawn.shape[axis_at] // blocks)).reshape([-1 if axis == axis_at else 1 for axis in range(drawn.ndim)]) for axis_at in (source, target)]
    chosen = jax.random.permutation(stream_key, blocks)[partner]
    strong = (owner == chosen) | (owner == (partner + blocks // 2) % blocks)
    return jnp.where(strong, factor * drawn, drawn)


def block_levels(own_key, extent, shards, smallest, high):
    loudness, own = 1.0, jax.random.fold_in(own_key, 6)
    for axis_at, blocks in shards:
        steps = jnp.exp(jax.random.uniform(jax.random.fold_in(own, axis_at), (blocks,), jnp.float32, smallest / len(shards), high / len(shards)))
        loudness = loudness * jnp.repeat(steps, extent[axis_at] // blocks).reshape([-1 if axis == axis_at else 1 for axis in range(len(extent))])
    return loudness


def normal_values(stream_key, extent, scale, limit, cuts=(), kind=jnp.bfloat16):
    values = scale * jax.random.normal(stream_key, extent, jnp.float32)
    if cuts:
        values = values * block_levels(stream_key, extent, cuts, -0.22, 0.18)
    return jnp.clip(values, -limit, limit).astype(kind)


def gaussian_with(rng, shape, deviation, most, split, heavy, kind=jnp.bfloat16):
    drawn = deviation * jax.random.normal(rng, shape, jnp.float32)
    if split:
        drawn = drawn * block_levels(rng, shape, split, -0.22, 0.18)
    return jnp.clip(raised(drawn, jax.random.fold_in(rng, 3), *heavy), -most, most).astype(kind)


def setup_inputs(seed: int = 0) -> dict:
    keys = jax.random.split(jax.random.key(seed), 16)
    tokens = normal_values(keys[0], (TOKENS, D), 1.0, 6.0, ((0, 32),))
    positions = draw_positions(jax.random.fold_in(keys[15], 71), 0)
    cotangent = gaussian_with(keys[2], (TOKENS, D), 1.0, 6.0, ((0, 32),), (0, 1, 32, 2.75))
    w_qkv = normal_values(keys[3], (D, 3 * D), D ** -0.5, 0.1875, ((0, 16), (1, 2)))
    b_qkv = normal_values(keys[4], (3 * D,), 0.5, 3.0, ((0, 2),), jnp.float32)
    w_dense = normal_values(keys[5], (D, D), (D // 16) ** -0.5, 0.75, ((0, 16), (1, 2)))
    b_dense = normal_values(keys[6], (D,), 0.5, 3.0, (), jnp.float32)
    w_fc1 = normal_values(keys[7], (D, FF), D ** -0.5, 0.1875, ((0, 16), (1, 2)))
    b_fc1 = normal_values(keys[8], (FF,), 0.5, 3.0, ((0, 2),), jnp.float32)
    w_fc2 = normal_values(keys[9], (D, FF), FF ** -0.5, 0.09375, ((0, 16), (1, 2)))
    b_fc2 = normal_values(keys[10], (D,), 0.5, 3.0, (), jnp.float32)
    norm1_gain = jnp.clip(1.0 + 0.15 * jax.random.normal(keys[11], (D,), jnp.float32), 0.25, 1.75)
    norm1_shift = normal_values(keys[12], (D,), 0.5, 3.0, (), jnp.float32)
    norm2_gain = jnp.clip(1.0 + 0.15 * jax.random.normal(keys[13], (D,), jnp.float32), 0.25, 1.75)
    norm2_shift = normal_values(keys[14], (D,), 0.5, 3.0, (), jnp.float32)
    return {"tokens": tokens, "positions": positions, "cotangent": cotangent, "w_qkv": w_qkv, "b_qkv": b_qkv, "w_dense": w_dense, "b_dense": b_dense, "w_fc1": w_fc1, "b_fc1": b_fc1, "w_fc2": w_fc2, "b_fc2": b_fc2, "norm1_gain": norm1_gain, "norm1_shift": norm1_shift, "norm2_gain": norm2_gain, "norm2_shift": norm2_shift}


EPSILON = 1e-05

@jax.custom_vjp
def low(v):
    return lax.optimization_barrier(v.astype(jnp.bfloat16)).astype(jnp.float32)

@jax.custom_vjp
def low_back(v):
    return v

def low_keep(v):
    return (low(v), None)

def low_pass(kept, grad):
    return (grad,)

def back_keep(v):
    return (v, None)

def back_low(kept, grad):
    return (low(grad),)
low.defvjp(low_keep, low_pass)
low_back.defvjp(back_keep, back_low)

def matmul(first_op, second_op):
    return jnp.dot(first_op, second_op, precision=lax.Precision.HIGHEST, preferred_element_type=jnp.float32)

def normalize(vectors, gain, shift):
    row_mean = lax.optimization_barrier(jnp.mean(vectors, axis=-1, keepdims=True))
    centered = vectors - row_mean
    spread = lax.optimization_barrier(jnp.mean(centered * centered, axis=-1, keepdims=True))
    return centered * lax.rsqrt(spread + EPSILON) * gain + shift

def turn_tables(pos_rows):
    half_rot = ROT // 2
    frequencies = 10000.0 ** (-jnp.arange(half_rot, dtype=jnp.float32) / half_rot)
    angles = pos_rows.astype(jnp.float32)[:, None] * frequencies[None, :]
    return (jnp.cos(angles)[:, None, :], jnp.sin(angles)[:, None, :])

def rotate(vectors, cosine, sine_rows):
    half_rot = ROT // 2
    front_half = vectors[..., :half_rot]
    second = vectors[..., half_rot:ROT]
    remainder = vectors[..., ROT:]
    return jnp.concatenate([front_half * cosine - second * sine_rows, second * cosine + front_half * sine_rows, remainder], axis=-1)

def layer(tokens, params, cosine, sine_rows):
    w_qkv, b_qkv, w_dense, b_dense, w_fc1, b_fc1, w_fc2, b_fc2, gain_one, shift_one, gain_two, shift_two = params
    length = tokens.shape[0]
    normed1 = low(normalize(tokens, gain_one, shift_one))
    normed2 = low(normalize(tokens, gain_two, shift_two))
    mixed_qkv = low_back(matmul(normed1, w_qkv) + b_qkv).reshape(length, HEADS, 3, HEAD)
    queries = low(rotate(mixed_qkv[:, :, 0], cosine, sine_rows))
    key_rows = low(rotate(mixed_qkv[:, :, 1], cosine, sine_rows))
    value_rows = low(mixed_qkv[:, :, 2])
    scores = low_back(jnp.einsum('qhd,khd->hqk', queries, key_rows, precision=lax.Precision.HIGHEST) * HEAD ** (-0.5))
    causal = jnp.arange(length)[:, None] >= jnp.arange(length)[None, :]
    scores = jnp.where(causal[None], scores, -1e+30)
    probs_low = low(jax.nn.softmax(scores, axis=-1))
    attended = jnp.einsum('hqk,khd->qhd', probs_low, value_rows, precision=lax.Precision.HIGHEST).reshape(length, D)
    attended = low(low_back(attended))
    pre_act = low_back(matmul(normed2, w_fc1) + b_fc1)
    hidden = low(jax.nn.gelu(pre_act, approximate=False))
    return tokens + matmul(attended, w_dense.T) + matmul(hidden, w_fc2.T) + b_dense + b_fc2

def add_pair(first_op, second_op):
    return first_op + second_op

def reference(tokens, positions, cotangent, w_qkv, b_qkv, w_dense, b_dense, w_fc1, b_fc1, w_fc2, b_fc2, norm1_gain, norm1_shift, norm2_gain, norm2_shift):
    params = tuple((array.astype(jnp.float32) for array in (w_qkv, b_qkv, w_dense, b_dense, w_fc1, b_fc1, w_fc2, b_fc2, norm1_gain, norm1_shift, norm2_gain, norm2_shift)))
    seq_total = TOKENS // SEQ_LEN
    token_seqs = tokens.astype(jnp.float32).reshape(seq_total, SEQ_LEN, D)
    cot_seqs = cotangent.astype(jnp.float32).reshape(seq_total, SEQ_LEN, D)
    pos_seqs = positions.reshape(seq_total, SEQ_LEN)

    def advance(totals, inputs):
        seq_tokens, seq_cot, seq_pos = inputs
        cosine, sine_rows = turn_tables(seq_pos)

        def apply_layer(token_rows, layer_params):
            return layer(token_rows, layer_params, cosine, sine_rows)
        result, pullback = jax.vjp(apply_layer, seq_tokens, params)
        token_grad, param_grads = pullback(seq_cot)
        totals = jax.tree.map(add_pair, totals, param_grads)
        return (totals, (result.astype(jnp.bfloat16), token_grad.astype(jnp.bfloat16)))
    initial = jax.tree.map(jnp.zeros_like, params)
    totals, (outputs, token_grads) = lax.scan(advance, initial, (token_seqs, cot_seqs, pos_seqs))
    return (outputs.reshape(TOKENS, D), token_grads.reshape(TOKENS, D), totals[0], totals[1], totals[2], totals[3], totals[4], totals[5], totals[6], totals[7], totals[8], totals[9], totals[10], totals[11])
```

```python
import functools

import jax
import jax.numpy as jnp
from jax import lax
from jax.experimental import pallas as pl
from jax.experimental.pallas import tpu as pltpu
from jax.sharding import PartitionSpec as P

HEAD = 64
ROT = 16
SEQ_LEN = 1024
EPSILON = 1e-05
LANES = 128
BF = jnp.bfloat16
F32 = jnp.float32
NN = (((1,), (0,)), ((), ()))
NT = (((1,), (1,)), ((), ()))
TN = (((0,), (0,)), ((), ()))


def dot(first_op, second_op, dims=NN):
    return lax.dot_general(first_op, second_op, dims, preferred_element_type=F32)


def row_kernel(body, rows, block, row_ins, full_ins, row_outs, sum_outs, flops, vmem=40, index=None):
    steps = rows // block
    n_index = 0 if index is None else 1

    def at_row(step, *_):
        return (step, 0)

    def at_zero(step, *_):
        return (0, 0)

    in_specs = [pl.BlockSpec((block, x.shape[1]), at_row) for x in row_ins]
    in_specs += [pl.BlockSpec(x.shape, at_zero) for x in full_ins]
    out_specs = [pl.BlockSpec((block, cols), at_row) for cols, _ in row_outs]
    out_specs += [pl.BlockSpec((1, width), at_zero) for width in sum_outs]
    out_shape = [jax.ShapeDtypeStruct((rows, cols), kind) for cols, kind in row_outs]
    out_shape += [jax.ShapeDtypeStruct((1, width), F32) for width in sum_outs]
    n_in, n_out = len(in_specs), len(row_outs)

    def kernel(*refs):
        ins = refs[: n_index + n_in]
        outs = refs[n_index + n_in : n_index + n_in + n_out]
        sums = refs[n_index + n_in + n_out :]
        if sums:

            @pl.when(pl.program_id(0) == 0)
            def _():
                for ref in sums:
                    ref[...] = jnp.zeros_like(ref)

        body(ins, outs, sums)

    moved = sum(x.size * x.dtype.itemsize for x in (*row_ins, *full_ins))
    moved += sum(rows * cols * jnp.dtype(kind).itemsize for cols, kind in row_outs)
    return pl.pallas_call(
        kernel,
        grid_spec=pltpu.PrefetchScalarGridSpec(
            num_scalar_prefetch=n_index, grid=(steps,), in_specs=in_specs, out_specs=out_specs
        ),
        out_shape=out_shape,
        compiler_params=pltpu.CompilerParams(vmem_limit_bytes=vmem * 2**20),
        cost_estimate=pl.CostEstimate(flops=flops, bytes_accessed=moved, transcendentals=0),
    )(*(() if index is None else (index,)), *row_ins, *full_ins)


def moments(vectors):
    row_mean = jnp.mean(vectors, axis=-1, keepdims=True)
    centered = vectors - row_mean
    spread = jnp.mean(centered * centered, axis=-1, keepdims=True)
    return centered, lax.rsqrt(spread + EPSILON)


def pieces_kernel(body, pieces, index, full_ins, row_outs, block):
    count = len(pieces)
    piece_rows, width = pieces[0].shape
    per = piece_rows // block
    rows = count * piece_rows

    def at_piece(i):
        def f(step, _):
            return (jnp.clip(step - i * per, 0, per - 1), 0)

        return f

    def kernel(perm, *refs):
        ins, fulls = refs[:count], refs[count : count + len(full_ins)]
        outs = refs[count + len(full_ins) : count + len(full_ins) + len(row_outs)]
        scratch = refs[-1]
        which = pl.program_id(0) // per
        for i in range(count):

            @pl.when(which == i)
            def _(i=i):
                scratch[...] = ins[i][...].astype(F32)

        body(perm, fulls, outs, scratch)

    return pl.pallas_call(
        kernel,
        grid_spec=pltpu.PrefetchScalarGridSpec(
            num_scalar_prefetch=1,
            grid=(rows // block,),
            in_specs=[pl.BlockSpec((block, width), at_piece(i)) for i in range(count)]
            + [pl.BlockSpec(x.shape, lambda step, _: (0, 0)) for x in full_ins],
            out_specs=[pl.BlockSpec((block, width), lambda step, _: (step, 0)) for _ in row_outs],
            scratch_shapes=[pltpu.VMEM((block, width), F32)],
        ),
        out_shape=[jax.ShapeDtypeStruct((rows, width), kind) for kind in row_outs],
        compiler_params=pltpu.CompilerParams(vmem_limit_bytes=32 * 2**20),
        cost_estimate=pl.CostEstimate(
            flops=10 * rows * width, bytes_accessed=rows * width * (2 + 2 * len(row_outs)), transcendentals=0
        ),
    )(index, *pieces, *full_ins)


def block_at(perm, place, width, count):
    if count == 1:
        return pl.ds(0, width)
    return pl.ds(pl.multiple_of(perm[place] * width, width), width)


def norm_body(count, perm, fulls, outs, scratch):
    gain_one, shift_one, gain_two, shift_two = fulls
    normed1, normed2, standard = outs
    centered, inverse = moments(scratch[...])
    scratch[...] = centered * inverse
    width = scratch.shape[1] // count
    for p in range(count):
        here = slice(p * width, (p + 1) * width)
        part = scratch[:, block_at(perm, p, width, count)]
        normed1[:, here] = (part * gain_one[:, here] + shift_one[:, here]).astype(BF)
        normed2[:, here] = (part * gain_two[:, here] + shift_two[:, here]).astype(BF)
        standard[:, here] = part.astype(BF)


def turn_body(count, perm, fulls, outs, scratch):
    width = scratch.shape[1] // count
    for p in range(count):
        outs[0][:, p * width : (p + 1) * width] = scratch[:, block_at(perm, p, width, count)].astype(BF)


def lane_roll(x, shift):
    if x.shape[1] == LANES:
        return pltpu.roll(x, shift % LANES, 1)
    return jnp.roll(x, shift, axis=1)


def turned(x, cosine, sine_next, sine_prev, sign):
    back = ROT // 2
    moved = lane_roll(x, -back) * sine_next + lane_roll(x, back) * sine_prev
    return x * cosine + moved if sign > 0 else x * cosine - moved


def qkv_body(chunks, ins, outs, sums):
    normed, cosine, sine_next, sine_prev, weight, bias = ins
    cols = bias.shape[1]
    mixed = dot(normed[...], weight[:, :cols]) + bias[...]
    width = cosine.shape[1]
    tables = (cosine[...], sine_next[...], sine_prev[...])
    for i in range(3 * chunks):
        here = slice(i * width, (i + 1) * width)
        part = mixed[:, here]
        if i < 2 * chunks:
            part = turned(part, *tables, 1)
        outs[0][:, here] = part.astype(BF)


def fc1_body(ins, outs, sums):
    normed, weight, bias = ins
    pre = dot(normed[...], weight[...]) + bias[...]
    phi = 0.5 * (1.0 + lax.erf(pre * 0.7071067811865476))
    outs[0][...] = (pre * phi).astype(BF)
    outs[1][...] = (phi + pre * jnp.exp(-0.5 * pre * pre) * 0.3989422804014327).astype(BF)


def pre_grad_body(ins, outs, sums):
    cot, slope, weight = ins
    grad = (dot(cot[...], weight[...]) * slope[...].astype(F32)).astype(BF)
    outs[0][...] = grad
    sums[0][...] += jnp.sum(grad.astype(F32), axis=0, keepdims=True)


def norm_grad_body(cols, ins, outs, sums):
    if len(ins) == 5:
        grad, standard, other, weight, gain = ins
    else:
        (grad, standard, weight, gain), other = ins, None
    value = dot(grad[...], weight[:, :cols], NT)
    sums[0][...] += jnp.sum(value * standard[...].astype(F32), axis=0, keepdims=True)
    sums[1][...] += jnp.sum(value, axis=0, keepdims=True)
    scaled = value * gain[...]
    if other is not None:
        scaled = scaled + other[...].astype(F32)
    outs[0][...] = scaled.astype(BF)


def out_body(cols, ins, outs, sums):
    hidden, attended, w_fc2, w_att = ins
    total = dot(hidden[...], w_fc2[...], NT) + dot(attended[...], w_att[:, cols:], NT)
    outs[0][...] = total.astype(BF)


def att_grad_body(cols, ins, outs, sums):
    cot, w_att = ins
    outs[0][...] = dot(cot[...], w_att[:, cols:]).astype(BF)


def attention_kernel(
    heads, flip, q_ref, k_ref, v_ref, g_ref, cos_ref, next_ref, prev_ref, att_ref, out_ref, keys, values, key_acc, value_acc
):
    halves, _, length, width = q_ref.shape
    per = width // HEAD
    n_groups = heads // per
    group = pl.program_id(1)
    block = min(256, length)

    def place(half):
        return half if halves == 1 else jnp.bitwise_xor(half, flip[0])

    for half in range(halves):
        rows = slice(half * length, (half + 1) * length)
        keys[rows, :] = k_ref[place(half), 0]
        values[rows, :] = v_ref[place(half), 0]
    key_acc[...] = jnp.zeros_like(key_acc)
    value_acc[...] = jnp.zeros_like(value_acc)
    lane = lax.broadcasted_iota(jnp.int32, (block, width), 1)
    scale = HEAD ** (-0.5)

    def columns(base):
        if n_groups == 1:
            return pl.ds(base * heads * HEAD, width)
        return pl.ds(pl.multiple_of(base * heads * HEAD + group * width, width), width)

    for i in range(halves * length // block):
        half, offset = i * block // length, i * block % length
        here = pl.ds(offset, block)
        extent = (i + 1) * block
        q_all = q_ref[place(half), 0, here, :]
        g_all = g_ref[place(half), 0, here, :]
        key_rows = keys[:extent, :]
        value_rows = values[:extent, :]
        causal = (
            lax.broadcasted_iota(jnp.int32, (block, extent), 0) + i * block
            >= lax.broadcasted_iota(jnp.int32, (block, extent), 1)
        )
        att_total = jnp.zeros((block, width), F32)
        query_total = jnp.zeros((block, width), F32)
        for h in range(per):
            mine = (lane >= h * HEAD) & (lane < (h + 1) * HEAD)
            q = jnp.where(mine, q_all.astype(F32) * scale, 0.0).astype(BF)
            g = jnp.where(mine, g_all.astype(F32), 0.0).astype(BF)
            scores = jnp.where(causal, dot(q, key_rows, NT), -1e30)
            expon = jnp.exp(scores - jnp.max(scores, axis=-1, keepdims=True))
            probs = expon * (1.0 / jnp.sum(expon, axis=-1, keepdims=True))
            low = probs.astype(BF)
            result = jnp.where(mine, dot(low, value_rows), 0.0)
            prob_grad = dot(g, value_rows, NT)
            row_dot = jnp.sum(result * g.astype(F32), axis=-1, keepdims=True)
            score_grad = (probs * (prob_grad - row_dot)).astype(BF)
            att_total += result
            query_total += jnp.where(mine, dot(score_grad, key_rows), 0.0)
            key_acc[:extent, :] += dot(score_grad, q, TN)
            value_acc[:extent, :] += dot(low, g, TN)
        att_ref[place(half), 0, here, :] = att_total.astype(BF)
        tables = [ref[place(half), 0, here, :] for ref in (cos_ref, next_ref, prev_ref)]
        out_ref[place(half), 0, here, columns(0)] = turned(query_total * scale, *tables, -1).astype(BF)
    for half in range(halves):
        rows = slice(half * length, (half + 1) * length)
        tables = [ref[place(half), 0] for ref in (cos_ref, next_ref, prev_ref)]
        out_ref[place(half), 0, :, columns(1)] = turned(key_acc[rows, :], *tables, -1).astype(BF)
        out_ref[place(half), 0, :, columns(2)] = value_acc[rows, :].astype(BF)


def attention(qkv, grad, tables, flip, halves, heads):
    total, cols = qkv.shape
    length = SEQ_LEN // halves
    seqs = total // SEQ_LEN
    per = 2 if heads % 2 == 0 else 1
    width, groups = per * HEAD, heads // per

    def four(x):
        return x.reshape(halves, seqs, length, x.shape[1])

    def spec(base):
        return pl.BlockSpec((halves, 1, length, width), lambda s, h, _: (0, s, 0, base * groups + h))

    table = pl.BlockSpec((halves, 1, length, width), lambda s, h, _: (0, s, 0, 0))
    operands, specs = [four(qkv)] * 3, [spec(0), spec(1), spec(2)]
    if width % LANES:
        operands, specs = [four(x) for x in jnp.split(qkv, 3, axis=1)], [spec(0)] * 3
    att, out = pl.pallas_call(
        functools.partial(attention_kernel, heads),
        grid_spec=pltpu.PrefetchScalarGridSpec(
            num_scalar_prefetch=1,
            grid=(seqs, groups),
            in_specs=[*specs, spec(0), table, table, table],
            out_specs=[spec(0), pl.BlockSpec((halves, 1, length, cols), lambda s, h, _: (0, s, 0, 0))],
            scratch_shapes=[
                pltpu.VMEM((SEQ_LEN, width), BF),
                pltpu.VMEM((SEQ_LEN, width), BF),
                pltpu.VMEM((SEQ_LEN, width), F32),
                pltpu.VMEM((SEQ_LEN, width), F32),
            ],
        ),
        out_shape=[
            jax.ShapeDtypeStruct((halves, seqs, length, heads * HEAD), BF),
            jax.ShapeDtypeStruct((halves, seqs, length, cols), BF),
        ],
        compiler_params=pltpu.CompilerParams(vmem_limit_bytes=48 * 2**20),
        cost_estimate=pl.CostEstimate(
            flops=seqs * heads * 12 * SEQ_LEN * SEQ_LEN * 256 * 5 // 8,
            bytes_accessed=total * cols * 6,
            transcendentals=0,
        ),
    )(flip, *operands, four(grad), *[four(t) for t in tables])
    return att.reshape(total, heads * HEAD), out.reshape(total, cols)


def out_final_body(count, ins, outs, sums):
    perm, tokens, own, other, bias = ins
    width = tokens.shape[1] // count
    for p in range(count):
        there = block_at(perm, p, width, count)
        here = slice(p * width, (p + 1) * width)
        outs[0][:, there] = (
            tokens[:, there].astype(F32) + own[:, here].astype(F32) + other[:, here].astype(F32) + bias[:, there]
        ).astype(BF)


def grad_final_body(count, ins, outs, sums):
    perm, tokens, own, other, cot, scratch_in = ins
    width = tokens.shape[1] // count
    grad = own[...].astype(F32) + other[...].astype(F32)
    centered, inverse = moments(tokens[...].astype(F32))
    standard = centered * inverse
    scratch = outs[1]
    for p in range(count):
        scratch[:, block_at(perm, p, width, count)] = grad[:, p * width : (p + 1) * width]
    grad = scratch[...]
    through = inverse * (
        grad
        - jnp.mean(grad, axis=-1, keepdims=True)
        - standard * jnp.mean(grad * standard, axis=-1, keepdims=True)
    )
    outs[0][...] = (cot[...].astype(F32) + through).astype(BF)


def swap_core(x, size):
    return lax.ppermute(x, "dp", [(i, i ^ 1) for i in range(size)])


def after(x, *first):
    return lax.optimization_barrier((x, *first))[0]


def sum_over(x, axis, size):
    if size & (size - 1):
        return lax.psum(x, axis)
    step = 1
    while step < size:
        x = x + lax.ppermute(x, axis, [(i, i ^ step) for i in range(size)])
        step *= 2
    return x


class Ring:
    def __init__(self, chips):
        self.chips = chips
        order = [2 * i for i in range(chips // 2)] + [2 * i + 1 for i in reversed(range(chips // 2))]
        self.order = order
        places = [0] * chips
        for place, chip in enumerate(order):
            places[chip] = place
        mine = jnp.asarray(places, jnp.int32)[lax.axis_index("dp") // 2]
        self.perm = jnp.asarray(order, jnp.int32)[(mine + jnp.arange(chips)) % chips]
        self.inverse = (jnp.asarray(places, jnp.int32) - mine) % chips

    def send(self, x, step):
        pairs = []
        for place, chip in enumerate(self.order):
            other = self.order[(place + step) % self.chips]
            pairs += [(2 * chip + c, 2 * other + c) for c in range(2)]
        return lax.ppermute(x, "dp", pairs)

    def gather(self, x):
        chips, half = self.chips, x.shape[0] // 2
        blocks = [x] + [None] * (chips - 1)
        up = down = x
        for step in range(1, chips // 2):
            up = self.send(up, 1)
            down = self.send(down, -1)
            blocks[chips - step], blocks[step] = up, down
        last = [self.send(down[:half], -1), self.send(up[half:], 1)]
        blocks[chips // 2] = jnp.concatenate(last, axis=0)
        return blocks

    def scatter(self, grad):
        chips = self.chips
        rows = grad.shape[0] // chips
        half = rows // 2
        parts = [grad[p * rows : (p + 1) * rows] for p in range(chips)]
        middle = chips // 2
        up = self.send(parts[middle][:half], 1)
        down = self.send(parts[middle][half:], -1)
        up = jnp.concatenate([parts[middle - 1][:half] + up, parts[middle - 1][half:]], axis=0)
        down = jnp.concatenate([parts[middle + 1][:half], parts[middle + 1][half:] + down], axis=0)
        for step in range(middle - 2, -1, -1):
            up, down = self.send(up, 1), self.send(down, -1)
            if step:
                up = parts[step] + up
                down = parts[chips - step] + down
        return parts[0].astype(F32) + up.astype(F32) + down.astype(F32)


def shards(dp, tensor, *arrays):
    tokens, positions, cotangent, w_qkv, b_qkv, w_dense, b_dense, w_fc1, b_fc1, w_fc2, b_fc2 = arrays[:11]
    norm1_gain, norm1_shift, norm2_gain, norm2_shift = arrays[11:]
    core = lax.axis_index("dp") % 2
    own_rows, width = tokens.shape
    row_share = w_qkv.shape[0]
    heads = w_qkv.shape[1] // (3 * HEAD) // 2
    qkv_cols, dense_cols = 3 * heads * HEAD, heads * HEAD
    chips = dp // 2
    ringed = chips % 2 == 0 and chips >= 4 and (2 * row_share) % LANES == 0 and chips * 2 * row_share == width
    halves = 2 if tensor == 2 and 2 * own_rows == SEQ_LEN else 1

    def by_heads(w):
        w = w.reshape(*w.shape[:-1], 2, heads, 3, HEAD)
        return jnp.swapaxes(w, -2, -3).reshape(*w.shape[:-4], 2, qkv_cols)

    def from_heads(w):
        w = w.reshape(*w.shape[:-1], 3, heads, HEAD)
        return jnp.swapaxes(w, -2, -3).reshape(*w.shape[:-3], qkv_cols)

    def chip_rows(w):
        mine = lax.dynamic_index_in_dim(w, core, 1, keepdims=False)
        other = swap_core(lax.dynamic_index_in_dim(w, 1 - core, 1, keepdims=False), dp)
        first = jnp.where(core == 0, mine, other)
        second = jnp.where(core == 0, other, mine)
        return jnp.concatenate([first, second], axis=0)

    def two(w):
        return w.reshape(w.shape[0], 2, w.shape[1] // 2)

    fc1_rows = chip_rows(two(w_fc1))
    fc2_rows = chip_rows(two(w_fc2))
    att_rows = chip_rows(jnp.concatenate([by_heads(w_qkv), two(w_dense)], axis=-1))

    def exchange(x, first=()):
        if halves == 2:
            other = lax.ppermute(after(x, *first) if first else x, "tensor", [(0, 1), (1, 0)])
            return [x, swap_core(x, dp), other, swap_core(other, dp)], other
        x = lax.all_gather(x, "tensor", axis=0, tiled=True)
        return [x, swap_core(x, dp)], x

    token_pieces, token_mark = exchange(tokens)
    cot_pieces, _ = exchange(cotangent, (token_mark,))

    if ringed:
        ring = Ring(chips)
        perm, inverse, count = ring.perm, ring.inverse, chips
        fc1_blocks = ring.gather(fc1_rows)
        fc2_blocks = ring.gather(fc2_rows)
        att_blocks = ring.gather(after(att_rows, fc1_blocks[2], fc2_blocks[2]))
        w1, w2, wa = (jnp.concatenate(b, axis=0) for b in (fc1_blocks, fc2_blocks, att_blocks))
        scatter = ring.scatter

        def relative(v):
            return v.reshape(-1, count, width // count)[:, perm].reshape(-1, width)

        def absolute(v):
            return v.reshape(-1, count, width // count)[:, inverse].reshape(-1, width)
    else:
        perm, count = jnp.zeros((1,), jnp.int32), 1
        groups = [[2 * k + c for k in range(chips)] for c in range(2)]

        def gather(rows):
            return lax.all_gather(rows, "dp", axis=0, tiled=True, axis_index_groups=groups)

        def scatter(grad):
            return lax.psum_scatter(grad, "dp", scatter_dimension=0, tiled=True, axis_index_groups=groups).astype(F32)

        def relative(v):
            return v

        absolute = relative
        w1, w2, wa = gather(fc1_rows), gather(fc2_rows), gather(att_rows)

    half_rot = ROT // 2
    frequencies = 10000.0 ** (-jnp.arange(half_rot, dtype=F32) / half_rot)
    if halves == 2:
        pos_first = lax.dynamic_index_in_dim(positions.reshape(2, -1), lax.axis_index("tensor"), 0, keepdims=False)
        pos_second = lax.dynamic_index_in_dim(positions.reshape(2, -1), 1 - lax.axis_index("tensor"), 0, keepdims=False)
        both = swap_core(jnp.stack([pos_first, pos_second]), dp)
        pos_rows = jnp.concatenate([pos_first, both[0], pos_second, both[1]])
    else:
        pos_rows = jnp.concatenate([positions, swap_core(positions, dp)])
    angles = frequencies[:, None] * pos_rows.astype(F32)[None, :]
    cosine, sine = jnp.cos(angles).T, jnp.sin(angles).T
    rows = pos_rows.shape[0]
    zeros8 = jnp.zeros((rows, half_rot), F32)
    rest = HEAD - ROT
    repeat = 2 if heads % 2 == 0 else 1
    cos_table = jnp.tile(jnp.concatenate([cosine, cosine, jnp.ones((rows, rest), F32)], axis=1), (1, repeat))
    next_table = jnp.tile(jnp.concatenate([-sine, zeros8, jnp.zeros((rows, rest), F32)], axis=1), (1, repeat))
    prev_table = jnp.tile(jnp.concatenate([zeros8, sine, jnp.zeros((rows, rest), F32)], axis=1), (1, repeat))
    tables = (cos_table, next_table, prev_table)
    flip = (lax.axis_index("tensor") if halves == 2 else jnp.int32(0)).astype(jnp.int32).reshape(1)

    gain_one, shift_one, gain_two, shift_two = (
        relative(v.reshape(1, width)) for v in (norm1_gain, norm1_shift, norm2_gain, norm2_shift)
    )
    block = 256
    normed1, normed2, standard = pieces_kernel(
        functools.partial(norm_body, count), token_pieces, perm, (gain_one, shift_one, gain_two, shift_two), (BF, BF, BF), block
    )
    (cot,) = pieces_kernel(functools.partial(turn_body, count), cot_pieces, perm, (), (BF,), block)
    hidden_cols = w1.shape[1]
    b1 = lax.dynamic_slice(b_fc1, (core * hidden_cols,), (hidden_cols,)).reshape(1, hidden_cols)
    bq = lax.dynamic_index_in_dim(by_heads(b_qkv), core, 0, keepdims=True)

    work = 2 * rows * width * hidden_cols
    hidden, slope = row_kernel(
        fc1_body, rows, block, (normed2,), (w1, b1), ((hidden_cols, BF), (hidden_cols, BF)), (), work
    )
    pre_grad, bias_fc1 = row_kernel(pre_grad_body, rows, block, (cot, slope), (w2,), ((hidden_cols, BF),), (hidden_cols,), work)
    grad_fc2 = dot(cot, hidden, TN).astype(BF)
    grad_fc1 = dot(normed2, pre_grad, TN).astype(BF)
    scaled_two, gain_two_grad, shift_two_grad = row_kernel(
        functools.partial(norm_grad_body, hidden_cols),
        rows, block, (pre_grad, standard), (w1, gain_two), ((width, BF),), (width, width), work,
    )
    own_fc2 = scatter(grad_fc2)
    own_fc1 = scatter(grad_fc1)

    chunks = dense_cols // cos_table.shape[1]
    (qkv,) = row_kernel(
        functools.partial(qkv_body, chunks), rows, block, (normed1, *tables), (wa, bq), ((qkv_cols, BF),), (), 2 * rows * width * qkv_cols
    )
    (att_grad,) = row_kernel(
        functools.partial(att_grad_body, qkv_cols), rows, block, (cot,), (wa,), ((dense_cols, BF),), (), 2 * rows * width * dense_cols
    )
    attended, qkv_grad = attention(qkv, att_grad, tables, flip, halves, heads)
    grad_att = jnp.concatenate([dot(normed1, qkv_grad, TN), dot(cot, attended, TN)], axis=1).astype(BF)
    own_att = scatter(grad_att)
    (out_part,) = row_kernel(
        functools.partial(out_body, qkv_cols), rows, block, (hidden, attended), (w2, wa), ((width, BF),), (), work + 2 * rows * width * dense_cols
    )
    scaled, gain_one_grad, shift_one_grad = row_kernel(
        functools.partial(norm_grad_body, qkv_cols),
        rows, block, (qkv_grad, standard, scaled_two), (wa, gain_one), ((width, BF),), (width, width), 2 * rows * width * qkv_cols,
    )
    bias_qkv = jnp.sum(qkv_grad.astype(F32), axis=0, keepdims=True)

    def reduce(part):
        if halves == 2:
            part = part.reshape(4, own_rows, width)
            got = swap_core(jnp.concatenate([part[3], part[1]], axis=0), dp)
            other = part[2] + got[:own_rows]
            own = part[0].astype(F32) + got[own_rows:].astype(F32)
            return own, lax.ppermute(other, "tensor", [(0, 1), (1, 0)])
        half = rows // 2
        part = part[:half] + swap_core(part[half:], dp)
        total = lax.psum_scatter(part, "tensor", scatter_dimension=0, tiled=True)
        return total, jnp.zeros_like(total)

    out_own, out_other = reduce(out_part)
    grad_own, grad_other = reduce(scaled)
    final_block = min(256, own_rows)
    (output,) = row_kernel(
        functools.partial(out_final_body, count), own_rows, final_block, (tokens, out_own, out_other),
        ((b_dense + b_fc2).reshape(1, width),), ((width, BF),), (), 0, index=perm,
    )
    grad_tokens, _ = row_kernel(
        functools.partial(grad_final_body, count), own_rows, final_block, (tokens, grad_own, grad_other, cotangent),
        (jnp.zeros((8, LANES), F32),), ((width, BF), (width, F32)), (), 0, index=perm,
    )

    out_bias = jnp.sum(cotangent.astype(F32), axis=0, keepdims=True)
    wide = jnp.concatenate(
        [absolute(jnp.concatenate([gain_one_grad, shift_one_grad, gain_two_grad, shift_two_grad], axis=0)), out_bias], axis=0
    )
    wide = sum_over(sum_over(wide, "tensor", tensor), "dp", dp)
    narrow = jnp.concatenate([from_heads(bias_qkv), bias_fc1], axis=1)
    zero = jnp.zeros_like(narrow)
    narrow = jnp.concatenate([jnp.where(core == 0, narrow, zero), jnp.where(core == 0, zero, narrow)], axis=0)
    narrow = sum_over(narrow, "dp", dp)
    bias_qkv, bias_fc1 = narrow[:, :qkv_cols].reshape(-1), narrow[:, qkv_cols:].reshape(-1)

    def share(own):
        own = own.reshape(2, row_share, own.shape[1])
        mine = lax.dynamic_index_in_dim(own, core, 0, keepdims=False)
        other = swap_core(lax.dynamic_index_in_dim(own, 1 - core, 0, keepdims=False), dp)
        return jnp.where(core == 0, mine, other), jnp.where(core == 0, other, mine)

    att_first, att_second = share(own_att)
    grad_w_qkv = jnp.concatenate([from_heads(att_first[:, :qkv_cols]), from_heads(att_second[:, :qkv_cols])], axis=1)
    grad_w_dense = jnp.concatenate([att_first[:, qkv_cols:], att_second[:, qkv_cols:]], axis=1)
    grad_w_fc1 = jnp.concatenate(share(own_fc1), axis=1)
    grad_w_fc2 = jnp.concatenate(share(own_fc2), axis=1)
    return (
        output, grad_tokens, grad_w_qkv, bias_qkv, grad_w_dense, wide[4], grad_w_fc1, bias_fc1, grad_w_fc2, wide[4],
        wide[0], wide[1], wide[2], wide[3],
    )


def solution(mesh):
    both, weight = P(("dp", "tensor"), None), P("dp", "tensor")
    return jax.shard_map(
        functools.partial(shards, mesh.shape["dp"], mesh.shape["tensor"]),
        mesh=mesh,
        in_specs=(both, P("dp"), both, weight, P("tensor"), weight, P(), weight, P("tensor"), weight, P(), P(), P(), P(), P()),
        out_specs=(both, both, weight, P("tensor"), weight, P(), weight, P("tensor"), weight, P(), P(), P(), P(), P()),
        check_vma=False,
    )
```

```python
import functools

import jax
import jax.numpy as jnp
from jax import lax
from jax.experimental import pallas as pl
from jax.experimental.pallas import tpu as pltpu
from jax.sharding import PartitionSpec as P

HEAD = 64
ROT = 16
SEQ_LEN = 1024
EPSILON = 1e-05
LANES = 128
BF = jnp.bfloat16
F32 = jnp.float32
NN = (((1,), (0,)), ((), ()))
NT = (((1,), (1,)), ((), ()))
TN = (((0,), (0,)), ((), ()))


def dot(first_op, second_op, dims=NN):
    return lax.dot_general(first_op, second_op, dims, preferred_element_type=F32)


class Order:
    def __init__(self, index, marks=()):
        self.index, self.marks = index, list(marks)
        self.shape = index.shape


def call(kernel, grid, in_specs, out_specs, out_shape, operands, flops, scratch=(), index=None, vmem=28):
    moved = sum(x.size * x.dtype.itemsize for x in operands)
    moved += sum(s.size * jnp.dtype(s.dtype).itemsize for s in out_shape)
    marks = []
    if isinstance(index, Order):
        index, marks = index.index, index.marks
    first, count = (0 if index is None else 1) + len(operands), len(marks)

    def body(*refs):
        kernel(*refs[:first], *refs[first + count :])

    return pl.pallas_call(
        body,
        grid_spec=pltpu.PrefetchScalarGridSpec(
            num_scalar_prefetch=0 if index is None else 1,
            grid=grid,
            in_specs=[*in_specs, *[pl.BlockSpec(memory_space=pl.ANY)] * count],
            out_specs=out_specs,
            scratch_shapes=list(scratch),
        ),
        out_shape=out_shape,
        compiler_params=pltpu.CompilerParams(vmem_limit_bytes=vmem * 2**20),
        cost_estimate=pl.CostEstimate(flops=flops, bytes_accessed=moved, transcendentals=0),
    )(*(() if index is None else (index,)), *operands, *marks)


def shape_of(rows, cols, kind=BF):
    return jax.ShapeDtypeStruct((rows, cols), kind)


def row_kernel(body, rows, block, row_ins, full_ins, row_outs, sum_outs, flops, index):
    steps = rows // block
    n_index = 1

    def at_row(first):
        return lambda step, *_: (step + first // block, 0)

    def at_zero(step, *_):
        return (0, 0)

    in_specs = [pl.BlockSpec((block, x.shape[1]), at_row(first)) for x, first in row_ins]
    in_specs += [pl.BlockSpec(x.shape, at_zero, pipeline_mode=pl.Buffered(1)) for x in full_ins]
    def out_spec(cols):
        if isinstance(cols, tuple):
            return pl.BlockSpec((cols[0], block, cols[1]), lambda step, *_: (0, step, 0))
        return pl.BlockSpec((block, cols), at_row(0))

    out_specs = [out_spec(cols) for cols, _ in row_outs]
    out_specs += [pl.BlockSpec((1, width), at_zero) for width in sum_outs]
    out_shape = [
        jax.ShapeDtypeStruct((cols[0], rows, cols[1]), kind) if isinstance(cols, tuple) else shape_of(rows, cols, kind)
        for cols, kind in row_outs
    ]
    out_shape += [shape_of(1, width, F32) for width in sum_outs]
    n_in, n_out = len(in_specs), len(row_outs)

    def kernel(*refs):
        ins = refs[: n_index + n_in]
        outs = refs[n_index + n_in : n_index + n_in + n_out]
        sums = refs[n_index + n_in + n_out :]
        if sums:

            @pl.when(pl.program_id(0) == 0)
            def _():
                for ref in sums:
                    ref[...] = jnp.zeros_like(ref)

        body(ins, outs, sums)

    operands = [x for x, _ in row_ins] + list(full_ins)
    return call(kernel, (steps,), in_specs, out_specs, out_shape, operands, flops, index=index)


def moments(vectors):
    row_mean = jnp.mean(vectors, axis=-1, keepdims=True)
    centered = vectors - row_mean
    spread = jnp.mean(centered * centered, axis=-1, keepdims=True)
    return centered, lax.rsqrt(spread + EPSILON)


def pieces_kernel(body, pieces, index, full_ins, row_outs, block):
    count = len(pieces)
    width = pieces[0][0].shape[1]
    rows = sum(x.shape[0] for x, _, _ in pieces)
    core_at = index.shape[0] - 1

    def slot(side, first, core):
        return (jnp.bitwise_xor(side, core) * (rows // 2) + first) // block

    def at_piece(x, side, first):
        return lambda step, idx: (jnp.clip(step - slot(side, first, idx[core_at]), 0, x.shape[0] // block - 1), 0)

    def kernel(idx, *refs):
        ins, fulls = refs[:count], refs[count : count + len(full_ins)]
        outs = refs[count + len(full_ins) : count + len(full_ins) + len(row_outs)]
        mark, scratch = refs[-2:]
        mark[...] = jnp.zeros_like(mark)
        step = pl.program_id(0)
        for ref, (x, side, first) in zip(ins, pieces):
            start = slot(side, first, idx[core_at])

            @pl.when((step >= start) & (step < start + x.shape[0] // block))
            def _(ref=ref):
                scratch[...] = ref[...].astype(F32)

        body(idx, fulls, outs, scratch)

    return call(
        kernel,
        (rows // block,),
        [pl.BlockSpec((block, width), at_piece(*p)) for p in pieces]
        + [pl.BlockSpec(x.shape, lambda step, _: (0, 0)) for x in full_ins],
        [pl.BlockSpec((block, width), lambda step, _: (step, 0)) for _ in row_outs]
        + [pl.BlockSpec((1, LANES), lambda step, _: (0, 0))],
        [*[shape_of(rows, width, kind) for kind in row_outs], shape_of(1, LANES, F32)],
        [*[x for x, _, _ in pieces], *full_ins],
        30 * rows * width,
        scratch=[pltpu.VMEM((block, width), F32)],
        index=index,
    )


def block_at(perm, place, width, count):
    if count == 1:
        return pl.ds(0, width)
    return pl.ds(pl.multiple_of(perm[place] * width, width), width)


def norm_body(count, perm, fulls, outs, scratch):
    gain_one, shift_one, gain_two, shift_two = fulls
    normed1, normed2, standard = outs
    centered, inverse = moments(scratch[...])
    scratch[...] = centered * inverse
    width = scratch.shape[1] // count
    for p in range(count):
        here = slice(p * width, (p + 1) * width)
        there = block_at(perm, p, width, count)
        part = scratch[:, there]
        normed1[:, here] = (part * gain_one[:, there] + shift_one[:, there]).astype(BF)
        normed2[:, here] = (part * gain_two[:, there] + shift_two[:, there]).astype(BF)
        standard[:, here] = part.astype(BF)


def turn_body(count, perm, fulls, outs, scratch):
    width = scratch.shape[1] // count
    for p in range(count):
        outs[0][:, p * width : (p + 1) * width] = scratch[:, block_at(perm, p, width, count)].astype(BF)


def lane_roll(x, shift):
    if x.shape[1] == LANES:
        return pltpu.roll(x, shift % LANES, 1)
    return jnp.roll(x, shift, axis=1)


def turned(x, table, sign):
    back = ROT // 2
    lane = lax.broadcasted_iota(jnp.int32, x.shape, 1) % HEAD
    sine = lane_roll(table, -ROT)
    moved = jnp.where(lane < back, -lane_roll(x, -back), lane_roll(x, back)) * sine
    total = x * table + moved if sign > 0 else x * table - moved
    return jnp.where(lane < ROT, total, x)


def by_kind(parts):
    if parts[0].shape[1] < LANES:
        return parts
    first, second, third = parts
    low = lax.broadcasted_iota(jnp.int32, first.shape, 1) < HEAD
    return (
        jnp.where(low, first, second),
        jnp.where(low, lane_roll(first, HEAD), lane_roll(third, HEAD)),
        jnp.where(low, second, third),
    )


def by_head(query, key, value):
    if query.shape[1] < LANES:
        return query, key, value
    low = lax.broadcasted_iota(jnp.int32, query.shape, 1) < HEAD
    swapped = lane_roll(key, HEAD)
    return jnp.where(low, query, swapped), jnp.where(low, value, query), jnp.where(low, swapped, value)


def qkv_body(groups, ins, outs, sums):
    _, normed, table, weight, bias = ins
    width = table.shape[1]
    for h in range(groups):
        cols = slice(3 * h * width, 3 * (h + 1) * width)
        mixed = dot(normed[...], weight[:, cols]) + bias[:, cols]
        query, key, value = by_kind([mixed[:, i * width : (i + 1) * width] for i in range(3)])
        outs[0][h] = turned(query, table[...], 1).astype(BF)
        outs[0][groups + h] = turned(key, table[...], 1).astype(BF)
        outs[0][2 * groups + h] = value.astype(BF)


def fc1_body(ins, outs, sums):
    _, normed, weight, bias = ins
    cols = weight.shape[1]
    step = min(256, cols)
    for j in range(cols // step):
        here = slice(j * step, (j + 1) * step)
        pre = dot(normed[...], weight[:, here]) + bias[:, here]
        phi = 0.5 * (1.0 + lax.erf(pre * 0.7071067811865476))
        outs[0][:, here] = (pre * phi).astype(BF)
        outs[1][:, here] = (phi + pre * jnp.exp(-0.5 * pre * pre) * 0.3989422804014327).astype(BF)


def pre_grad_body(ins, outs, sums):
    _, cot, slope, weight = ins
    grad = (dot(cot[...], weight[...]) * slope[...].astype(F32)).astype(BF)
    outs[0][...] = grad
    sums[0][...] += jnp.sum(grad.astype(F32), axis=0, keepdims=True)


def att_grad_body(cols, ins, outs, sums):
    _, cot, w_att = ins
    grad = dot(cot[...], w_att[:, cols:]).astype(BF)
    groups, _, width = outs[0].shape
    for h in range(groups):
        outs[0][h] = grad[:, h * width : (h + 1) * width]


def tail_body(groups, count, ins, outs, sums):
    perm, hidden, pre_grad, standard = ins[:4]
    attended, grads = ins[4 : 4 + groups], ins[4 + groups : 4 + 2 * groups]
    w1, w2, wa, gain_one, gain_two = ins[4 + 2 * groups :]
    dense = groups * grads[0].shape[1]
    att = jnp.concatenate([x[...] for x in attended], axis=1)
    grad = jnp.concatenate([x[...] for x in grads], axis=1)
    width = standard.shape[1] // count
    step = min(256, standard.shape[1])
    for j in range(standard.shape[1] // step):
        cols = slice(j * step, (j + 1) * step)
        total = dot(hidden[...], w2[cols, :], NT) + dot(att, wa[cols, dense:], NT)
        outs[0][0, :, cols] = total.astype(BF)
        two = dot(pre_grad[...], w1[cols, :], NT)
        one = dot(grad, wa[cols, :dense], NT)
        std = standard[:, cols].astype(F32)
        values = (one * std, one, two * std, two)
        values = [jnp.sum(v, axis=0, keepdims=True) for v in values]
        if count == 1:
            for ref, value in zip(sums, values):
                ref[:, cols] += value
            outs[0][1, :, cols] = (one * gain_one[:, cols] + two * gain_two[:, cols]).astype(BF)
            continue
        for k in range(step // width):
            there = block_at(perm, j * (step // width) + k, width, count)
            part = slice(k * width, (k + 1) * width)
            for ref, value in zip(sums, values):
                ref[:, there] += value[:, part]
            scaled = one[:, part] * gain_one[:, there] + two[:, part] * gain_two[:, there]
            outs[0][1, :, j * step + k * width : j * step + (k + 1) * width] = scaled.astype(BF)


def att_weight_body(groups, rows, _, *refs):
    normed, cot = refs[:2]
    attended, grads = refs[2 : 2 + 2 * groups], refs[2 + 2 * groups : 2 + 4 * groups]
    out, mark, joined = refs[-3:]
    mark[...] = jnp.zeros_like(mark)
    width, wide = attended[0].shape[1], grads[0].shape[1]
    dense = groups * wide

    @pl.when(pl.program_id(0) == 0)
    def _():
        for which in range(2):
            here = slice(which * rows, (which + 1) * rows)
            for h in range(groups):
                joined[here, h * wide : (h + 1) * wide] = grads[which * groups + h][...]
                joined[here, dense + h * width : dense + (h + 1) * width] = attended[which * groups + h][...]

    out[:, :dense] = dot(normed[...], joined[:, :dense], TN).astype(BF)
    out[:, dense:] = dot(cot[...], joined[:, dense:], TN).astype(BF)


def att_weight_kernel(index, normed, cot, attended, grads):
    groups = len(attended) // 2
    rows, depth = normed.shape
    cols = sum(x.shape[1] for x in (*attended[:groups], *grads[:groups]))
    step = min(256, depth)

    def whole(x):
        return pl.BlockSpec(x.shape, lambda i, _: (0, 0), pipeline_mode=pl.Buffered(1))

    return call(
        functools.partial(att_weight_body, groups, rows // 2),
        (depth // step,),
        [pl.BlockSpec((rows, step), lambda i, _: (0, i))] * 2 + [whole(x) for x in (*attended, *grads)],
        [pl.BlockSpec((step, cols), lambda i, _: (i, 0)), pl.BlockSpec((1, LANES), lambda i, _: (0, 0))],
        [shape_of(depth, cols), shape_of(1, LANES, F32)],
        [normed, cot, *attended, *grads],
        2 * rows * depth * cols,
        scratch=[pltpu.VMEM((rows, cols), BF)],
        index=index,
    )


def attention_kernel(flip, q_ref, k_ref, v_ref, g_ref, table_ref, att_ref, out_ref, sum_ref, keys, values, q_acc, key_acc, value_acc):
    _, _, halves, length, width = q_ref.shape
    per = width // HEAD
    block = min(256, length)

    def place(half):
        return half if halves == 1 else jnp.bitwise_xor(half, flip[0])

    @pl.when(pl.program_id(0) == 0)
    def _():
        sum_ref[...] = jnp.zeros_like(sum_ref)

    for half in range(halves):
        rows = slice(half * length, (half + 1) * length)
        keys[rows, :] = k_ref[0, 0, place(half)]
        values[rows, :] = v_ref[0, 0, place(half)]
    key_acc[...] = jnp.zeros_like(key_acc)
    value_acc[...] = jnp.zeros_like(value_acc)
    lane = lax.broadcasted_iota(jnp.int32, (block, width), 1)
    scale = HEAD ** (-0.5)

    for i in range(halves * length // block):
        half, offset = i * block // length, i * block % length
        here = pl.ds(offset, block)
        extent = (i + 1) * block
        q_all = q_ref[0, 0, place(half), here, :]
        g_all = g_ref[0, 0, place(half), here, :]
        key_rows = keys[:extent, :]
        value_rows = values[:extent, :]
        causal = (
            lax.broadcasted_iota(jnp.int32, (block, extent), 0) + i * block
            >= lax.broadcasted_iota(jnp.int32, (block, extent), 1)
        )
        att_total = jnp.zeros((block, width), F32)
        query_total = jnp.zeros((block, width), F32)
        for h in range(per):
            mine = (lane >= h * HEAD) & (lane < (h + 1) * HEAD)
            q = jnp.where(mine, q_all.astype(F32) * scale, 0.0).astype(BF)
            g = jnp.where(mine, g_all.astype(F32), 0.0).astype(BF)
            scores = jnp.where(causal, dot(q, key_rows, NT), -1e30)
            expon = jnp.exp(scores - jnp.max(scores, axis=-1, keepdims=True))
            probs = expon * (1.0 / jnp.sum(expon, axis=-1, keepdims=True))
            low = probs.astype(BF)
            result = jnp.where(mine, dot(low, value_rows), 0.0)
            prob_grad = dot(g, value_rows, NT)
            row_dot = jnp.sum(result * g.astype(F32), axis=-1, keepdims=True)
            score_grad = (probs * (prob_grad - row_dot)).astype(BF)
            att_total += result
            query_total += jnp.where(mine, dot(score_grad, key_rows), 0.0)
            key_acc[:extent, :] += dot(score_grad, q, TN)
            value_acc[:extent, :] += dot(low, g, TN)
        att_ref[0, place(half), here, :] = att_total.astype(BF)
        q_acc[i * block : (i + 1) * block, :] = query_total
    for half in range(halves):
        rows = slice(half * length, (half + 1) * length)
        table = table_ref[0, place(half)]
        query = turned(q_acc[rows, :] * scale, table, -1)
        key = turned(key_acc[rows, :], table, -1)
        for j, part in enumerate(by_head(query, key, value_acc[rows, :])):
            part = part.astype(BF)
            out_ref[0, place(half), :, j * width : (j + 1) * width] = part
            sum_ref[:, j * width : (j + 1) * width] += jnp.sum(part.astype(F32), axis=0, keepdims=True)


def attention(qkv, grad, table, flip, halves, which, group):
    groups, total, width = grad.shape
    length = SEQ_LEN // halves
    seqs = total // SEQ_LEN
    own = seqs // 2

    def split(x):
        return x.reshape(*x.shape[:-2], seqs, halves, length, width)

    def spec(at):
        return pl.BlockSpec((1, 1, halves, length, width), lambda s, _: (at, which * own + s, 0, 0, 0))

    def out_spec(cols):
        return pl.BlockSpec((1, halves, length, cols), lambda s, _: (s, 0, 0, 0))

    acc = pltpu.VMEM((SEQ_LEN, width), F32)
    low = pltpu.VMEM((SEQ_LEN, width), BF)
    att, out, sums = call(
        attention_kernel,
        (own,),
        [*[spec(base * groups + group) for base in range(3)], spec(group)]
        + [pl.BlockSpec((1, halves, length, width), lambda s, _: (which * own + s, 0, 0, 0))],
        [out_spec(width), out_spec(3 * width), pl.BlockSpec((1, 3 * width), lambda s, _: (0, 0))],
        [
            jax.ShapeDtypeStruct((own, halves, length, width), BF),
            jax.ShapeDtypeStruct((own, halves, length, 3 * width), BF),
            shape_of(1, 3 * width, F32),
        ],
        [split(qkv)] * 3 + [split(grad), split(table)],
        own * (width // HEAD) * 12 * SEQ_LEN * SEQ_LEN * 256 * 5 // 8,
        scratch=[low, low, acc, acc, acc],
        index=flip,
    )
    return att.reshape(-1, width), out.reshape(-1, 3 * width), sums


def table_kernel(positions, flip, halves, repeat):
    rows = positions.shape[1]
    width, half_rot = repeat * HEAD, ROT // 2
    length = SEQ_LEN // halves

    def kernel(flip_ref, pos_ref, out):
        index = lax.broadcasted_iota(jnp.int32, (half_rot, 1), 0).astype(F32)
        frequencies = jnp.exp(index * (-9.210340371976184 / half_rot))
        frequencies = jnp.where(index == 0.0, 1.0, frequencies)
        angles = frequencies * pos_ref[...].astype(F32)
        lane = lax.broadcasted_iota(jnp.int32, (half_rot, width), 1) % HEAD
        place = lax.broadcasted_iota(jnp.int32, (half_rot, width), 0)
        first = ((lane == place) | (lane == place + half_rot)).astype(F32)
        second = ((lane == place + ROT) | (lane == place + ROT + half_rot)).astype(F32)

        def spread(x, y):
            return lax.dot_general(x, y, TN, precision=lax.Precision.HIGHEST, preferred_element_type=F32)

        table = spread(jnp.cos(angles), first) + spread(jnp.sin(angles), second)
        for f in range(halves):

            @pl.when(flip_ref[0] == f)
            def _(f=f):
                for start in range(0, rows, SEQ_LEN):
                    for half in range(halves):
                        there = start + (half ^ f) * length
                        here = start + half * length
                        out[there : there + length, :] = table[here : here + length, :]

    return one_step(kernel, [positions], [shape_of(rows, width, F32)], index=flip)[0]


def final_body(count, n_parts, ins, outs, sums):
    perm, tokens, cot = ins[:3]
    parts, bias = ins[3:-1], ins[-1]
    width = tokens.shape[1] // count

    def total(refs):
        value = refs[0][...].astype(F32)
        for ref in refs[1:]:
            value = value + ref[...].astype(F32)
        return value

    out_total, grad_total = total(parts[:n_parts]), total(parts[n_parts:])
    scratch = outs[2]
    for p in range(count):
        there = block_at(perm, p, width, count)
        here = slice(p * width, (p + 1) * width)
        scratch[:, there] = grad_total[:, here]
        outs[0][:, there] = (tokens[:, there].astype(F32) + out_total[:, here] + bias[:, there]).astype(BF)
    grad = scratch[...]
    centered, inverse = moments(tokens[...].astype(F32))
    standard = centered * inverse
    through = inverse * (
        grad
        - jnp.mean(grad, axis=-1, keepdims=True)
        - standard * jnp.mean(grad * standard, axis=-1, keepdims=True)
    )
    outs[1][...] = (cot[...].astype(F32) + through).astype(BF)


def pair_add_kernel(index, part, got):
    _, rows, width = part.shape
    rows //= 2
    block = min(256, rows)
    per = rows // block

    def kernel(_, part_ref, got_ref, *outs):
        for k in range(2):
            outs[k][...] = (part_ref[k].astype(F32) + got_ref[k].astype(F32)).astype(BF)

    high = pl.BlockSpec((2, block, width), lambda i, _: (0, i + per, 0))
    other = pl.BlockSpec((block, width), lambda i, _: (i, 0))
    return call(
        kernel, (per,), [high, high], [other, other], [shape_of(rows, width)] * 2, [part, got], 2 * rows * width,
        index=index,
    )


def own_kernel(index, pairs):
    _, rows, width = pairs[0][0].shape
    rows //= 2
    block = min(256, rows)

    def kernel(idx, *refs):
        zero, one = (refs[2 * i][...].astype(F32) + refs[2 * i + 1][...].astype(F32) for i in range(2))
        total = jnp.where(idx[idx.shape[0] - 1] == 0, zero, one).astype(BF)
        refs[-2][...], refs[-1][...] = total[0], total[1]

    low = pl.BlockSpec((2, block, width), lambda i, _: (0, i, 0))
    own = pl.BlockSpec((block, width), lambda i, _: (i, 0))
    operands = [x for pair in pairs for x in pair]
    return call(
        kernel, (rows // block,), [low] * 4, [own] * 2, [shape_of(rows, width)] * 2, operands, 6 * rows * width,
        index=index,
    )


def one_step(kernel, operands, shapes, index=None):
    def whole(shape):
        return pl.BlockSpec(shape, lambda i, *_: (0,) * len(shape))

    return call(
        kernel, (1,), [whole(x.shape) for x in operands], [whole(s.shape) for s in shapes], shapes, operands, 0,
        index=index, vmem=40,
    )


def split_kernel(core, weights):
    w_qkv, w_dense, w_fc1, w_fc2 = weights
    rows = w_qkv.shape[0]
    cols = [w.shape[1] // 2 for w in weights]

    def kernel(core_ref, qkv, dense, fc1, fc2, *outs):
        for c in range(2):

            @pl.when(core_ref[0] == c)
            def _(c=c):
                for out, k in zip(outs, (c, 1 - c)):
                    out[:rows, : cols[0]] = qkv[:, k * cols[0] : (k + 1) * cols[0]]
                    out[:rows, cols[0] :] = dense[:, k * cols[1] : (k + 1) * cols[1]]
                    out[rows : 2 * rows, :] = fc1[:, k * cols[2] : (k + 1) * cols[2]]
                    out[2 * rows :, :] = fc2[:, k * cols[3] : (k + 1) * cols[3]]

    return one_step(kernel, list(weights), [shape_of(3 * rows, cols[2])] * 2, index=core)


def place_kernel(core, mine, other):
    rows = mine.shape[0] // 3

    def kernel(core_ref, a, b, first, second):
        for c in range(2):

            @pl.when(core_ref[0] == c)
            def _(c=c):
                for ref, k in ((a, c), (b, 1 - c)):
                    first[k * rows : (k + 1) * rows, :] = ref[:rows, :]
                    first[(2 + k) * rows : (3 + k) * rows, :] = ref[rows : 2 * rows, :]
                    second[k * rows : (k + 1) * rows, :] = ref[2 * rows :, :]

    cols = mine.shape[1]
    return one_step(kernel, [mine, other], [shape_of(4 * rows, cols), shape_of(2 * rows, cols)], index=core)


def join_kernel(blocks, stack):
    rows = blocks[0].shape[0] // stack
    whole = sum(b.shape[0] for b in blocks) // stack

    def kernel(*refs):
        outs = refs[-stack:]
        first, filled = 0, 0
        for ref in refs[:-stack]:
            if ref.shape[0] == stack * rows:
                for k in range(stack):
                    outs[k][first : first + rows, :] = ref[k * rows : (k + 1) * rows, :]
                first += rows
                continue
            got = ref.shape[0]
            place = first + (filled % rows)
            outs[filled // rows][place : place + got, :] = ref[...]
            filled += got
            if filled == stack * rows:
                first += rows

    return one_step(kernel, blocks, [shape_of(whole, blocks[0].shape[1])] * stack)


def reorder_kernel(arrays, perm, count, gather):
    rows, cols = arrays[0].shape
    block = rows // count
    wide = cols * len(arrays)

    def kernel(_, *refs):
        for i, ref in enumerate(refs[:-1]):
            refs[-1][:, i * cols : (i + 1) * cols] = ref[...]

    def moved(p, perm_ref):
        return (perm_ref[p], 0)

    def plain(p, _):
        return (p, 0)

    return call(
        kernel,
        (count,),
        [pl.BlockSpec((block, cols), moved if gather else plain)] * len(arrays),
        [pl.BlockSpec((block, wide), plain if gather else moved)],
        [shape_of(rows, wide)],
        arrays,
        0,
        index=perm,
    )[0]


def share_kernel(core, parts):
    rows = parts[0].shape[0] // 2

    def kernel(core_ref, *refs):
        for c in range(2):

            @pl.when(core_ref[0] == c)
            def _(c=c):
                for out, k in zip(refs[-2:], (c, 1 - c)):
                    here = slice(k * rows, (k + 1) * rows)
                    total = refs[0][here, :].astype(F32)
                    for ref in refs[1:-2]:
                        total = total + ref[here, :].astype(F32)
                    out[...] = total

    return one_step(kernel, list(parts), [shape_of(rows, parts[0].shape[1], F32)] * 2, index=core)


def columns_kernel(core, mine, other, cuts):
    rows = mine.shape[0]

    def kernel(core_ref, a, b, *outs):
        for c in range(2):

            @pl.when(core_ref[0] == c)
            def _(c=c):
                for out, low, high in zip(outs, cuts, cuts[1:]):
                    cols = high - low
                    out[:, c * cols : (c + 1) * cols] = a[:, low:high]
                    out[:, (1 - c) * cols : (2 - c) * cols] = b[:, low:high]

    shapes = [shape_of(rows, 2 * (high - low), F32) for low, high in zip(cuts, cuts[1:])]
    return one_step(kernel, [mine, other], shapes, index=core)


def add_kernel(grads, chips, places, received, spans):
    block = grads[0].shape[0] // chips
    cols = grads[0].shape[1]
    count = len(grads)

    def whole(shape):
        return pl.BlockSpec(shape, lambda i: (0, 0))

    def kernel(*refs):
        for way in range(2):
            ins = refs[way * count : (way + 1) * count]
            out = refs[-2 + way]
            low, high = spans[way]
            for i in range(count):
                if received is None:
                    size = high - low
                    out[i * size : (i + 1) * size, :] = ins[i][low:high, :]
                    continue
                got = refs[2 * count + way]
                size = high - low
                first = i * block
                if low:
                    out[first : first + low, :] = ins[i][:low, :]
                if high < block:
                    out[first + high : first + block, :] = ins[i][high:, :]
                total = ins[i][low:high, :].astype(F32) + got[i * size : (i + 1) * size, :].astype(F32)
                out[first + low : first + high, :] = total.astype(BF)

    specs = [
        pl.BlockSpec((block, cols), functools.partial(lambda place, i: (place, 0), places[way]))
        for way in range(2)
        for _ in range(count)
    ]
    operands = [*grads, *grads]
    out_rows = [count * block] * 2
    if received is None:
        out_rows = [count * (high - low) for low, high in spans]
    else:
        specs += [whole(x.shape) for x in received]
        operands += list(received)
    return call(
        kernel, (1,), specs, [whole((r, cols)) for r in out_rows], [shape_of(r, cols) for r in out_rows], operands, 0
    )


def swap_core(x, size):
    return lax.ppermute(x, "dp", [(i, i ^ 1) for i in range(size)])


def tie(*trees):
    return lax.optimization_barrier(trees)


def sum_step(x, axis, size, step):
    return x + lax.ppermute(x, axis, [(i, i ^ step) for i in range(size)])


def sum_over(x, axis, size):
    if size & (size - 1):
        return lax.psum(x, axis)
    step = 1
    while step < size:
        x = sum_step(x, axis, size, step)
        step *= 2
    return x


class Ring:
    def __init__(self, chips):
        self.chips = chips
        order = [2 * i for i in range(chips // 2)] + [2 * i + 1 for i in reversed(range(chips // 2))]
        self.order = order
        places = [0] * chips
        for place, chip in enumerate(order):
            places[chip] = place
        mine = jnp.asarray(places, jnp.int32)[lax.axis_index("dp") // 2]
        self.perm = jnp.asarray(order, jnp.int32)[(mine + jnp.arange(chips)) % chips]
        self.inverse = (jnp.asarray(places, jnp.int32) - mine) % chips

    def send(self, x, step):
        pairs = []
        for place, chip in enumerate(self.order):
            other = self.order[(place + step) % self.chips]
            pairs += [(2 * chip + c, 2 * other + c) for c in range(2)]
        return lax.ppermute(x, "dp", pairs)


class Gather:
    def __init__(self, ring, x, stack):
        self.ring, self.step, self.last, self.stack = ring, 0, (x, x), stack
        self.blocks = [x] + [None] * (ring.chips - 1)

    def run(self):
        self.step += 1
        up, down = self.last
        if self.step == self.ring.chips // 2:
            half = up.shape[0] // 2
            up, down = up[:half], down[half:]
        self.last = (self.ring.send(up, 1), self.ring.send(down, -1))

    def keep(self):
        up, down = self.last
        if self.step == self.ring.chips // 2:
            self.middle = [up, down]
        else:
            self.blocks[self.ring.chips - self.step], self.blocks[self.step] = up, down

    def result(self):
        middle = self.ring.chips // 2
        return join_kernel([*self.blocks[:middle], *self.middle, *self.blocks[middle + 1 :]], self.stack)


class Scatter:
    def __init__(self, ring, grads):
        self.ring, self.grads, self.step, self.last = ring, grads, 0, None

    def run(self):
        chips = self.ring.chips
        middle, block = chips // 2, self.grads[0].shape[0] // chips
        places = (middle - self.step, middle + self.step)
        if self.step < 2:
            spans = ((0, block // 2), (block // 2, block))
        else:
            spans = ((0, block), (0, block))
        up, down = add_kernel(self.grads, chips, places, self.last, spans)
        self.step += 1
        self.last = (self.ring.send(up, 1), self.ring.send(down, -1))

    def result(self):
        rows = self.grads[0].shape[0] // self.ring.chips
        return [self.grads[0][:rows], *self.last]


def shards(dp, tensor, *arrays):
    tokens, positions, cotangent, w_qkv, b_qkv, w_dense, b_dense, w_fc1, b_fc1, w_fc2, b_fc2 = arrays[:11]
    norm1_gain, norm1_shift, norm2_gain, norm2_shift = arrays[11:]
    core = lax.axis_index("dp") % 2
    own_rows, width = tokens.shape
    row_share = w_qkv.shape[0]
    heads = w_qkv.shape[1] // (3 * HEAD) // 2
    qkv_cols, dense_cols = 3 * heads * HEAD, heads * HEAD
    groups = heads // 2 if heads % 2 == 0 else heads
    chips = dp // 2
    ringed = chips % 2 == 0 and chips >= 4 and (2 * row_share) % LANES == 0 and chips * 2 * row_share == width
    halves = 2 if tensor == 2 and 2 * own_rows == SEQ_LEN else 1
    core_index = core.astype(jnp.int32).reshape(1)
    block, row_block = 256, 512

    if ringed:
        ring = Ring(chips)
        count = chips
        perm = jnp.concatenate([ring.perm, core_index])
    else:
        count = 1
        perm = jnp.concatenate([jnp.zeros((1,), jnp.int32), core_index])

    def over_x(x):
        return lax.ppermute(x, "tensor", [(0, 1), (1, 0)])

    flip = (lax.axis_index("tensor") if halves == 2 else jnp.int32(0)).astype(jnp.int32).reshape(1)

    def make_tables(both):
        repeat = 2 if heads % 2 == 0 else 1
        return table_kernel(both, flip, halves, repeat)

    gains = tuple(v.reshape(1, width) for v in (norm1_gain, norm1_shift, norm2_gain, norm2_shift))
    gain_one, _, gain_two, _ = gains
    hidden_cols = w_fc1.shape[1] // 2
    b1 = lax.dynamic_slice(b_fc1, (core * hidden_cols,), (hidden_cols,)).reshape(1, hidden_cols)
    bq = lax.dynamic_slice(b_qkv, (core * qkv_cols,), (qkv_cols,)).reshape(1, qkv_cols)
    rows = 2 * own_rows * tensor
    group_rows = rows // 2
    work = 2 * rows * width * hidden_cols

    mine, other = split_kernel(core_index, (w_qkv, w_dense, w_fc1, w_fc2))
    in_rows, fc2_rows = place_kernel(core_index, mine, swap_core(other, dp))
    pos = positions.reshape(1, -1)
    other = swap_core(pos, dp)
    positions_two = jnp.where(
        core == 0, jnp.concatenate([pos, other], axis=1), jnp.concatenate([other, pos], axis=1)
    )

    def run_norm(pieces, order=perm):
        return pieces_kernel(functools.partial(norm_body, count), pieces, order, gains, (BF, BF, BF), block)

    def run_turn(pieces, order=perm):
        return pieces_kernel(functools.partial(turn_body, count), pieces, order, (), (BF,), block)

    def run_qkv(normed1, table, wa, order=perm):
        return row_kernel(
            functools.partial(qkv_body, groups), rows, row_block, [(normed1, 0), (table, 0)], (wa, bq),
            (((3 * groups, dense_cols // groups), BF),), (LANES,), 2 * rows * width * qkv_cols, order,
        )

    def run_fc1(normed2, w1, order=perm):
        return row_kernel(
            fc1_body, rows, row_block, [(normed2, 0)], (w1, b1), ((hidden_cols, BF), (hidden_cols, BF)), (LANES,), work, order
        )

    def run_att_grad(cot, wa, order=perm):
        return row_kernel(
            functools.partial(att_grad_body, qkv_cols), rows, row_block, [(cot, 0)], (wa,), (((groups, dense_cols // groups), BF),), (LANES,),
            2 * rows * width * dense_cols, order,
        )

    def run_pre_grad(cot, slope, w2, order=perm):
        return row_kernel(
            pre_grad_body, rows, row_block, [(cot, 0), (slope, 0)], (w2,), ((hidden_cols, BF),), (hidden_cols,), work, order
        )

    def run_tail(which, hidden, pre_grad, standard, attended, grads, w1, w2, wa, order=perm):
        first = which * group_rows
        return row_kernel(
            functools.partial(tail_body, groups, count), group_rows, row_block,
            [(hidden, first), (pre_grad, first), (standard, first), *[(x, 0) for x in (*attended, *grads)]],
            (w1, w2, wa, gain_one, gain_two), (((2, width), BF),), (width,) * 4,
            work + group_rows * width * (qkv_cols + dense_cols) * 2, order,
        )

    def run_attention(qkv, att_grad, table, which, group, order=flip):
        return attention(qkv, att_grad, table, order, halves, which, group)

    def to_owner(which, part):
        return lax.ppermute(part, "dp", [(2 * k + 1 - which, 2 * k + which) for k in range(chips)])

    out_bias = jnp.sum(cotangent.astype(F32), axis=0, keepdims=True)

    def small_sums(sums, bias_qkv, bias_fc1):
        wide = jnp.concatenate([*sums, out_bias], axis=1)
        wide = sum_over(wide, "tensor", tensor)
        narrow = jnp.concatenate([bias_qkv, bias_fc1], axis=1)
        zero = jnp.zeros_like(narrow)
        return jnp.concatenate([wide, jnp.where(core == 0, narrow, zero), jnp.where(core == 0, zero, narrow)], axis=1)

    def reduce_x(which, other):
        pairs = [(2 * i + x, 2 * i + 1 - x) for i in range(which, dp, 2) for x in range(2)]
        return lax.ppermute(other, ("dp", "tensor"), pairs)

    if ringed and halves == 2:
        flow = ring_flow
    else:
        flow = plain_flow
    env = dict(locals())
    results = flow(env)
    final_block = min(256, own_rows)
    parts = results["parts"]
    output, grad_tokens, _ = row_kernel(
        functools.partial(final_body, count, len(parts) // 2), own_rows, final_block,
        [(tokens, 0), (cotangent, 0), *parts],
        ((b_dense + b_fc2).reshape(1, width),), ((width, BF), (width, BF), (width, F32)), (), 0, perm,
    )

    small = results["small"]
    wide, first, second = jnp.split(small[0], [5 * width, 5 * width + qkv_cols + hidden_cols])
    wide = wide.reshape(5, width)
    bias_qkv = jnp.concatenate([first[:qkv_cols], second[:qkv_cols]])
    bias_fc1 = jnp.concatenate([first[qkv_cols:], second[qkv_cols:]])
    grad_w_qkv, grad_w_dense, grad_w_fc1, grad_w_fc2 = results["weights"]
    return (
        output, grad_tokens, grad_w_qkv, bias_qkv, grad_w_dense, wide[4], grad_w_fc1, bias_fc1, grad_w_fc2, wide[4],
        wide[0], wide[1], wide[2], wide[3],
    )


def plain_flow(env):
    dp, chips, groups = env["dp"], env["chips"], env["groups"]
    core, perm = env["core"], env["perm"]
    sets = [[2 * k + c for k in range(chips)] for c in range(2)]

    def gather(x):
        return lax.all_gather(x, "dp", axis=0, tiled=True, axis_index_groups=sets)

    def scatter(x):
        return lax.psum_scatter(x, "dp", scatter_dimension=0, tiled=True, axis_index_groups=sets)

    def pieces(x):
        x = lax.all_gather(x, "tensor", axis=0, tiled=True)
        return [(x, 0, 0), (swap_core(x, dp), 1, 0)]

    half = env["in_rows"].shape[0] // 2
    wa, w1, w2 = gather(env["in_rows"][:half]), gather(env["in_rows"][half:]), gather(env["fc2_rows"])
    table = env["make_tables"](env["positions_two"])
    normed1, normed2, standard, _ = env["run_norm"](pieces(env["tokens"]))
    cot, _ = env["run_turn"](pieces(env["cotangent"]))
    hidden, slope, _ = env["run_fc1"](normed2, w1)
    pre_grad, bias_fc1 = env["run_pre_grad"](cot, slope, w2)
    qkv, _ = env["run_qkv"](normed1, table, wa)
    att_grad, _ = env["run_att_grad"](cot, wa)
    attended, grads, sums, totals, biases = [], [], [0.0] * 4, [], []
    for which in range(2):
        got = [env["run_attention"](qkv, att_grad, table, which, h) for h in range(groups)]
        attended += [x[0] for x in got]
        grads += [x[1] for x in got]
        biases.append(jnp.concatenate([x[2] for x in got], axis=1))
        part, *some = env["run_tail"](
            which, hidden, pre_grad, standard, attended[-groups:], grads[-groups:], w1, w2, wa
        )
        sums = [a + b for a, b in zip(sums, some)]
        part = part + env["to_owner"](which, part)
        totals.append([lax.psum_scatter(part[k], "tensor", scatter_dimension=0, tiled=True) for k in range(2)])
    cols = env["qkv_cols"]
    ff = [scatter(x) for x in (dot(normed2, pre_grad, TN).astype(BF), dot(cot, hidden, TN).astype(BF))]
    grad_att = att_weight_kernel(perm, normed1, cot, attended, grads)[0]
    weights = share_weights(env, [scatter(grad_att)], (0, cols, ff[0].shape[1]))
    weights += share_weights(env, [jnp.concatenate(ff, axis=1)], (0, ff[0].shape[1], 2 * ff[0].shape[1]))
    small = env["small_sums"](sums, biases[0] + biases[1], bias_fc1)
    parts = [(jnp.where(core == 0, totals[0][k], totals[1][k]), 0) for k in range(2)]
    return dict(parts=parts, small=sum_over(small, "dp", dp), weights=weights)


def share_weights(env, parts, cuts):
    mine, other = share_kernel(env["core_index"], parts)
    return list(columns_kernel(env["core_index"], mine, swap_core(other, env["dp"]), cuts))


def ring_flow(env):
    dp, ring, groups, chips = env["dp"], env["ring"], env["groups"], env["chips"]
    over_x, own_rows = env["over_x"], env["own_rows"]
    tokens, cotangent, pos = env["tokens"], env["cotangent"], env["positions_two"]
    sets = [[2 * k + c for k in range(chips)] for c in range(2)]
    half = own_rows // 2
    order = [Order(env["perm"]), Order(env["flip"])]

    def settle(rings, *values):
        lasts, values = tie([r.last for r in rings], list(values))
        marks = [x for x in jax.tree.leaves(values) if x.size <= 8 * LANES]
        order[:] = [Order(o.index, marks) for o in order]
        for r, last in zip(rings, lasts):
            r.last = last
            if isinstance(r, Gather):
                r.keep()
        return values

    weights_in = Gather(ring, env["in_rows"], 2)
    weights_out = Gather(ring, env["fc2_rows"], 1)

    tok_a = over_x(tokens[:half])
    tok_sib = swap_core(tokens, dp)
    weights_in.run()
    tok_a, tok_rest, pos = settle([weights_in], tok_a, tokens[half:], pos)
    tok_b = over_x(tok_rest)
    tok_a_sib = swap_core(tok_a, dp)
    weights_in.run()
    table = env["make_tables"](pos)
    tok_b, cot_first, _ = settle([weights_in], tok_b, cotangent[:half], table[:8])
    cot_a = over_x(cot_first)
    tok_b_sib = swap_core(tok_b, dp)
    weights_in.run()
    normed1, normed2, standard, mark = env["run_norm"](
        [(tokens, 0, 0), (tok_sib, 1, 0), (tok_a, 0, own_rows), (tok_b, 0, own_rows + half),
         (tok_a_sib, 1, own_rows), (tok_b_sib, 1, own_rows + half)], order[0],
    )
    cot_a, cot_rest, mark = settle([weights_in], cot_a, cotangent[half:], mark)
    cot_b = over_x(cot_rest)
    cot_a_sib = swap_core(cot_a, dp)
    cot_sib = swap_core(cotangent, dp)
    weights_in.run()
    cot_b, cot_a_sib, cot_sib = settle([weights_in], cot_b, cot_a_sib, cot_sib)
    wa, w1 = weights_in.result()
    cot_b_sib = swap_core(cot_b, dp)
    weights_out.run()
    qkv, mark = env["run_qkv"](normed1, table, wa, order[0])
    settle([weights_out], mark)
    weights_out.run()
    hidden, slope, mark = env["run_fc1"](normed2, w1, order[0])
    cot_b_sib, mark = settle([weights_out], cot_b_sib, mark)
    weights_out.run()
    cot, mark = env["run_turn"](
        [(cotangent, 0, 0), (cot_sib, 1, 0), (cot_a, 0, own_rows), (cot_b, 0, own_rows + half),
         (cot_a_sib, 1, own_rows), (cot_b_sib, 1, own_rows + half)], order[0],
    )
    settle([weights_out], mark)
    weights_out.run()
    att_grad, mark = env["run_att_grad"](cot, wa, order[0])

    def run_att(which, h):
        return env["run_attention"](qkv, att_grad, table, which, h, order[1])

    def run_tail(which, got):
        return env["run_tail"](
            which, hidden, pre_grad, standard, [x[0] for x in got], [x[1] for x in got], w1, w2, wa, order[0]
        )

    settle([weights_out], mark)
    (w2,) = weights_out.result()
    pre_grad, bias_fc1 = env["run_pre_grad"](cot, slope, w2, order[0])
    grad_fc2 = dot(cot, hidden, TN).astype(BF)
    grad_fc1 = dot(normed2, pre_grad, TN).astype(BF)
    grad_ff = reorder_kernel([grad_fc1, grad_fc2], order[0], chips, False)
    grad_ff, mark = settle([], grad_ff, bias_fc1)
    own_ff = lax.psum_scatter(grad_ff, "dp", scatter_dimension=0, tiled=True, axis_index_groups=sets)
    first = [run_att(0, h) for h in range(groups)]
    part0, *sums0 = run_tail(0, first)
    part0, mark = settle([], part0, sums0[0])
    sent0 = env["to_owner"](0, part0)
    second = [run_att(1, 0)]
    sent0, _ = settle([], sent0, second[0][2])
    out0, grad0 = pair_add_kernel(order[0], part0, sent0)
    out0 = env["reduce_x"](0, out0)
    second += [run_att(1, h) for h in range(1, groups)]
    out0, grad0, mark = settle([], out0, grad0, second[-1][2])
    grad0 = env["reduce_x"](0, grad0)
    part1, *sums1 = run_tail(1, second)
    grad0, part1, own_ff, mark = settle([], grad0, part1, own_ff, sums1[0])
    sent1 = env["to_owner"](1, part1)
    bias_qkv = jnp.concatenate([a[2] + b[2] for a, b in zip(first, second)], axis=1)
    small = env["small_sums"]([a + b for a, b in zip(sums0, sums1)], bias_qkv, bias_fc1)
    grad_att, mark = att_weight_kernel(
        order[0], normed1, cot, [x[0] for x in (*first, *second)], [x[1] for x in (*first, *second)]
    )
    sent1, mark, small = settle([], sent1, mark, small)
    scattered = Scatter(ring, [grad_att])
    scattered.run()
    out1, grad1 = pair_add_kernel(order[0], part1, sent1)
    out1, grad1, mark = settle([scattered], out1, grad1, mark)
    out1 = env["reduce_x"](1, out1)
    steps = [1 << k for k in range(dp.bit_length() - 1)]
    middle = chips // 2 - 2
    for i in range(middle):
        scattered.run()
        if steps:
            small = sum_step(small, "dp", dp, steps.pop(0))
        if i == 0:
            own = own_kernel(order[0], [(part0, sent0), (part1, sent1)])
        values = [small, own] + ([out1] if i == middle - 1 else [])
        small, own, *out1_now = settle([scattered], *values)
    (out1,) = out1_now
    grad1 = env["reduce_x"](1, grad1)
    scattered.run()
    if steps:
        small = sum_step(small, "dp", dp, steps.pop(0))
    (small,) = settle([scattered], small)
    wide, cols = env["hidden_cols"], env["qkv_cols"]
    for step in steps:
        small = sum_step(small, "dp", dp, step)
    weights = share_weights(env, scattered.result(), (0, cols, wide))
    weights += share_weights(env, [own_ff], (0, wide, 2 * wide))
    parts = [(x, 0) for x in (own[0], out0, out1, own[1], grad0, grad1)]
    return dict(parts=parts, small=small, weights=weights)


def solution(mesh):
    both, weight = P(("dp", "tensor"), None), P("dp", "tensor")
    return jax.shard_map(
        functools.partial(shards, mesh.shape["dp"], mesh.shape["tensor"]),
        mesh=mesh,
        in_specs=(both, P("dp"), both, weight, P("tensor"), weight, P(), weight, P("tensor"), weight, P(), P(), P(), P(), P()),
        out_specs=(both, both, weight, P("tensor"), weight, P(), weight, P("tensor"), weight, P(), P(), P(), P(), P()),
        check_vma=False,
    )
```

```python
import functools

import jax
import jax.numpy as jnp
from jax import lax
from jax.experimental import pallas as pl
from jax.experimental.pallas import tpu as pltpu
from jax.sharding import PartitionSpec as P

HEAD = 64
ROT = 16
SEQ_LEN = 1024
EPSILON = 1e-05
LANES = 128
BF = jnp.bfloat16
F32 = jnp.float32
NN = (((1,), (0,)), ((), ()))
NT = (((1,), (1,)), ((), ()))
TN = (((0,), (0,)), ((), ()))


def dot(first_op, second_op, dims=NN):
    return lax.dot_general(first_op, second_op, dims, preferred_element_type=F32)


class Order:
    def __init__(self, index, marks=()):
        self.index, self.marks = index, list(marks)
        self.shape = index.shape


def call(kernel, grid, in_specs, out_specs, out_shape, operands, flops, scratch=(), index=None, vmem=28):
    moved = sum(x.size * x.dtype.itemsize for x in operands)
    moved += sum(s.size * jnp.dtype(s.dtype).itemsize for s in out_shape)
    marks = []
    if isinstance(index, Order):
        index, marks = index.index, index.marks
    first, count = (0 if index is None else 1) + len(operands), len(marks)

    def body(*refs):
        kernel(*refs[:first], *refs[first + count :])

    return pl.pallas_call(
        body,
        grid_spec=pltpu.PrefetchScalarGridSpec(
            num_scalar_prefetch=0 if index is None else 1,
            grid=grid,
            in_specs=[*in_specs, *[pl.BlockSpec(memory_space=pl.ANY)] * count],
            out_specs=out_specs,
            scratch_shapes=list(scratch),
        ),
        out_shape=out_shape,
        compiler_params=pltpu.CompilerParams(vmem_limit_bytes=vmem * 2**20),
        cost_estimate=pl.CostEstimate(flops=flops, bytes_accessed=moved, transcendentals=0),
    )(*(() if index is None else (index,)), *operands, *marks)


def shape_of(rows, cols, kind=BF):
    return jax.ShapeDtypeStruct((rows, cols), kind)


def row_kernel(body, rows, block, row_ins, full_ins, row_outs, sum_outs, flops, index):
    steps = rows // block
    n_index = 1

    def at_row(first):
        return lambda step, *_: (step + first // block, 0)

    def at_zero(step, *_):
        return (0, 0)

    in_specs = [pl.BlockSpec((block, x.shape[1]), at_row(first)) for x, first in row_ins]
    in_specs += [pl.BlockSpec(x.shape, at_zero, pipeline_mode=pl.Buffered(1)) for x in full_ins]
    def out_spec(cols):
        if isinstance(cols, tuple):
            return pl.BlockSpec((cols[0], block, cols[1]), lambda step, *_: (0, step, 0))
        return pl.BlockSpec((block, cols), at_row(0))

    out_specs = [out_spec(cols) for cols, _ in row_outs]
    out_specs += [pl.BlockSpec((1, width), at_zero) for width in sum_outs]
    out_shape = [
        jax.ShapeDtypeStruct((cols[0], rows, cols[1]), kind) if isinstance(cols, tuple) else shape_of(rows, cols, kind)
        for cols, kind in row_outs
    ]
    out_shape += [shape_of(1, width, F32) for width in sum_outs]
    n_in, n_out = len(in_specs), len(row_outs)

    def kernel(*refs):
        ins = refs[: n_index + n_in]
        outs = refs[n_index + n_in : n_index + n_in + n_out]
        sums = refs[n_index + n_in + n_out :]
        if sums:

            @pl.when(pl.program_id(0) == 0)
            def _():
                for ref in sums:
                    ref[...] = jnp.zeros_like(ref)

        body(ins, outs, sums)

    operands = [x for x, _ in row_ins] + list(full_ins)
    return call(kernel, (steps,), in_specs, out_specs, out_shape, operands, flops, index=index)


def moments(vectors):
    row_mean = jnp.mean(vectors, axis=-1, keepdims=True)
    centered = vectors - row_mean
    spread = jnp.mean(centered * centered, axis=-1, keepdims=True)
    return centered, lax.rsqrt(spread + EPSILON)


def pieces_kernel(body, pieces, index, full_ins, row_outs, block):
    count = len(pieces)
    width = pieces[0][0].shape[1]
    rows = sum(x.shape[0] for x, _, _ in pieces)
    core_at = index.shape[0] - 1

    def slot(side, first, core):
        return (jnp.bitwise_xor(side, core) * (rows // 2) + first) // block

    def at_piece(x, side, first):
        return lambda step, idx: (jnp.clip(step - slot(side, first, idx[core_at]), 0, x.shape[0] // block - 1), 0)

    def kernel(idx, *refs):
        ins, fulls = refs[:count], refs[count : count + len(full_ins)]
        outs = refs[count + len(full_ins) : count + len(full_ins) + len(row_outs)]
        mark, scratch = refs[-2:]
        mark[...] = jnp.zeros_like(mark)
        step = pl.program_id(0)
        for ref, (x, side, first) in zip(ins, pieces):
            start = slot(side, first, idx[core_at])

            @pl.when((step >= start) & (step < start + x.shape[0] // block))
            def _(ref=ref):
                scratch[...] = ref[...].astype(F32)

        body(idx, fulls, outs, scratch)

    return call(
        kernel,
        (rows // block,),
        [pl.BlockSpec((block, width), at_piece(*p)) for p in pieces]
        + [pl.BlockSpec(x.shape, lambda step, _: (0, 0)) for x in full_ins],
        [pl.BlockSpec((block, width), lambda step, _: (step, 0)) for _ in row_outs]
        + [pl.BlockSpec((1, LANES), lambda step, _: (0, 0))],
        [*[shape_of(rows, width, kind) for kind in row_outs], shape_of(1, LANES, F32)],
        [*[x for x, _, _ in pieces], *full_ins],
        30 * rows * width,
        scratch=[pltpu.VMEM((block, width), F32)],
        index=index,
    )


def block_at(perm, place, width, count):
    if count == 1:
        return pl.ds(0, width)
    return pl.ds(pl.multiple_of(perm[place] * width, width), width)


def norm_body(count, perm, fulls, outs, scratch):
    gain_one, shift_one, gain_two, shift_two = fulls
    normed1, normed2, standard = outs
    centered, inverse = moments(scratch[...])
    scratch[...] = centered * inverse
    width = scratch.shape[1] // count
    for p in range(count):
        here = slice(p * width, (p + 1) * width)
        there = block_at(perm, p, width, count)
        part = scratch[:, there]
        normed1[:, here] = (part * gain_one[:, there] + shift_one[:, there]).astype(BF)
        normed2[:, here] = (part * gain_two[:, there] + shift_two[:, there]).astype(BF)
        standard[:, here] = part.astype(BF)


def turn_body(count, perm, fulls, outs, scratch):
    width = scratch.shape[1] // count
    for p in range(count):
        outs[0][:, p * width : (p + 1) * width] = scratch[:, block_at(perm, p, width, count)].astype(BF)


def lane_roll(x, shift):
    if x.shape[1] == LANES:
        return pltpu.roll(x, shift % LANES, 1)
    return jnp.roll(x, shift, axis=1)


def turned(x, table, sign):
    back = ROT // 2
    lane = lax.broadcasted_iota(jnp.int32, x.shape, 1) % HEAD
    sine = lane_roll(table, -ROT)
    moved = jnp.where(lane < back, -lane_roll(x, -back), lane_roll(x, back)) * sine
    total = x * table + moved if sign > 0 else x * table - moved
    return jnp.where(lane < ROT, total, x)


def by_kind(parts):
    if parts[0].shape[1] < LANES:
        return parts
    first, second, third = parts
    low = lax.broadcasted_iota(jnp.int32, first.shape, 1) < HEAD
    return (
        jnp.where(low, first, second),
        jnp.where(low, lane_roll(first, HEAD), lane_roll(third, HEAD)),
        jnp.where(low, second, third),
    )


def by_head(query, key, value):
    if query.shape[1] < LANES:
        return query, key, value
    low = lax.broadcasted_iota(jnp.int32, query.shape, 1) < HEAD
    swapped = lane_roll(key, HEAD)
    return jnp.where(low, query, swapped), jnp.where(low, value, query), jnp.where(low, swapped, value)


def qkv_body(groups, ins, outs, sums):
    _, normed, table, weight, bias = ins
    width = table.shape[1]
    for h in range(groups):
        cols = slice(3 * h * width, 3 * (h + 1) * width)
        mixed = dot(normed[...], weight[:, cols]) + bias[:, cols]
        query, key, value = by_kind([mixed[:, i * width : (i + 1) * width] for i in range(3)])
        outs[0][h] = turned(query, table[...], 1).astype(BF)
        outs[0][groups + h] = turned(key, table[...], 1).astype(BF)
        outs[0][2 * groups + h] = value.astype(BF)


def fc1_body(ins, outs, sums):
    _, normed, weight, bias = ins
    cols = weight.shape[1]
    step = min(256, cols)
    for j in range(cols // step):
        here = slice(j * step, (j + 1) * step)
        pre = dot(normed[...], weight[:, here]) + bias[:, here]
        phi = 0.5 * (1.0 + lax.erf(pre * 0.7071067811865476))
        outs[0][:, here] = (pre * phi).astype(BF)
        outs[1][:, here] = (phi + pre * jnp.exp(-0.5 * pre * pre) * 0.3989422804014327).astype(BF)


def pre_grad_body(ins, outs, sums):
    _, cot, slope, weight = ins
    grad = (dot(cot[...], weight[...]) * slope[...].astype(F32)).astype(BF)
    outs[0][...] = grad
    sums[0][...] += jnp.sum(grad.astype(F32), axis=0, keepdims=True)


def att_grad_body(cols, ins, outs, sums):
    _, cot, w_att = ins
    grad = dot(cot[...], w_att[:, cols:]).astype(BF)
    groups, _, width = outs[0].shape
    for h in range(groups):
        outs[0][h] = grad[:, h * width : (h + 1) * width]


def tail_body(groups, count, ins, outs, sums):
    perm, hidden, pre_grad, standard = ins[:4]
    attended, grads = ins[4 : 4 + groups], ins[4 + groups : 4 + 2 * groups]
    w1, w2, wa, gain_one, gain_two = ins[4 + 2 * groups :]
    dense = groups * grads[0].shape[1]
    att = jnp.concatenate([x[...] for x in attended], axis=1)
    grad = jnp.concatenate([x[...] for x in grads], axis=1)
    width = standard.shape[1] // count
    step = min(256, standard.shape[1])
    for j in range(standard.shape[1] // step):
        cols = slice(j * step, (j + 1) * step)
        total = dot(hidden[...], w2[cols, :], NT) + dot(att, wa[cols, dense:], NT)
        outs[0][0, :, cols] = total.astype(BF)
        two = dot(pre_grad[...], w1[cols, :], NT)
        one = dot(grad, wa[cols, :dense], NT)
        std = standard[:, cols].astype(F32)
        values = (one * std, one, two * std, two)
        values = [jnp.sum(v, axis=0, keepdims=True) for v in values]
        if count == 1:
            for ref, value in zip(sums, values):
                ref[:, cols] += value
            outs[0][1, :, cols] = (one * gain_one[:, cols] + two * gain_two[:, cols]).astype(BF)
            continue
        for k in range(step // width):
            there = block_at(perm, j * (step // width) + k, width, count)
            part = slice(k * width, (k + 1) * width)
            for ref, value in zip(sums, values):
                ref[:, there] += value[:, part]
            scaled = one[:, part] * gain_one[:, there] + two[:, part] * gain_two[:, there]
            outs[0][1, :, j * step + k * width : j * step + (k + 1) * width] = scaled.astype(BF)


def att_weight_body(groups, rows, _, *refs):
    normed, cot = refs[:2]
    attended, grads = refs[2 : 2 + 2 * groups], refs[2 + 2 * groups : 2 + 4 * groups]
    out, mark, joined = refs[-3:]
    mark[...] = jnp.zeros_like(mark)
    width, wide = attended[0].shape[1], grads[0].shape[1]
    dense = groups * wide

    @pl.when(pl.program_id(0) == 0)
    def _():
        for which in range(2):
            here = slice(which * rows, (which + 1) * rows)
            for h in range(groups):
                joined[here, h * wide : (h + 1) * wide] = grads[which * groups + h][...]
                joined[here, dense + h * width : dense + (h + 1) * width] = attended[which * groups + h][...]

    out[:, :dense] = dot(normed[...], joined[:, :dense], TN).astype(BF)
    out[:, dense:] = dot(cot[...], joined[:, dense:], TN).astype(BF)


def att_weight_kernel(index, normed, cot, attended, grads):
    groups = len(attended) // 2
    rows, depth = normed.shape
    cols = sum(x.shape[1] for x in (*attended[:groups], *grads[:groups]))
    step = min(256, depth)

    def whole(x):
        return pl.BlockSpec(x.shape, lambda i, _: (0, 0), pipeline_mode=pl.Buffered(1))

    return call(
        functools.partial(att_weight_body, groups, rows // 2),
        (depth // step,),
        [pl.BlockSpec((rows, step), lambda i, _: (0, i))] * 2 + [whole(x) for x in (*attended, *grads)],
        [pl.BlockSpec((step, cols), lambda i, _: (i, 0)), pl.BlockSpec((1, LANES), lambda i, _: (0, 0))],
        [shape_of(depth, cols), shape_of(1, LANES, F32)],
        [normed, cot, *attended, *grads],
        2 * rows * depth * cols,
        scratch=[pltpu.VMEM((rows, cols), BF)],
        index=index,
        vmem=56,
    )


def attention_kernel(flip, q_ref, k_ref, v_ref, g_ref, table_ref, att_ref, out_ref, sum_ref, keys, values, q_acc, key_acc, value_acc):
    _, _, halves, length, width = q_ref.shape
    per = width // HEAD
    block = min(256, length)

    def place(half):
        return half if halves == 1 else jnp.bitwise_xor(half, flip[0])

    @pl.when(pl.program_id(0) == 0)
    def _():
        sum_ref[...] = jnp.zeros_like(sum_ref)

    for half in range(halves):
        rows = slice(half * length, (half + 1) * length)
        keys[rows, :] = k_ref[0, 0, place(half)]
        values[rows, :] = v_ref[0, 0, place(half)]
    key_acc[...] = jnp.zeros_like(key_acc)
    value_acc[...] = jnp.zeros_like(value_acc)
    lane = lax.broadcasted_iota(jnp.int32, (block, width), 1)
    scale = HEAD ** (-0.5)

    for i in range(halves * length // block):
        half, offset = i * block // length, i * block % length
        here = pl.ds(offset, block)
        extent = (i + 1) * block
        q_all = q_ref[0, 0, place(half), here, :]
        g_all = g_ref[0, 0, place(half), here, :]
        key_rows = keys[:extent, :]
        value_rows = values[:extent, :]
        causal = (
            lax.broadcasted_iota(jnp.int32, (block, extent), 0) + i * block
            >= lax.broadcasted_iota(jnp.int32, (block, extent), 1)
        )
        att_total = jnp.zeros((block, width), F32)
        query_total = jnp.zeros((block, width), F32)
        for h in range(per):
            mine = (lane >= h * HEAD) & (lane < (h + 1) * HEAD)
            q = jnp.where(mine, q_all.astype(F32) * scale, 0.0).astype(BF)
            g = jnp.where(mine, g_all.astype(F32), 0.0).astype(BF)
            scores = jnp.where(causal, dot(q, key_rows, NT), -1e30)
            expon = jnp.exp(scores - jnp.max(scores, axis=-1, keepdims=True))
            probs = expon * (1.0 / jnp.sum(expon, axis=-1, keepdims=True))
            low = probs.astype(BF)
            result = jnp.where(mine, dot(low, value_rows), 0.0)
            prob_grad = dot(g, value_rows, NT)
            row_dot = jnp.sum(result * g.astype(F32), axis=-1, keepdims=True)
            score_grad = (probs * (prob_grad - row_dot)).astype(BF)
            att_total += result
            query_total += jnp.where(mine, dot(score_grad, key_rows), 0.0)
            key_acc[:extent, :] += dot(score_grad, q, TN)
            value_acc[:extent, :] += dot(low, g, TN)
        att_ref[0, place(half), here, :] = att_total.astype(BF)
        q_acc[i * block : (i + 1) * block, :] = query_total
    for half in range(halves):
        rows = slice(half * length, (half + 1) * length)
        table = table_ref[0, place(half)]
        query = turned(q_acc[rows, :] * scale, table, -1)
        key = turned(key_acc[rows, :], table, -1)
        for j, part in enumerate(by_head(query, key, value_acc[rows, :])):
            part = part.astype(BF)
            out_ref[0, place(half), :, j * width : (j + 1) * width] = part
            sum_ref[:, j * width : (j + 1) * width] += jnp.sum(part.astype(F32), axis=0, keepdims=True)


def attention(qkv, grad, table, flip, halves, which, group):
    groups, total, width = grad.shape
    length = SEQ_LEN // halves
    seqs = total // SEQ_LEN
    own = seqs // 2

    def split(x):
        return x.reshape(*x.shape[:-2], seqs, halves, length, width)

    def spec(at):
        return pl.BlockSpec((1, 1, halves, length, width), lambda s, _: (at, which * own + s, 0, 0, 0))

    def out_spec(cols):
        return pl.BlockSpec((1, halves, length, cols), lambda s, _: (s, 0, 0, 0))

    acc = pltpu.VMEM((SEQ_LEN, width), F32)
    low = pltpu.VMEM((SEQ_LEN, width), BF)
    att, out, sums = call(
        attention_kernel,
        (own,),
        [*[spec(base * groups + group) for base in range(3)], spec(group)]
        + [pl.BlockSpec((1, halves, length, width), lambda s, _: (which * own + s, 0, 0, 0))],
        [out_spec(width), out_spec(3 * width), pl.BlockSpec((1, 3 * width), lambda s, _: (0, 0))],
        [
            jax.ShapeDtypeStruct((own, halves, length, width), BF),
            jax.ShapeDtypeStruct((own, halves, length, 3 * width), BF),
            shape_of(1, 3 * width, F32),
        ],
        [split(qkv)] * 3 + [split(grad), split(table)],
        own * (width // HEAD) * 12 * SEQ_LEN * SEQ_LEN * 256 * 5 // 8,
        scratch=[low, low, acc, acc, acc],
        index=flip,
    )
    return att.reshape(-1, width), out.reshape(-1, 3 * width), sums


def table_kernel(positions, flip, halves, repeat):
    rows = positions.shape[1]
    width, half_rot = repeat * HEAD, ROT // 2
    length = SEQ_LEN // halves

    def kernel(flip_ref, pos_ref, out):
        index = lax.broadcasted_iota(jnp.int32, (half_rot, 1), 0).astype(F32)
        frequencies = jnp.exp(index * (-9.210340371976184 / half_rot))
        frequencies = jnp.where(index == 0.0, 1.0, frequencies)
        angles = frequencies * pos_ref[...].astype(F32)
        lane = lax.broadcasted_iota(jnp.int32, (half_rot, width), 1) % HEAD
        place = lax.broadcasted_iota(jnp.int32, (half_rot, width), 0)
        first = ((lane == place) | (lane == place + half_rot)).astype(F32)
        second = ((lane == place + ROT) | (lane == place + ROT + half_rot)).astype(F32)

        def spread(x, y):
            return lax.dot_general(x, y, TN, precision=lax.Precision.HIGHEST, preferred_element_type=F32)

        table = spread(jnp.cos(angles), first) + spread(jnp.sin(angles), second)
        for f in range(halves):

            @pl.when(flip_ref[0] == f)
            def _(f=f):
                for start in range(0, rows, SEQ_LEN):
                    for half in range(halves):
                        there = start + (half ^ f) * length
                        here = start + half * length
                        out[there : there + length, :] = table[here : here + length, :]

    return one_step(kernel, [positions], [shape_of(rows, width, F32)], index=flip)[0]


def final_body(count, n_parts, ins, outs, sums):
    perm, tokens, cot = ins[:3]
    parts, bias = ins[3:-1], ins[-1]
    width = tokens.shape[1] // count

    def total(refs):
        value = refs[0][...].astype(F32)
        for ref in refs[1:]:
            value = value + ref[...].astype(F32)
        return value

    out_total, grad_total = total(parts[:n_parts]), total(parts[n_parts:])
    scratch = outs[2]
    for p in range(count):
        there = block_at(perm, p, width, count)
        here = slice(p * width, (p + 1) * width)
        scratch[:, there] = grad_total[:, here]
        outs[0][:, there] = (tokens[:, there].astype(F32) + out_total[:, here] + bias[:, there]).astype(BF)
    grad = scratch[...]
    centered, inverse = moments(tokens[...].astype(F32))
    standard = centered * inverse
    through = inverse * (
        grad
        - jnp.mean(grad, axis=-1, keepdims=True)
        - standard * jnp.mean(grad * standard, axis=-1, keepdims=True)
    )
    outs[1][...] = (cot[...].astype(F32) + through).astype(BF)


def pair_add_kernel(index, part, got):
    _, rows, width = part.shape
    rows //= 2
    block = min(256, rows)
    per = rows // block

    def kernel(_, part_ref, got_ref, *outs):
        for k in range(2):
            outs[k][...] = (part_ref[k].astype(F32) + got_ref[k].astype(F32)).astype(BF)

    high = pl.BlockSpec((2, block, width), lambda i, _: (0, i + per, 0))
    other = pl.BlockSpec((block, width), lambda i, _: (i, 0))
    return call(
        kernel, (per,), [high, high], [other, other], [shape_of(rows, width)] * 2, [part, got], 2 * rows * width,
        index=index,
    )


def own_kernel(index, pairs):
    _, rows, width = pairs[0][0].shape
    rows //= 2
    block = min(256, rows)

    def kernel(idx, *refs):
        zero, one = (refs[2 * i][...].astype(F32) + refs[2 * i + 1][...].astype(F32) for i in range(2))
        total = jnp.where(idx[idx.shape[0] - 1] == 0, zero, one).astype(BF)
        refs[-2][...], refs[-1][...] = total[0], total[1]

    low = pl.BlockSpec((2, block, width), lambda i, _: (0, i, 0))
    own = pl.BlockSpec((block, width), lambda i, _: (i, 0))
    operands = [x for pair in pairs for x in pair]
    return call(
        kernel, (rows // block,), [low] * 4, [own] * 2, [shape_of(rows, width)] * 2, operands, 6 * rows * width,
        index=index,
    )


def one_step(kernel, operands, shapes, index=None):
    def whole(shape):
        return pl.BlockSpec(shape, lambda i, *_: (0,) * len(shape))

    return call(
        kernel, (1,), [whole(x.shape) for x in operands], [whole(s.shape) for s in shapes], shapes, operands, 0,
        index=index, vmem=40,
    )


def split_kernel(core, weights):
    w_qkv, w_dense, w_fc1, w_fc2 = weights
    rows = w_qkv.shape[0]
    cols = [w.shape[1] // 2 for w in weights]

    def kernel(core_ref, qkv, dense, fc1, fc2, *outs):
        for c in range(2):

            @pl.when(core_ref[0] == c)
            def _(c=c):
                for out, k in zip(outs, (c, 1 - c)):
                    out[:rows, : cols[0]] = qkv[:, k * cols[0] : (k + 1) * cols[0]]
                    out[:rows, cols[0] :] = dense[:, k * cols[1] : (k + 1) * cols[1]]
                    out[rows : 2 * rows, :] = fc1[:, k * cols[2] : (k + 1) * cols[2]]
                    out[2 * rows :, :] = fc2[:, k * cols[3] : (k + 1) * cols[3]]

    return one_step(kernel, list(weights), [shape_of(3 * rows, cols[2])] * 2, index=core)


def place_kernel(core, mine, other):
    rows = mine.shape[0] // 3

    def kernel(core_ref, a, b, first, second):
        for c in range(2):

            @pl.when(core_ref[0] == c)
            def _(c=c):
                for ref, k in ((a, c), (b, 1 - c)):
                    first[k * rows : (k + 1) * rows, :] = ref[:rows, :]
                    first[(2 + k) * rows : (3 + k) * rows, :] = ref[rows : 2 * rows, :]
                    second[k * rows : (k + 1) * rows, :] = ref[2 * rows :, :]

    cols = mine.shape[1]
    return one_step(kernel, [mine, other], [shape_of(4 * rows, cols), shape_of(2 * rows, cols)], index=core)


def join_kernel(blocks, stack):
    rows = blocks[0].shape[0] // stack
    whole = sum(b.shape[0] for b in blocks) // stack

    def kernel(*refs):
        outs = refs[-stack:]
        first, filled = 0, 0
        for ref in refs[:-stack]:
            if ref.shape[0] == stack * rows:
                for k in range(stack):
                    outs[k][first : first + rows, :] = ref[k * rows : (k + 1) * rows, :]
                first += rows
                continue
            got = ref.shape[0]
            place = first + (filled % rows)
            outs[filled // rows][place : place + got, :] = ref[...]
            filled += got
            if filled == stack * rows:
                first += rows

    return one_step(kernel, blocks, [shape_of(whole, blocks[0].shape[1])] * stack)


def reorder_kernel(arrays, perm, count, gather):
    rows, cols = arrays[0].shape
    block = rows // count
    wide = cols * len(arrays)

    def kernel(_, *refs):
        for i, ref in enumerate(refs[:-1]):
            refs[-1][:, i * cols : (i + 1) * cols] = ref[...]

    def moved(p, perm_ref):
        return (perm_ref[p], 0)

    def plain(p, _):
        return (p, 0)

    return call(
        kernel,
        (count,),
        [pl.BlockSpec((block, cols), moved if gather else plain)] * len(arrays),
        [pl.BlockSpec((block, wide), plain if gather else moved)],
        [shape_of(rows, wide)],
        arrays,
        0,
        index=perm,
    )[0]


def share_kernel(core, parts):
    rows = parts[0].shape[0] // 2

    def kernel(core_ref, *refs):
        for c in range(2):

            @pl.when(core_ref[0] == c)
            def _(c=c):
                for out, k in zip(refs[-2:], (c, 1 - c)):
                    here = slice(k * rows, (k + 1) * rows)
                    total = refs[0][here, :].astype(F32)
                    for ref in refs[1:-2]:
                        total = total + ref[here, :].astype(F32)
                    out[...] = total

    return one_step(kernel, list(parts), [shape_of(rows, parts[0].shape[1], F32)] * 2, index=core)


def columns_kernel(core, mine, other, cuts):
    rows = mine.shape[0]

    def kernel(core_ref, a, b, *outs):
        for c in range(2):

            @pl.when(core_ref[0] == c)
            def _(c=c):
                for out, low, high in zip(outs, cuts, cuts[1:]):
                    cols = high - low
                    out[:, c * cols : (c + 1) * cols] = a[:, low:high]
                    out[:, (1 - c) * cols : (2 - c) * cols] = b[:, low:high]

    shapes = [shape_of(rows, 2 * (high - low), F32) for low, high in zip(cuts, cuts[1:])]
    return one_step(kernel, [mine, other], shapes, index=core)


def add_kernel(grads, chips, places, received, spans):
    block = grads[0].shape[0] // chips
    cols = grads[0].shape[1]
    count = len(grads)

    def whole(shape):
        return pl.BlockSpec(shape, lambda i: (0, 0))

    def kernel(*refs):
        for way in range(2):
            ins = refs[way * count : (way + 1) * count]
            out = refs[-2 + way]
            low, high = spans[way]
            for i in range(count):
                if received is None:
                    size = high - low
                    out[i * size : (i + 1) * size, :] = ins[i][low:high, :]
                    continue
                got = refs[2 * count + way]
                size = high - low
                first = i * block
                if low:
                    out[first : first + low, :] = ins[i][:low, :]
                if high < block:
                    out[first + high : first + block, :] = ins[i][high:, :]
                total = ins[i][low:high, :].astype(F32) + got[i * size : (i + 1) * size, :].astype(F32)
                out[first + low : first + high, :] = total.astype(BF)

    specs = [
        pl.BlockSpec((block, cols), functools.partial(lambda place, i: (place, 0), places[way]))
        for way in range(2)
        for _ in range(count)
    ]
    operands = [*grads, *grads]
    out_rows = [count * block] * 2
    if received is None:
        out_rows = [count * (high - low) for low, high in spans]
    else:
        specs += [whole(x.shape) for x in received]
        operands += list(received)
    return call(
        kernel, (1,), specs, [whole((r, cols)) for r in out_rows], [shape_of(r, cols) for r in out_rows], operands, 0
    )


def swap_core(x, size):
    return lax.ppermute(x, "dp", [(i, i ^ 1) for i in range(size)])


def tie(*trees):
    return lax.optimization_barrier(trees)


def sum_step(x, axis, size, step):
    return x + lax.ppermute(x, axis, [(i, i ^ step) for i in range(size)])


def sum_over(x, axis, size):
    if size & (size - 1):
        return lax.psum(x, axis)
    step = 1
    while step < size:
        x = sum_step(x, axis, size, step)
        step *= 2
    return x


class Ring:
    def __init__(self, chips):
        self.chips = chips
        order = [2 * i for i in range(chips // 2)] + [2 * i + 1 for i in reversed(range(chips // 2))]
        self.order = order
        places = [0] * chips
        for place, chip in enumerate(order):
            places[chip] = place
        mine = jnp.asarray(places, jnp.int32)[lax.axis_index("dp") // 2]
        self.perm = jnp.asarray(order, jnp.int32)[(mine + jnp.arange(chips)) % chips]
        self.inverse = (jnp.asarray(places, jnp.int32) - mine) % chips

    def send(self, x, step):
        pairs = []
        for place, chip in enumerate(self.order):
            other = self.order[(place + step) % self.chips]
            pairs += [(2 * chip + c, 2 * other + c) for c in range(2)]
        return lax.ppermute(x, "dp", pairs)


class Gather:
    def __init__(self, ring, x, stack):
        self.ring, self.step, self.last, self.stack = ring, 0, (x, x), stack
        self.blocks = [x] + [None] * (ring.chips - 1)

    def run(self):
        self.step += 1
        up, down = self.last
        if self.step == self.ring.chips // 2:
            half = up.shape[0] // 2
            up, down = up[:half], down[half:]
        self.last = (self.ring.send(up, 1), self.ring.send(down, -1))

    def keep(self):
        up, down = self.last
        if self.step == self.ring.chips // 2:
            self.middle = [up, down]
        else:
            self.blocks[self.ring.chips - self.step], self.blocks[self.step] = up, down

    def result(self):
        middle = self.ring.chips // 2
        return join_kernel([*self.blocks[:middle], *self.middle, *self.blocks[middle + 1 :]], self.stack)


class Scatter:
    def __init__(self, ring, grads):
        self.ring, self.grads, self.step, self.last = ring, grads, 0, None

    def run(self):
        chips = self.ring.chips
        middle, block = chips // 2, self.grads[0].shape[0] // chips
        places = (middle - self.step, middle + self.step)
        if self.step < 2:
            spans = ((0, block // 2), (block // 2, block))
        else:
            spans = ((0, block), (0, block))
        up, down = add_kernel(self.grads, chips, places, self.last, spans)
        self.step += 1
        self.last = (self.ring.send(up, 1), self.ring.send(down, -1))

    def result(self):
        rows = self.grads[0].shape[0] // self.ring.chips
        return [self.grads[0][:rows], *self.last]


def shards(dp, tensor, *arrays):
    tokens, positions, cotangent, w_qkv, b_qkv, w_dense, b_dense, w_fc1, b_fc1, w_fc2, b_fc2 = arrays[:11]
    norm1_gain, norm1_shift, norm2_gain, norm2_shift = arrays[11:]
    core = lax.axis_index("dp") % 2
    own_rows, width = tokens.shape
    row_share = w_qkv.shape[0]
    heads = w_qkv.shape[1] // (3 * HEAD) // 2
    qkv_cols, dense_cols = 3 * heads * HEAD, heads * HEAD
    groups = heads // 2 if heads % 2 == 0 else heads
    chips = dp // 2
    ringed = chips % 2 == 0 and chips >= 4 and (2 * row_share) % LANES == 0 and chips * 2 * row_share == width
    halves = 2 if tensor == 2 and 2 * own_rows == SEQ_LEN else 1
    core_index = core.astype(jnp.int32).reshape(1)
    block, row_block = 256, 512

    if ringed:
        ring = Ring(chips)
        count = chips
        perm = jnp.concatenate([ring.perm, core_index])
    else:
        count = 1
        perm = jnp.concatenate([jnp.zeros((1,), jnp.int32), core_index])

    def over_x(x):
        return lax.ppermute(x, "tensor", [(0, 1), (1, 0)])

    flip = (lax.axis_index("tensor") if halves == 2 else jnp.int32(0)).astype(jnp.int32).reshape(1)

    def make_tables(both):
        repeat = 2 if heads % 2 == 0 else 1
        return table_kernel(both, flip, halves, repeat)

    gains = tuple(v.reshape(1, width) for v in (norm1_gain, norm1_shift, norm2_gain, norm2_shift))
    gain_one, _, gain_two, _ = gains
    hidden_cols = w_fc1.shape[1] // 2
    b1 = lax.dynamic_slice(b_fc1, (core * hidden_cols,), (hidden_cols,)).reshape(1, hidden_cols)
    bq = lax.dynamic_slice(b_qkv, (core * qkv_cols,), (qkv_cols,)).reshape(1, qkv_cols)
    rows = 2 * own_rows * tensor
    group_rows = rows // 2
    work = 2 * rows * width * hidden_cols

    mine, other = split_kernel(core_index, (w_qkv, w_dense, w_fc1, w_fc2))
    in_rows, fc2_rows = place_kernel(core_index, mine, swap_core(other, dp))
    pos = positions.reshape(1, -1)
    other = swap_core(pos, dp)
    positions_two = jnp.where(
        core == 0, jnp.concatenate([pos, other], axis=1), jnp.concatenate([other, pos], axis=1)
    )

    def run_norm(pieces, order=perm):
        return pieces_kernel(functools.partial(norm_body, count), pieces, order, gains, (BF, BF, BF), block)

    def run_turn(pieces, order=perm):
        return pieces_kernel(functools.partial(turn_body, count), pieces, order, (), (BF,), block)

    def run_qkv(normed1, table, wa, order=perm):
        return row_kernel(
            functools.partial(qkv_body, groups), rows, row_block, [(normed1, 0), (table, 0)], (wa, bq),
            (((3 * groups, dense_cols // groups), BF),), (LANES,), 2 * rows * width * qkv_cols, order,
        )

    def run_fc1(normed2, w1, order=perm):
        return row_kernel(
            fc1_body, rows, row_block, [(normed2, 0)], (w1, b1), ((hidden_cols, BF), (hidden_cols, BF)), (LANES,), work, order
        )

    def run_att_grad(cot, wa, order=perm):
        return row_kernel(
            functools.partial(att_grad_body, qkv_cols), rows, row_block, [(cot, 0)], (wa,), (((groups, dense_cols // groups), BF),), (LANES,),
            2 * rows * width * dense_cols, order,
        )

    def run_pre_grad(cot, slope, w2, order=perm):
        return row_kernel(
            pre_grad_body, rows, row_block, [(cot, 0), (slope, 0)], (w2,), ((hidden_cols, BF),), (hidden_cols,), work, order
        )

    def run_tail(which, hidden, pre_grad, standard, attended, grads, w1, w2, wa, order=perm):
        first = which * group_rows
        return row_kernel(
            functools.partial(tail_body, groups, count), group_rows, row_block,
            [(hidden, first), (pre_grad, first), (standard, first), *[(x, 0) for x in (*attended, *grads)]],
            (w1, w2, wa, gain_one, gain_two), (((2, width), BF),), (width,) * 4,
            work + group_rows * width * (qkv_cols + dense_cols) * 2, order,
        )

    def run_attention(qkv, att_grad, table, which, group, order=flip):
        return attention(qkv, att_grad, table, order, halves, which, group)

    def to_owner(which, part):
        return lax.ppermute(part, "dp", [(2 * k + 1 - which, 2 * k + which) for k in range(chips)])

    out_bias = jnp.sum(cotangent.astype(F32), axis=0, keepdims=True)

    def small_sums(sums, bias_qkv, bias_fc1):
        wide = jnp.concatenate([*sums, out_bias], axis=1)
        wide = sum_over(wide, "tensor", tensor)
        narrow = jnp.concatenate([bias_qkv, bias_fc1], axis=1)
        zero = jnp.zeros_like(narrow)
        return jnp.concatenate([wide, jnp.where(core == 0, narrow, zero), jnp.where(core == 0, zero, narrow)], axis=1)

    def reduce_x(which, other):
        pairs = [(2 * i + x, 2 * i + 1 - x) for i in range(which, dp, 2) for x in range(2)]
        return lax.ppermute(other, ("dp", "tensor"), pairs)

    if ringed and halves == 2:
        flow = ring_flow
    else:
        flow = plain_flow
    env = dict(locals())
    results = flow(env)
    final_block = min(256, own_rows)
    parts = results["parts"]
    output, grad_tokens, _ = row_kernel(
        functools.partial(final_body, count, len(parts) // 2), own_rows, final_block,
        [(tokens, 0), (cotangent, 0), *parts],
        ((b_dense + b_fc2).reshape(1, width),), ((width, BF), (width, BF), (width, F32)), (), 0, perm,
    )

    small = results["small"]
    wide, first, second = jnp.split(small[0], [5 * width, 5 * width + qkv_cols + hidden_cols])
    wide = wide.reshape(5, width)
    bias_qkv = jnp.concatenate([first[:qkv_cols], second[:qkv_cols]])
    bias_fc1 = jnp.concatenate([first[qkv_cols:], second[qkv_cols:]])
    grad_w_qkv, grad_w_dense, grad_w_fc1, grad_w_fc2 = results["weights"]
    return (
        output, grad_tokens, grad_w_qkv, bias_qkv, grad_w_dense, wide[4], grad_w_fc1, bias_fc1, grad_w_fc2, wide[4],
        wide[0], wide[1], wide[2], wide[3],
    )


def plain_flow(env):
    dp, chips, groups = env["dp"], env["chips"], env["groups"]
    core, perm = env["core"], env["perm"]
    sets = [[2 * k + c for k in range(chips)] for c in range(2)]

    def gather(x):
        return lax.all_gather(x, "dp", axis=0, tiled=True, axis_index_groups=sets)

    def scatter(x):
        return lax.psum_scatter(x, "dp", scatter_dimension=0, tiled=True, axis_index_groups=sets)

    def pieces(x):
        x = lax.all_gather(x, "tensor", axis=0, tiled=True)
        return [(x, 0, 0), (swap_core(x, dp), 1, 0)]

    half = env["in_rows"].shape[0] // 2
    wa, w1, w2 = gather(env["in_rows"][:half]), gather(env["in_rows"][half:]), gather(env["fc2_rows"])
    table = env["make_tables"](env["positions_two"])
    normed1, normed2, standard, _ = env["run_norm"](pieces(env["tokens"]))
    cot, _ = env["run_turn"](pieces(env["cotangent"]))
    hidden, slope, _ = env["run_fc1"](normed2, w1)
    pre_grad, bias_fc1 = env["run_pre_grad"](cot, slope, w2)
    qkv, _ = env["run_qkv"](normed1, table, wa)
    att_grad, _ = env["run_att_grad"](cot, wa)
    attended, grads, sums, totals, biases = [], [], [0.0] * 4, [], []
    for which in range(2):
        got = [env["run_attention"](qkv, att_grad, table, which, h) for h in range(groups)]
        attended += [x[0] for x in got]
        grads += [x[1] for x in got]
        biases.append(jnp.concatenate([x[2] for x in got], axis=1))
        part, *some = env["run_tail"](
            which, hidden, pre_grad, standard, attended[-groups:], grads[-groups:], w1, w2, wa
        )
        sums = [a + b for a, b in zip(sums, some)]
        part = part + env["to_owner"](which, part)
        totals.append([lax.psum_scatter(part[k], "tensor", scatter_dimension=0, tiled=True) for k in range(2)])
    cols = env["qkv_cols"]
    ff = [scatter(x) for x in (dot(normed2, pre_grad, TN).astype(BF), dot(cot, hidden, TN).astype(BF))]
    grad_att = att_weight_kernel(perm, normed1, cot, attended, grads)[0]
    weights = share_weights(env, [scatter(grad_att)], (0, cols, ff[0].shape[1]))
    weights += share_weights(env, [jnp.concatenate(ff, axis=1)], (0, ff[0].shape[1], 2 * ff[0].shape[1]))
    small = env["small_sums"](sums, biases[0] + biases[1], bias_fc1)
    parts = [(jnp.where(core == 0, totals[0][k], totals[1][k]), 0) for k in range(2)]
    return dict(parts=parts, small=sum_over(small, "dp", dp), weights=weights)


def share_weights(env, parts, cuts):
    mine, other = share_kernel(env["core_index"], parts)
    return list(columns_kernel(env["core_index"], mine, swap_core(other, env["dp"]), cuts))


def ring_flow(env):
    dp, ring, groups, chips = env["dp"], env["ring"], env["groups"], env["chips"]
    over_x, own_rows = env["over_x"], env["own_rows"]
    tokens, cotangent, pos = env["tokens"], env["cotangent"], env["positions_two"]
    sets = [[2 * k + c for k in range(chips)] for c in range(2)]
    half = own_rows // 2
    order = [Order(env["perm"]), Order(env["flip"])]

    def settle(rings, *values):
        lasts, values = tie([r.last for r in rings], list(values))
        marks = [x for x in jax.tree.leaves(values) if x.size <= 8 * LANES]
        order[:] = [Order(o.index, marks) for o in order]
        for r, last in zip(rings, lasts):
            r.last = last
            if isinstance(r, Gather):
                r.keep()
        return values

    weights_in = Gather(ring, env["in_rows"], 2)
    weights_out = Gather(ring, env["fc2_rows"], 1)

    tok_a = over_x(tokens[:half])
    tok_sib = swap_core(tokens, dp)
    weights_in.run()
    tok_a, tok_rest, pos = settle([weights_in], tok_a, tokens[half:], pos)
    tok_b = over_x(tok_rest)
    tok_a_sib = swap_core(tok_a, dp)
    weights_in.run()
    table = env["make_tables"](pos)
    tok_b, cot_first, _ = settle([weights_in], tok_b, cotangent[:half], table[:8])
    cot_a = over_x(cot_first)
    tok_b_sib = swap_core(tok_b, dp)
    weights_in.run()
    normed1, normed2, standard, mark = env["run_norm"](
        [(tokens, 0, 0), (tok_sib, 1, 0), (tok_a, 0, own_rows), (tok_b, 0, own_rows + half),
         (tok_a_sib, 1, own_rows), (tok_b_sib, 1, own_rows + half)], order[0],
    )
    cot_a, cot_rest, mark = settle([weights_in], cot_a, cotangent[half:], mark)
    cot_b = over_x(cot_rest)
    cot_a_sib = swap_core(cot_a, dp)
    cot_sib = swap_core(cotangent, dp)
    weights_in.run()
    cot_b, cot_a_sib, cot_sib = settle([weights_in], cot_b, cot_a_sib, cot_sib)
    wa, w1 = weights_in.result()
    cot_b_sib = swap_core(cot_b, dp)
    weights_out.run()
    qkv, mark = env["run_qkv"](normed1, table, wa, order[0])
    settle([weights_out], mark)
    weights_out.run()
    hidden, slope, mark = env["run_fc1"](normed2, w1, order[0])
    cot_b_sib, mark = settle([weights_out], cot_b_sib, mark)
    weights_out.run()
    cot, mark = env["run_turn"](
        [(cotangent, 0, 0), (cot_sib, 1, 0), (cot_a, 0, own_rows), (cot_b, 0, own_rows + half),
         (cot_a_sib, 1, own_rows), (cot_b_sib, 1, own_rows + half)], order[0],
    )
    settle([weights_out], mark)
    weights_out.run()
    att_grad, mark = env["run_att_grad"](cot, wa, order[0])

    def run_att(which, h):
        return env["run_attention"](qkv, att_grad, table, which, h, order[1])

    def run_tail(which, got):
        return env["run_tail"](
            which, hidden, pre_grad, standard, [x[0] for x in got], [x[1] for x in got], w1, w2, wa, order[0]
        )

    settle([weights_out], mark)
    (w2,) = weights_out.result()
    pre_grad, bias_fc1 = env["run_pre_grad"](cot, slope, w2, order[0])
    grad_fc2 = dot(cot, hidden, TN).astype(BF)
    grad_fc1 = dot(normed2, pre_grad, TN).astype(BF)
    grad_ff = reorder_kernel([grad_fc1, grad_fc2], order[0], chips, False)
    grad_ff, mark = settle([], grad_ff, bias_fc1)
    own_ff = lax.psum_scatter(grad_ff, "dp", scatter_dimension=0, tiled=True, axis_index_groups=sets)
    first = [run_att(0, h) for h in range(groups)]
    part0, *sums0 = run_tail(0, first)
    part0, mark = settle([], part0, sums0[0])
    sent0 = env["to_owner"](0, part0)
    second = [run_att(1, 0)]
    sent0, _ = settle([], sent0, second[0][2])
    out0, grad0 = pair_add_kernel(order[0], part0, sent0)
    out0 = env["reduce_x"](0, out0)
    second += [run_att(1, h) for h in range(1, groups)]
    out0, grad0, mark = settle([], out0, grad0, second[-1][2])
    grad0 = env["reduce_x"](0, grad0)
    part1, *sums1 = run_tail(1, second)
    grad0, part1, own_ff, mark = settle([], grad0, part1, own_ff, sums1[0])
    sent1 = env["to_owner"](1, part1)
    bias_qkv = jnp.concatenate([a[2] + b[2] for a, b in zip(first, second)], axis=1)
    small = env["small_sums"]([a + b for a, b in zip(sums0, sums1)], bias_qkv, bias_fc1)
    grad_att, mark = att_weight_kernel(
        order[0], normed1, cot, [x[0] for x in (*first, *second)], [x[1] for x in (*first, *second)]
    )
    sent1, mark, small = settle([], sent1, mark, small)
    scattered = Scatter(ring, [grad_att])
    scattered.run()
    steps = [1 << k for k in range(dp.bit_length() - 1)]
    if steps:
        small = sum_step(small, "dp", dp, steps.pop(0))
    out1, grad1 = pair_add_kernel(order[0], part1, sent1)
    out1, grad1, mark, small = settle([scattered], out1, grad1, mark, small)
    out1 = env["reduce_x"](1, out1)
    middle = chips // 2 - 2
    for i in range(middle):
        scattered.run()
        if steps:
            small = sum_step(small, "dp", dp, steps.pop(0))
        if i == 0:
            own = own_kernel(order[0], [(part0, sent0), (part1, sent1)])
        values = [small, own] + ([out1] if i == middle - 1 else [])
        small, own, *out1_now = settle([scattered], *values)
    (out1,) = out1_now
    grad1 = env["reduce_x"](1, grad1)
    scattered.run()
    if steps:
        small = sum_step(small, "dp", dp, steps.pop(0))
    (small,) = settle([scattered], small)
    wide, cols = env["hidden_cols"], env["qkv_cols"]
    for step in steps:
        small = sum_step(small, "dp", dp, step)
    weights = share_weights(env, scattered.result(), (0, cols, wide))
    weights += share_weights(env, [own_ff], (0, wide, 2 * wide))
    parts = [(x, 0) for x in (own[0], out0, out1, own[1], grad0, grad1)]
    return dict(parts=parts, small=small, weights=weights)


def solution(mesh):
    both, weight = P(("dp", "tensor"), None), P("dp", "tensor")
    return jax.shard_map(
        functools.partial(shards, mesh.shape["dp"], mesh.shape["tensor"]),
        mesh=mesh,
        in_specs=(both, P("dp"), both, weight, P("tensor"), weight, P(), weight, P("tensor"), weight, P(), P(), P(), P(), P()),
        out_specs=(both, both, weight, P("tensor"), weight, P(), weight, P("tensor"), weight, P(), P(), P(), P(), P()),
        check_vma=False,
    )
```

```python
import functools

import jax
import jax.numpy as jnp
from jax import lax
from jax.experimental import pallas as pl
from jax.experimental.pallas import tpu as pltpu
from jax.sharding import PartitionSpec as P

HEAD = 64
ROT = 16
SEQ_LEN = 1024
EPSILON = 1e-05
LANES = 128
BF = jnp.bfloat16
F32 = jnp.float32
NN = (((1,), (0,)), ((), ()))
NT = (((1,), (1,)), ((), ()))
TN = (((0,), (0,)), ((), ()))


def dot(first_op, second_op, dims=NN):
    return lax.dot_general(first_op, second_op, dims, preferred_element_type=F32)


class Order:
    def __init__(self, index, marks=()):
        self.index, self.marks = index, list(marks)
        self.shape = index.shape


def call(kernel, grid, in_specs, out_specs, out_shape, operands, flops, scratch=(), index=None, vmem=28):
    moved = sum(x.size * x.dtype.itemsize for x in operands)
    moved += sum(s.size * jnp.dtype(s.dtype).itemsize for s in out_shape)
    marks = []
    if isinstance(index, Order):
        index, marks = index.index, index.marks
    first, count = (0 if index is None else 1) + len(operands), len(marks)

    def body(*refs):
        kernel(*refs[:first], *refs[first + count :])

    return pl.pallas_call(
        body,
        grid_spec=pltpu.PrefetchScalarGridSpec(
            num_scalar_prefetch=0 if index is None else 1,
            grid=grid,
            in_specs=[*in_specs, *[pl.BlockSpec(memory_space=pl.ANY)] * count],
            out_specs=out_specs,
            scratch_shapes=list(scratch),
        ),
        out_shape=out_shape,
        compiler_params=pltpu.CompilerParams(vmem_limit_bytes=vmem * 2**20),
        cost_estimate=pl.CostEstimate(flops=flops, bytes_accessed=moved, transcendentals=0),
    )(*(() if index is None else (index,)), *operands, *marks)


def shape_of(rows, cols, kind=BF):
    return jax.ShapeDtypeStruct((rows, cols), kind)


def row_kernel(body, rows, block, row_ins, full_ins, row_outs, sum_outs, flops, index):
    steps = rows // block
    n_index = 1

    def at_row(first):
        return lambda step, *_: (step + first // block, 0)

    def at_zero(step, *_):
        return (0, 0)

    in_specs = [pl.BlockSpec((block, x.shape[1]), at_row(first)) for x, first in row_ins]
    in_specs += [pl.BlockSpec(x.shape, at_zero, pipeline_mode=pl.Buffered(1)) for x in full_ins]
    def out_spec(cols):
        if isinstance(cols, tuple):
            return pl.BlockSpec((cols[0], block, cols[1]), lambda step, *_: (0, step, 0))
        return pl.BlockSpec((block, cols), at_row(0))

    out_specs = [out_spec(cols) for cols, _ in row_outs]
    out_specs += [pl.BlockSpec((1, width), at_zero) for width in sum_outs]
    out_shape = [
        jax.ShapeDtypeStruct((cols[0], rows, cols[1]), kind) if isinstance(cols, tuple) else shape_of(rows, cols, kind)
        for cols, kind in row_outs
    ]
    out_shape += [shape_of(1, width, F32) for width in sum_outs]
    n_in, n_out = len(in_specs), len(row_outs)

    def kernel(*refs):
        ins = refs[: n_index + n_in]
        outs = refs[n_index + n_in : n_index + n_in + n_out]
        sums = refs[n_index + n_in + n_out :]
        if sums:

            @pl.when(pl.program_id(0) == 0)
            def _():
                for ref in sums:
                    ref[...] = jnp.zeros_like(ref)

        body(ins, outs, sums)

    operands = [x for x, _ in row_ins] + list(full_ins)
    return call(kernel, (steps,), in_specs, out_specs, out_shape, operands, flops, index=index)


def moments(vectors):
    row_mean = jnp.mean(vectors, axis=-1, keepdims=True)
    centered = vectors - row_mean
    spread = jnp.mean(centered * centered, axis=-1, keepdims=True)
    return centered, lax.rsqrt(spread + EPSILON)


def pieces_kernel(body, pieces, index, full_ins, row_outs, block):
    count = len(pieces)
    width = pieces[0][0].shape[1]
    rows = sum(x.shape[0] for x, _, _ in pieces)
    core_at = index.shape[0] - 1

    def slot(side, first, core):
        return (jnp.bitwise_xor(side, core) * (rows // 2) + first) // block

    def at_piece(x, side, first):
        return lambda step, idx: (jnp.clip(step - slot(side, first, idx[core_at]), 0, x.shape[0] // block - 1), 0)

    def kernel(idx, *refs):
        ins, fulls = refs[:count], refs[count : count + len(full_ins)]
        outs = refs[count + len(full_ins) : count + len(full_ins) + len(row_outs)]
        mark, scratch = refs[-2:]
        mark[...] = jnp.zeros_like(mark)
        step = pl.program_id(0)
        for ref, (x, side, first) in zip(ins, pieces):
            start = slot(side, first, idx[core_at])

            @pl.when((step >= start) & (step < start + x.shape[0] // block))
            def _(ref=ref):
                scratch[...] = ref[...].astype(F32)

        body(idx, fulls, outs, scratch)

    return call(
        kernel,
        (rows // block,),
        [pl.BlockSpec((block, width), at_piece(*p)) for p in pieces]
        + [pl.BlockSpec(x.shape, lambda step, _: (0, 0)) for x in full_ins],
        [pl.BlockSpec((block, width), lambda step, _: (step, 0)) for _ in row_outs]
        + [pl.BlockSpec((1, LANES), lambda step, _: (0, 0))],
        [*[shape_of(rows, width, kind) for kind in row_outs], shape_of(1, LANES, F32)],
        [*[x for x, _, _ in pieces], *full_ins],
        30 * rows * width,
        scratch=[pltpu.VMEM((block, width), F32)],
        index=index,
    )


def block_at(perm, place, width, count):
    if count == 1:
        return pl.ds(0, width)
    return pl.ds(pl.multiple_of(perm[place] * width, width), width)


def norm_body(count, perm, fulls, outs, scratch):
    gain_one, shift_one, gain_two, shift_two = fulls
    normed1, normed2, standard = outs
    centered, inverse = moments(scratch[...])
    scratch[...] = centered * inverse
    width = scratch.shape[1] // count
    for p in range(count):
        here = slice(p * width, (p + 1) * width)
        there = block_at(perm, p, width, count)
        part = scratch[:, there]
        normed1[:, here] = (part * gain_one[:, there] + shift_one[:, there]).astype(BF)
        normed2[:, here] = (part * gain_two[:, there] + shift_two[:, there]).astype(BF)
        standard[:, here] = part.astype(BF)


def turn_body(count, perm, fulls, outs, scratch):
    width = scratch.shape[1] // count
    for p in range(count):
        outs[0][:, p * width : (p + 1) * width] = scratch[:, block_at(perm, p, width, count)].astype(BF)


def lane_roll(x, shift):
    if x.shape[1] == LANES:
        return pltpu.roll(x, shift % LANES, 1)
    return jnp.roll(x, shift, axis=1)


def turned(x, table, sign):
    back = ROT // 2
    lane = lax.broadcasted_iota(jnp.int32, x.shape, 1) % HEAD
    sine = lane_roll(table, -ROT)
    moved = jnp.where(lane < back, -lane_roll(x, -back), lane_roll(x, back)) * sine
    total = x * table + moved if sign > 0 else x * table - moved
    return jnp.where(lane < ROT, total, x)


def by_kind(parts):
    if parts[0].shape[1] < LANES:
        return parts
    first, second, third = parts
    low = lax.broadcasted_iota(jnp.int32, first.shape, 1) < HEAD
    return (
        jnp.where(low, first, second),
        jnp.where(low, lane_roll(first, HEAD), lane_roll(third, HEAD)),
        jnp.where(low, second, third),
    )


def by_head(query, key, value):
    if query.shape[1] < LANES:
        return query, key, value
    low = lax.broadcasted_iota(jnp.int32, query.shape, 1) < HEAD
    swapped = lane_roll(key, HEAD)
    return jnp.where(low, query, swapped), jnp.where(low, value, query), jnp.where(low, swapped, value)


def qkv_body(groups, ins, outs, sums):
    _, normed, table, weight, bias = ins
    width = table.shape[1]
    for h in range(groups):
        cols = slice(3 * h * width, 3 * (h + 1) * width)
        mixed = dot(normed[...], weight[:, cols]) + bias[:, cols]
        query, key, value = by_kind([mixed[:, i * width : (i + 1) * width] for i in range(3)])
        outs[0][h] = turned(query, table[...], 1).astype(BF)
        outs[0][groups + h] = turned(key, table[...], 1).astype(BF)
        outs[0][2 * groups + h] = value.astype(BF)


def fc1_body(ins, outs, sums):
    _, normed, weight, bias = ins
    cols = weight.shape[1]
    step = min(256, cols)
    for j in range(cols // step):
        here = slice(j * step, (j + 1) * step)
        pre = dot(normed[...], weight[:, here]) + bias[:, here]
        phi = 0.5 * (1.0 + lax.erf(pre * 0.7071067811865476))
        outs[0][:, here] = (pre * phi).astype(BF)
        outs[1][:, here] = (phi + pre * jnp.exp(-0.5 * pre * pre) * 0.3989422804014327).astype(BF)


def pre_grad_body(ins, outs, sums):
    _, cot, slope, weight = ins
    grad = (dot(cot[...], weight[...]) * slope[...].astype(F32)).astype(BF)
    outs[0][...] = grad
    sums[0][...] += jnp.sum(grad.astype(F32), axis=0, keepdims=True)


def att_grad_body(cols, ins, outs, sums):
    _, cot, w_att = ins
    grad = dot(cot[...], w_att[:, cols:]).astype(BF)
    groups, _, width = outs[0].shape
    for h in range(groups):
        outs[0][h] = grad[:, h * width : (h + 1) * width]


def tail_body(groups, count, ins, outs, sums):
    perm, hidden, pre_grad, standard = ins[:4]
    attended, grads = ins[4 : 4 + groups], ins[4 + groups : 4 + 2 * groups]
    w1, w2, wa, gain_one, gain_two = ins[4 + 2 * groups :]
    dense = groups * grads[0].shape[1]
    att = jnp.concatenate([x[...] for x in attended], axis=1)
    grad = jnp.concatenate([x[...] for x in grads], axis=1)
    width = standard.shape[1] // count
    step = min(256, standard.shape[1])
    for j in range(standard.shape[1] // step):
        cols = slice(j * step, (j + 1) * step)
        total = dot(hidden[...], w2[cols, :], NT) + dot(att, wa[cols, dense:], NT)
        outs[0][0, :, cols] = total.astype(BF)
        two = dot(pre_grad[...], w1[cols, :], NT)
        one = dot(grad, wa[cols, :dense], NT)
        std = standard[:, cols].astype(F32)
        values = (one * std, one, two * std, two)
        values = [jnp.sum(v, axis=0, keepdims=True) for v in values]
        if count == 1:
            for ref, value in zip(sums, values):
                ref[:, cols] += value
            outs[0][1, :, cols] = (one * gain_one[:, cols] + two * gain_two[:, cols]).astype(BF)
            continue
        for k in range(step // width):
            there = block_at(perm, j * (step // width) + k, width, count)
            part = slice(k * width, (k + 1) * width)
            for ref, value in zip(sums, values):
                ref[:, there] += value[:, part]
            scaled = one[:, part] * gain_one[:, there] + two[:, part] * gain_two[:, there]
            outs[0][1, :, j * step + k * width : j * step + (k + 1) * width] = scaled.astype(BF)


def att_weight_body(groups, rows, _, *refs):
    normed, cot = refs[:2]
    attended, grads = refs[2 : 2 + 2 * groups], refs[2 + 2 * groups : 2 + 4 * groups]
    out, mark, joined = refs[-3:]
    mark[...] = jnp.zeros_like(mark)
    width, wide = attended[0].shape[1], grads[0].shape[1]
    dense = groups * wide

    @pl.when(pl.program_id(0) == 0)
    def _():
        for which in range(2):
            here = slice(which * rows, (which + 1) * rows)
            for h in range(groups):
                joined[here, h * wide : (h + 1) * wide] = grads[which * groups + h][...]
                joined[here, dense + h * width : dense + (h + 1) * width] = attended[which * groups + h][...]

    out[:, :dense] = dot(normed[...], joined[:, :dense], TN).astype(BF)
    out[:, dense:] = dot(cot[...], joined[:, dense:], TN).astype(BF)


def att_weight_kernel(index, normed, cot, attended, grads):
    groups = len(attended) // 2
    rows, depth = normed.shape
    cols = sum(x.shape[1] for x in (*attended[:groups], *grads[:groups]))
    step = min(256, depth)

    def whole(x):
        return pl.BlockSpec(x.shape, lambda i, _: (0, 0), pipeline_mode=pl.Buffered(1))

    return call(
        functools.partial(att_weight_body, groups, rows // 2),
        (depth // step,),
        [pl.BlockSpec((rows, step), lambda i, _: (0, i))] * 2 + [whole(x) for x in (*attended, *grads)],
        [pl.BlockSpec((step, cols), lambda i, _: (i, 0)), pl.BlockSpec((1, LANES), lambda i, _: (0, 0))],
        [shape_of(depth, cols), shape_of(1, LANES, F32)],
        [normed, cot, *attended, *grads],
        2 * rows * depth * cols,
        scratch=[pltpu.VMEM((rows, cols), BF)],
        index=index,
        vmem=56,
    )


def attention_kernel(
    places, flip, qkv_all, g_all, table_all, att_ref, out_ref, sum_ref,
    q_ref, k_ref, v_ref, g_ref, table_ref, keys, values, q_acc, key_acc, value_acc, sems,
):
    first, group, groups = places
    seq = first + pl.program_id(0)
    copies = [
        pltpu.make_async_copy(source, target, sems.at[i])
        for i, (source, target) in enumerate(
            [(qkv_all.at[k * groups + group, seq], ref) for k, ref in enumerate((q_ref, k_ref, v_ref))]
            + [(g_all.at[group, seq], g_ref), (table_all.at[seq], table_ref)]
        )
    ]
    for copy in copies:
        copy.start()
    for copy in copies:
        copy.wait()
    halves, length, width = q_ref.shape
    per = width // HEAD
    block = min(256, length)

    def place(half):
        return half if halves == 1 else jnp.bitwise_xor(half, flip[0])

    @pl.when(pl.program_id(0) == 0)
    def _():
        sum_ref[...] = jnp.zeros_like(sum_ref)

    for half in range(halves):
        rows = slice(half * length, (half + 1) * length)
        keys[rows, :] = k_ref[place(half)]
        values[rows, :] = v_ref[place(half)]
    key_acc[...] = jnp.zeros_like(key_acc)
    value_acc[...] = jnp.zeros_like(value_acc)
    lane = lax.broadcasted_iota(jnp.int32, (block, width), 1)
    scale = HEAD ** (-0.5)

    for i in range(halves * length // block):
        half, offset = i * block // length, i * block % length
        here = pl.ds(offset, block)
        extent = (i + 1) * block
        q_block = q_ref[place(half), here, :]
        g_block = g_ref[place(half), here, :]
        key_rows = keys[:extent, :]
        value_rows = values[:extent, :]
        causal = (
            lax.broadcasted_iota(jnp.int32, (block, extent), 0) + i * block
            >= lax.broadcasted_iota(jnp.int32, (block, extent), 1)
        )
        att_total = jnp.zeros((block, width), F32)
        query_total = jnp.zeros((block, width), F32)
        for h in range(per):
            mine = (lane >= h * HEAD) & (lane < (h + 1) * HEAD)
            q = jnp.where(mine, q_block.astype(F32) * scale, 0.0).astype(BF)
            g = jnp.where(mine, g_block.astype(F32), 0.0).astype(BF)
            scores = jnp.where(causal, dot(q, key_rows, NT), -1e30)
            expon = jnp.exp(scores - jnp.max(scores, axis=-1, keepdims=True))
            probs = expon * (1.0 / jnp.sum(expon, axis=-1, keepdims=True))
            low = probs.astype(BF)
            result = jnp.where(mine, dot(low, value_rows), 0.0)
            prob_grad = dot(g, value_rows, NT)
            row_dot = jnp.sum(result * g.astype(F32), axis=-1, keepdims=True)
            score_grad = (probs * (prob_grad - row_dot)).astype(BF)
            att_total += result
            query_total += jnp.where(mine, dot(score_grad, key_rows), 0.0)
            key_acc[:extent, :] += dot(score_grad, q, TN)
            value_acc[:extent, :] += dot(low, g, TN)
        att_ref[0, place(half), here, :] = att_total.astype(BF)
        q_acc[i * block : (i + 1) * block, :] = query_total
    for half in range(halves):
        rows = slice(half * length, (half + 1) * length)
        table = table_ref[place(half)]
        query = turned(q_acc[rows, :] * scale, table, -1)
        key = turned(key_acc[rows, :], table, -1)
        for j, part in enumerate(by_head(query, key, value_acc[rows, :])):
            part = part.astype(BF)
            out_ref[0, place(half), :, j * width : (j + 1) * width] = part
            sum_ref[:, j * width : (j + 1) * width] += jnp.sum(part.astype(F32), axis=0, keepdims=True)


def attention(qkv, grad, table, flip, halves, which, group):
    groups, total, width = grad.shape
    length = SEQ_LEN // halves
    seqs = total // SEQ_LEN
    own = seqs // 2

    def split(x):
        return x.reshape(*x.shape[:-2], seqs, halves, length, width)

    def out_spec(cols):
        return pl.BlockSpec((1, halves, length, cols), lambda s, _: (s, 0, 0, 0))

    acc = pltpu.VMEM((SEQ_LEN, width), F32)
    low = pltpu.VMEM((SEQ_LEN, width), BF)
    att, out, sums = call(
        functools.partial(attention_kernel, (which * own, group, groups)),
        (own,),
        [pl.BlockSpec(memory_space=pltpu.HBM)] * 3,
        [out_spec(width), out_spec(3 * width), pl.BlockSpec((1, 3 * width), lambda s, _: (0, 0))],
        [
            jax.ShapeDtypeStruct((own, halves, length, width), BF),
            jax.ShapeDtypeStruct((own, halves, length, 3 * width), BF),
            shape_of(1, 3 * width, F32),
        ],
        [split(qkv), split(grad), split(table)],
        own * (width // HEAD) * 12 * SEQ_LEN * SEQ_LEN * 256 * 5 // 8,
        scratch=[
            *[pltpu.VMEM((halves, length, width), kind) for kind in (BF, BF, BF, BF, F32)],
            low, low, acc, acc, acc, pltpu.SemaphoreType.DMA((5,)),
        ],
        index=flip,
    )
    return att.reshape(-1, width), out.reshape(-1, 3 * width), sums


def table_kernel(positions, flip, halves, repeat):
    rows = positions.shape[1]
    width, half_rot = repeat * HEAD, ROT // 2
    length = SEQ_LEN // halves

    def kernel(flip_ref, pos_ref, out):
        index = lax.broadcasted_iota(jnp.int32, (half_rot, 1), 0).astype(F32)
        frequencies = jnp.exp(index * (-9.210340371976184 / half_rot))
        frequencies = jnp.where(index == 0.0, 1.0, frequencies)
        angles = frequencies * pos_ref[...].astype(F32)
        lane = lax.broadcasted_iota(jnp.int32, (half_rot, width), 1) % HEAD
        place = lax.broadcasted_iota(jnp.int32, (half_rot, width), 0)
        first = ((lane == place) | (lane == place + half_rot)).astype(F32)
        second = ((lane == place + ROT) | (lane == place + ROT + half_rot)).astype(F32)

        def spread(x, y):
            return lax.dot_general(x, y, TN, precision=lax.Precision.HIGHEST, preferred_element_type=F32)

        table = spread(jnp.cos(angles), first) + spread(jnp.sin(angles), second)
        for f in range(halves):

            @pl.when(flip_ref[0] == f)
            def _(f=f):
                for start in range(0, rows, SEQ_LEN):
                    for half in range(halves):
                        there = start + (half ^ f) * length
                        here = start + half * length
                        out[there : there + length, :] = table[here : here + length, :]

    return one_step(kernel, [positions], [shape_of(rows, width, F32)], index=flip)[0]


def final_body(count, n_parts, ins, outs, sums):
    perm, tokens, cot = ins[:3]
    parts, bias = ins[3:-1], ins[-1]
    width = tokens.shape[1] // count

    def total(refs):
        value = refs[0][...].astype(F32)
        for ref in refs[1:]:
            value = value + ref[...].astype(F32)
        return value

    out_total, grad_total = total(parts[:n_parts]), total(parts[n_parts:])
    scratch = outs[2]
    for p in range(count):
        there = block_at(perm, p, width, count)
        here = slice(p * width, (p + 1) * width)
        scratch[:, there] = grad_total[:, here]
        outs[0][:, there] = (tokens[:, there].astype(F32) + out_total[:, here] + bias[:, there]).astype(BF)
    grad = scratch[...]
    centered, inverse = moments(tokens[...].astype(F32))
    standard = centered * inverse
    through = inverse * (
        grad
        - jnp.mean(grad, axis=-1, keepdims=True)
        - standard * jnp.mean(grad * standard, axis=-1, keepdims=True)
    )
    outs[1][...] = (cot[...].astype(F32) + through).astype(BF)


def pair_add_kernel(index, part, got):
    _, rows, width = part.shape
    rows //= 2
    block = min(256, rows)
    per = rows // block

    def kernel(_, part_ref, got_ref, *outs):
        for k in range(2):
            outs[k][...] = (part_ref[k].astype(F32) + got_ref[k].astype(F32)).astype(BF)

    high = pl.BlockSpec((2, block, width), lambda i, _: (0, i + per, 0))
    other = pl.BlockSpec((block, width), lambda i, _: (i, 0))
    return call(
        kernel, (per,), [high, high], [other, other], [shape_of(rows, width)] * 2, [part, got], 2 * rows * width,
        index=index,
    )


def own_kernel(index, pairs):
    _, rows, width = pairs[0][0].shape
    rows //= 2
    block = min(256, rows)

    def kernel(idx, *refs):
        zero, one = (refs[2 * i][...].astype(F32) + refs[2 * i + 1][...].astype(F32) for i in range(2))
        total = jnp.where(idx[idx.shape[0] - 1] == 0, zero, one).astype(BF)
        refs[-2][...], refs[-1][...] = total[0], total[1]

    low = pl.BlockSpec((2, block, width), lambda i, _: (0, i, 0))
    own = pl.BlockSpec((block, width), lambda i, _: (i, 0))
    operands = [x for pair in pairs for x in pair]
    return call(
        kernel, (rows // block,), [low] * 4, [own] * 2, [shape_of(rows, width)] * 2, operands, 6 * rows * width,
        index=index,
    )


def one_step(kernel, operands, shapes, index=None):
    def whole(shape):
        return pl.BlockSpec(shape, lambda i, *_: (0,) * len(shape))

    return call(
        kernel, (1,), [whole(x.shape) for x in operands], [whole(s.shape) for s in shapes], shapes, operands, 0,
        index=index, vmem=40,
    )


def split_kernel(core, weights):
    w_qkv, w_dense, w_fc1, w_fc2 = weights
    rows = w_qkv.shape[0]
    cols = [w.shape[1] // 2 for w in weights]

    def kernel(core_ref, qkv, dense, fc1, fc2, *outs):
        for c in range(2):

            @pl.when(core_ref[0] == c)
            def _(c=c):
                for out, k in zip(outs, (c, 1 - c)):
                    out[:rows, : cols[0]] = qkv[:, k * cols[0] : (k + 1) * cols[0]]
                    out[:rows, cols[0] :] = dense[:, k * cols[1] : (k + 1) * cols[1]]
                    out[rows : 2 * rows, :] = fc1[:, k * cols[2] : (k + 1) * cols[2]]
                    out[2 * rows :, :] = fc2[:, k * cols[3] : (k + 1) * cols[3]]

    return one_step(kernel, list(weights), [shape_of(3 * rows, cols[2])] * 2, index=core)


def place_kernel(core, mine, other):
    rows = mine.shape[0] // 3

    def kernel(core_ref, a, b, first, second):
        for c in range(2):

            @pl.when(core_ref[0] == c)
            def _(c=c):
                for ref, k in ((a, c), (b, 1 - c)):
                    first[k * rows : (k + 1) * rows, :] = ref[:rows, :]
                    first[(2 + k) * rows : (3 + k) * rows, :] = ref[rows : 2 * rows, :]
                    second[k * rows : (k + 1) * rows, :] = ref[2 * rows :, :]

    cols = mine.shape[1]
    return one_step(kernel, [mine, other], [shape_of(4 * rows, cols), shape_of(2 * rows, cols)], index=core)


def join_kernel(blocks, stack):
    rows = blocks[0].shape[0] // stack
    whole = sum(b.shape[0] for b in blocks) // stack

    def kernel(*refs):
        outs = refs[-stack:]
        first, filled = 0, 0
        for ref in refs[:-stack]:
            if ref.shape[0] == stack * rows:
                for k in range(stack):
                    outs[k][first : first + rows, :] = ref[k * rows : (k + 1) * rows, :]
                first += rows
                continue
            got = ref.shape[0]
            place = first + (filled % rows)
            outs[filled // rows][place : place + got, :] = ref[...]
            filled += got
            if filled == stack * rows:
                first += rows

    return one_step(kernel, blocks, [shape_of(whole, blocks[0].shape[1])] * stack)


def reorder_kernel(arrays, perm, count, gather):
    rows, cols = arrays[0].shape
    block = rows // count
    wide = cols * len(arrays)

    def kernel(_, *refs):
        for i, ref in enumerate(refs[:-1]):
            refs[-1][:, i * cols : (i + 1) * cols] = ref[...]

    def moved(p, perm_ref):
        return (perm_ref[p], 0)

    def plain(p, _):
        return (p, 0)

    return call(
        kernel,
        (count,),
        [pl.BlockSpec((block, cols), moved if gather else plain)] * len(arrays),
        [pl.BlockSpec((block, wide), plain if gather else moved)],
        [shape_of(rows, wide)],
        arrays,
        0,
        index=perm,
    )[0]


def share_kernel(core, parts):
    rows = parts[0].shape[0] // 2

    def kernel(core_ref, *refs):
        for c in range(2):

            @pl.when(core_ref[0] == c)
            def _(c=c):
                for out, k in zip(refs[-2:], (c, 1 - c)):
                    here = slice(k * rows, (k + 1) * rows)
                    total = refs[0][here, :].astype(F32)
                    for ref in refs[1:-2]:
                        total = total + ref[here, :].astype(F32)
                    out[...] = total

    return one_step(kernel, list(parts), [shape_of(rows, parts[0].shape[1], F32)] * 2, index=core)


def columns_kernel(core, mine, other, cuts):
    rows = mine.shape[0]

    def kernel(core_ref, a, b, *outs):
        for c in range(2):

            @pl.when(core_ref[0] == c)
            def _(c=c):
                for out, low, high in zip(outs, cuts, cuts[1:]):
                    cols = high - low
                    out[:, c * cols : (c + 1) * cols] = a[:, low:high]
                    out[:, (1 - c) * cols : (2 - c) * cols] = b[:, low:high]

    shapes = [shape_of(rows, 2 * (high - low), F32) for low, high in zip(cuts, cuts[1:])]
    return one_step(kernel, [mine, other], shapes, index=core)


def add_kernel(grads, chips, places, received, spans):
    block = grads[0].shape[0] // chips
    cols = grads[0].shape[1]
    count = len(grads)

    def whole(shape):
        return pl.BlockSpec(shape, lambda i: (0, 0))

    def kernel(*refs):
        for way in range(2):
            ins = refs[way * count : (way + 1) * count]
            out = refs[-2 + way]
            low, high = spans[way]
            for i in range(count):
                if received is None:
                    size = high - low
                    out[i * size : (i + 1) * size, :] = ins[i][low:high, :]
                    continue
                got = refs[2 * count + way]
                size = high - low
                first = i * block
                if low:
                    out[first : first + low, :] = ins[i][:low, :]
                if high < block:
                    out[first + high : first + block, :] = ins[i][high:, :]
                total = ins[i][low:high, :].astype(F32) + got[i * size : (i + 1) * size, :].astype(F32)
                out[first + low : first + high, :] = total.astype(BF)

    specs = [
        pl.BlockSpec((block, cols), functools.partial(lambda place, i: (place, 0), places[way]))
        for way in range(2)
        for _ in range(count)
    ]
    operands = [*grads, *grads]
    out_rows = [count * block] * 2
    if received is None:
        out_rows = [count * (high - low) for low, high in spans]
    else:
        specs += [whole(x.shape) for x in received]
        operands += list(received)
    return call(
        kernel, (1,), specs, [whole((r, cols)) for r in out_rows], [shape_of(r, cols) for r in out_rows], operands, 0
    )


def swap_core(x, size):
    return lax.ppermute(x, "dp", [(i, i ^ 1) for i in range(size)])


def tie(*trees):
    return lax.optimization_barrier(trees)


def sum_step(x, axis, size, step):
    return x + lax.ppermute(x, axis, [(i, i ^ step) for i in range(size)])


def sum_over(x, axis, size):
    if size & (size - 1):
        return lax.psum(x, axis)
    step = 1
    while step < size:
        x = sum_step(x, axis, size, step)
        step *= 2
    return x


class Ring:
    def __init__(self, chips):
        self.chips = chips
        order = [2 * i for i in range(chips // 2)] + [2 * i + 1 for i in reversed(range(chips // 2))]
        self.order = order
        places = [0] * chips
        for place, chip in enumerate(order):
            places[chip] = place
        mine = jnp.asarray(places, jnp.int32)[lax.axis_index("dp") // 2]
        self.perm = jnp.asarray(order, jnp.int32)[(mine + jnp.arange(chips)) % chips]
        self.inverse = (jnp.asarray(places, jnp.int32) - mine) % chips

    def send(self, x, step):
        pairs = []
        for place, chip in enumerate(self.order):
            other = self.order[(place + step) % self.chips]
            pairs += [(2 * chip + c, 2 * other + c) for c in range(2)]
        return lax.ppermute(x, "dp", pairs)


class Gather:
    def __init__(self, ring, x, stack):
        self.ring, self.step, self.last, self.stack = ring, 0, (x, x), stack
        self.blocks = [x] + [None] * (ring.chips - 1)

    def run(self):
        self.step += 1
        up, down = self.last
        if self.step == self.ring.chips // 2:
            half = up.shape[0] // 2
            up, down = up[:half], down[half:]
        self.last = (self.ring.send(up, 1), self.ring.send(down, -1))

    def keep(self):
        up, down = self.last
        if self.step == self.ring.chips // 2:
            self.middle = [up, down]
        else:
            self.blocks[self.ring.chips - self.step], self.blocks[self.step] = up, down

    def result(self):
        middle = self.ring.chips // 2
        return join_kernel([*self.blocks[:middle], *self.middle, *self.blocks[middle + 1 :]], self.stack)


class Scatter:
    def __init__(self, ring, grads):
        self.ring, self.grads, self.step, self.last = ring, grads, 0, None

    def run(self):
        chips = self.ring.chips
        middle, block = chips // 2, self.grads[0].shape[0] // chips
        places = (middle - self.step, middle + self.step)
        if self.step < 2:
            spans = ((0, block // 2), (block // 2, block))
        else:
            spans = ((0, block), (0, block))
        up, down = add_kernel(self.grads, chips, places, self.last, spans)
        self.step += 1
        self.last = (self.ring.send(up, 1), self.ring.send(down, -1))

    def result(self):
        rows = self.grads[0].shape[0] // self.ring.chips
        return [self.grads[0][:rows], *self.last]


def shards(dp, tensor, *arrays):
    tokens, positions, cotangent, w_qkv, b_qkv, w_dense, b_dense, w_fc1, b_fc1, w_fc2, b_fc2 = arrays[:11]
    norm1_gain, norm1_shift, norm2_gain, norm2_shift = arrays[11:]
    core = lax.axis_index("dp") % 2
    own_rows, width = tokens.shape
    row_share = w_qkv.shape[0]
    heads = w_qkv.shape[1] // (3 * HEAD) // 2
    qkv_cols, dense_cols = 3 * heads * HEAD, heads * HEAD
    groups = heads // 2 if heads % 2 == 0 else heads
    chips = dp // 2
    ringed = chips % 2 == 0 and chips >= 4 and (2 * row_share) % LANES == 0 and chips * 2 * row_share == width
    halves = 2 if tensor == 2 and 2 * own_rows == SEQ_LEN else 1
    core_index = core.astype(jnp.int32).reshape(1)
    block, row_block = 256, 512

    if ringed:
        ring = Ring(chips)
        count = chips
        perm = jnp.concatenate([ring.perm, core_index])
    else:
        count = 1
        perm = jnp.concatenate([jnp.zeros((1,), jnp.int32), core_index])

    def over_x(x):
        return lax.ppermute(x, "tensor", [(0, 1), (1, 0)])

    flip = (lax.axis_index("tensor") if halves == 2 else jnp.int32(0)).astype(jnp.int32).reshape(1)

    def make_tables(both):
        repeat = 2 if heads % 2 == 0 else 1
        return table_kernel(both, flip, halves, repeat)

    gains = tuple(v.reshape(1, width) for v in (norm1_gain, norm1_shift, norm2_gain, norm2_shift))
    gain_one, _, gain_two, _ = gains
    hidden_cols = w_fc1.shape[1] // 2
    b1 = lax.dynamic_slice(b_fc1, (core * hidden_cols,), (hidden_cols,)).reshape(1, hidden_cols)
    bq = lax.dynamic_slice(b_qkv, (core * qkv_cols,), (qkv_cols,)).reshape(1, qkv_cols)
    rows = 2 * own_rows * tensor
    group_rows = rows // 2
    work = 2 * rows * width * hidden_cols

    mine, other = split_kernel(core_index, (w_qkv, w_dense, w_fc1, w_fc2))
    in_rows, fc2_rows = place_kernel(core_index, mine, swap_core(other, dp))
    pos = positions.reshape(1, -1)
    other = swap_core(pos, dp)
    positions_two = jnp.where(
        core == 0, jnp.concatenate([pos, other], axis=1), jnp.concatenate([other, pos], axis=1)
    )

    def run_norm(pieces, order=perm):
        return pieces_kernel(functools.partial(norm_body, count), pieces, order, gains, (BF, BF, BF), block)

    def run_turn(pieces, order=perm):
        return pieces_kernel(functools.partial(turn_body, count), pieces, order, (), (BF,), block)

    def run_qkv(normed1, table, wa, order=perm):
        return row_kernel(
            functools.partial(qkv_body, groups), rows, row_block, [(normed1, 0), (table, 0)], (wa, bq),
            (((3 * groups, dense_cols // groups), BF),), (LANES,), 2 * rows * width * qkv_cols, order,
        )

    def run_fc1(normed2, w1, order=perm):
        return row_kernel(
            fc1_body, rows, row_block, [(normed2, 0)], (w1, b1), ((hidden_cols, BF), (hidden_cols, BF)), (LANES,), work, order
        )

    def run_att_grad(cot, wa, order=perm):
        return row_kernel(
            functools.partial(att_grad_body, qkv_cols), rows, row_block, [(cot, 0)], (wa,), (((groups, dense_cols // groups), BF),), (LANES,),
            2 * rows * width * dense_cols, order,
        )

    def run_pre_grad(cot, slope, w2, order=perm):
        return row_kernel(
            pre_grad_body, rows, row_block, [(cot, 0), (slope, 0)], (w2,), ((hidden_cols, BF),), (hidden_cols,), work, order
        )

    def run_tail(which, hidden, pre_grad, standard, attended, grads, w1, w2, wa, order=perm):
        first = which * group_rows
        return row_kernel(
            functools.partial(tail_body, groups, count), group_rows, row_block,
            [(hidden, first), (pre_grad, first), (standard, first), *[(x, 0) for x in (*attended, *grads)]],
            (w1, w2, wa, gain_one, gain_two), (((2, width), BF),), (width,) * 4,
            work + group_rows * width * (qkv_cols + dense_cols) * 2, order,
        )

    def run_attention(qkv, att_grad, table, which, group, order=flip):
        return attention(qkv, att_grad, table, order, halves, which, group)

    def to_owner(which, part):
        return lax.ppermute(part, "dp", [(2 * k + 1 - which, 2 * k + which) for k in range(chips)])

    out_bias = jnp.sum(cotangent.astype(F32), axis=0, keepdims=True)

    def small_sums(sums, bias_qkv, bias_fc1):
        wide = jnp.concatenate([*sums, out_bias], axis=1)
        wide = sum_over(wide, "tensor", tensor)
        narrow = jnp.concatenate([bias_qkv, bias_fc1], axis=1)
        zero = jnp.zeros_like(narrow)
        return jnp.concatenate([wide, jnp.where(core == 0, narrow, zero), jnp.where(core == 0, zero, narrow)], axis=1)

    def reduce_x(which, other):
        pairs = [(2 * i + x, 2 * i + 1 - x) for i in range(which, dp, 2) for x in range(2)]
        return lax.ppermute(other, ("dp", "tensor"), pairs)

    if ringed and halves == 2:
        flow = ring_flow
    else:
        flow = plain_flow
    env = dict(locals())
    results = flow(env)
    final_block = min(256, own_rows)
    parts = results["parts"]
    output, grad_tokens, _ = row_kernel(
        functools.partial(final_body, count, len(parts) // 2), own_rows, final_block,
        [(tokens, 0), (cotangent, 0), *parts],
        ((b_dense + b_fc2).reshape(1, width),), ((width, BF), (width, BF), (width, F32)), (), 0, perm,
    )

    small = results["small"]
    wide, first, second = jnp.split(small[0], [5 * width, 5 * width + qkv_cols + hidden_cols])
    wide = wide.reshape(5, width)
    bias_qkv = jnp.concatenate([first[:qkv_cols], second[:qkv_cols]])
    bias_fc1 = jnp.concatenate([first[qkv_cols:], second[qkv_cols:]])
    grad_w_qkv, grad_w_dense, grad_w_fc1, grad_w_fc2 = results["weights"]
    return (
        output, grad_tokens, grad_w_qkv, bias_qkv, grad_w_dense, wide[4], grad_w_fc1, bias_fc1, grad_w_fc2, wide[4],
        wide[0], wide[1], wide[2], wide[3],
    )


def plain_flow(env):
    dp, chips, groups = env["dp"], env["chips"], env["groups"]
    core, perm = env["core"], env["perm"]
    sets = [[2 * k + c for k in range(chips)] for c in range(2)]

    def gather(x):
        return lax.all_gather(x, "dp", axis=0, tiled=True, axis_index_groups=sets)

    def scatter(x):
        return lax.psum_scatter(x, "dp", scatter_dimension=0, tiled=True, axis_index_groups=sets)

    def pieces(x):
        x = lax.all_gather(x, "tensor", axis=0, tiled=True)
        return [(x, 0, 0), (swap_core(x, dp), 1, 0)]

    half = env["in_rows"].shape[0] // 2
    wa, w1, w2 = gather(env["in_rows"][:half]), gather(env["in_rows"][half:]), gather(env["fc2_rows"])
    table = env["make_tables"](env["positions_two"])
    normed1, normed2, standard, _ = env["run_norm"](pieces(env["tokens"]))
    cot, _ = env["run_turn"](pieces(env["cotangent"]))
    hidden, slope, _ = env["run_fc1"](normed2, w1)
    pre_grad, bias_fc1 = env["run_pre_grad"](cot, slope, w2)
    qkv, _ = env["run_qkv"](normed1, table, wa)
    att_grad, _ = env["run_att_grad"](cot, wa)
    attended, grads, sums, totals, biases = [], [], [0.0] * 4, [], []
    for which in range(2):
        got = [env["run_attention"](qkv, att_grad, table, which, h) for h in range(groups)]
        attended += [x[0] for x in got]
        grads += [x[1] for x in got]
        biases.append(jnp.concatenate([x[2] for x in got], axis=1))
        part, *some = env["run_tail"](
            which, hidden, pre_grad, standard, attended[-groups:], grads[-groups:], w1, w2, wa
        )
        sums = [a + b for a, b in zip(sums, some)]
        part = part + env["to_owner"](which, part)
        totals.append([lax.psum_scatter(part[k], "tensor", scatter_dimension=0, tiled=True) for k in range(2)])
    cols = env["qkv_cols"]
    ff = [scatter(x) for x in (dot(normed2, pre_grad, TN).astype(BF), dot(cot, hidden, TN).astype(BF))]
    grad_att = att_weight_kernel(perm, normed1, cot, attended, grads)[0]
    weights = share_weights(env, [scatter(grad_att)], (0, cols, ff[0].shape[1]))
    weights += share_weights(env, [jnp.concatenate(ff, axis=1)], (0, ff[0].shape[1], 2 * ff[0].shape[1]))
    small = env["small_sums"](sums, biases[0] + biases[1], bias_fc1)
    parts = [(jnp.where(core == 0, totals[0][k], totals[1][k]), 0) for k in range(2)]
    return dict(parts=parts, small=sum_over(small, "dp", dp), weights=weights)


def share_weights(env, parts, cuts):
    mine, other = share_kernel(env["core_index"], parts)
    return list(columns_kernel(env["core_index"], mine, swap_core(other, env["dp"]), cuts))


def ring_flow(env):
    dp, ring, groups, chips = env["dp"], env["ring"], env["groups"], env["chips"]
    over_x, own_rows = env["over_x"], env["own_rows"]
    tokens, cotangent, pos = env["tokens"], env["cotangent"], env["positions_two"]
    sets = [[2 * k + c for k in range(chips)] for c in range(2)]
    half = own_rows // 2
    order = [Order(env["perm"]), Order(env["flip"])]

    def settle(rings, *values):
        lasts, values = tie([r.last for r in rings], list(values))
        marks = [x for x in jax.tree.leaves(values) if x.size <= 8 * LANES]
        order[:] = [Order(o.index, marks) for o in order]
        for r, last in zip(rings, lasts):
            r.last = last
            if isinstance(r, Gather):
                r.keep()
        return values

    weights_in = Gather(ring, env["in_rows"], 2)
    weights_out = Gather(ring, env["fc2_rows"], 1)

    tok_a = over_x(tokens[:half])
    tok_sib = swap_core(tokens, dp)
    weights_in.run()
    tok_a, tok_rest, pos = settle([weights_in], tok_a, tokens[half:], pos)
    tok_b = over_x(tok_rest)
    tok_a_sib = swap_core(tok_a, dp)
    weights_in.run()
    table = env["make_tables"](pos)
    tok_b, cot_first, _ = settle([weights_in], tok_b, cotangent[:half], table[:8])
    cot_a = over_x(cot_first)
    tok_b_sib = swap_core(tok_b, dp)
    weights_in.run()
    normed1, normed2, standard, mark = env["run_norm"](
        [(tokens, 0, 0), (tok_sib, 1, 0), (tok_a, 0, own_rows), (tok_b, 0, own_rows + half),
         (tok_a_sib, 1, own_rows), (tok_b_sib, 1, own_rows + half)], order[0],
    )
    cot_a, cot_rest, mark = settle([weights_in], cot_a, cotangent[half:], mark)
    cot_b = over_x(cot_rest)
    cot_a_sib = swap_core(cot_a, dp)
    cot_sib = swap_core(cotangent, dp)
    weights_in.run()
    cot_b, cot_a_sib, cot_sib = settle([weights_in], cot_b, cot_a_sib, cot_sib)
    wa, w1 = weights_in.result()
    cot_b_sib = swap_core(cot_b, dp)
    weights_out.run()
    qkv, mark = env["run_qkv"](normed1, table, wa, order[0])
    settle([weights_out], mark)
    weights_out.run()
    hidden, slope, mark = env["run_fc1"](normed2, w1, order[0])
    cot_b_sib, mark = settle([weights_out], cot_b_sib, mark)
    weights_out.run()
    cot, mark = env["run_turn"](
        [(cotangent, 0, 0), (cot_sib, 1, 0), (cot_a, 0, own_rows), (cot_b, 0, own_rows + half),
         (cot_a_sib, 1, own_rows), (cot_b_sib, 1, own_rows + half)], order[0],
    )
    settle([weights_out], mark)
    weights_out.run()
    att_grad, mark = env["run_att_grad"](cot, wa, order[0])

    def run_att(which, h):
        return env["run_attention"](qkv, att_grad, table, which, h, order[1])

    def run_tail(which, got):
        return env["run_tail"](
            which, hidden, pre_grad, standard, [x[0] for x in got], [x[1] for x in got], w1, w2, wa, order[0]
        )

    settle([weights_out], mark)
    (w2,) = weights_out.result()
    pre_grad, bias_fc1 = env["run_pre_grad"](cot, slope, w2, order[0])
    grad_fc2 = dot(cot, hidden, TN).astype(BF)
    grad_fc1 = dot(normed2, pre_grad, TN).astype(BF)
    grad_ff = reorder_kernel([grad_fc1, grad_fc2], order[0], chips, False)
    grad_ff, mark = settle([], grad_ff, bias_fc1)
    own_ff = lax.psum_scatter(grad_ff, "dp", scatter_dimension=0, tiled=True, axis_index_groups=sets)
    first = [run_att(0, h) for h in range(groups)]
    part0, *sums0 = run_tail(0, first)
    part0, mark = settle([], part0, sums0[0])
    sent0 = env["to_owner"](0, part0)
    second = [run_att(1, 0)]
    sent0, _ = settle([], sent0, second[0][2])
    out0, grad0 = pair_add_kernel(order[0], part0, sent0)
    out0 = env["reduce_x"](0, out0)
    second += [run_att(1, h) for h in range(1, groups)]
    out0, grad0, mark = settle([], out0, grad0, second[-1][2])
    grad0 = env["reduce_x"](0, grad0)
    part1, *sums1 = run_tail(1, second)
    grad0, part1, own_ff, mark = settle([], grad0, part1, own_ff, sums1[0])
    sent1 = env["to_owner"](1, part1)
    bias_qkv = jnp.concatenate([a[2] + b[2] for a, b in zip(first, second)], axis=1)
    small = env["small_sums"]([a + b for a, b in zip(sums0, sums1)], bias_qkv, bias_fc1)
    grad_att, mark = att_weight_kernel(
        order[0], normed1, cot, [x[0] for x in (*first, *second)], [x[1] for x in (*first, *second)]
    )
    sent1, mark, small = settle([], sent1, mark, small)
    scattered = Scatter(ring, [grad_att])
    scattered.run()
    steps = [1 << k for k in range(dp.bit_length() - 1)]
    if steps:
        small = sum_step(small, "dp", dp, steps.pop(0))
    out1, grad1 = pair_add_kernel(order[0], part1, sent1)
    out1, grad1, mark, small = settle([scattered], out1, grad1, mark, small)
    out1 = env["reduce_x"](1, out1)
    middle = chips // 2 - 2
    for i in range(middle):
        scattered.run()
        if steps:
            small = sum_step(small, "dp", dp, steps.pop(0))
        if i == 0:
            own = own_kernel(order[0], [(part0, sent0), (part1, sent1)])
        values = [small, own] + ([out1] if i == middle - 1 else [])
        small, own, *out1_now = settle([scattered], *values)
    (out1,) = out1_now
    grad1 = env["reduce_x"](1, grad1)
    scattered.run()
    if steps:
        small = sum_step(small, "dp", dp, steps.pop(0))
    (small,) = settle([scattered], small)
    wide, cols = env["hidden_cols"], env["qkv_cols"]
    for step in steps:
        small = sum_step(small, "dp", dp, step)
    weights = share_weights(env, scattered.result(), (0, cols, wide))
    weights += share_weights(env, [own_ff], (0, wide, 2 * wide))
    parts = [(x, 0) for x in (own[0], out0, out1, own[1], grad0, grad1)]
    return dict(parts=parts, small=small, weights=weights)


def solution(mesh):
    both, weight = P(("dp", "tensor"), None), P("dp", "tensor")
    return jax.shard_map(
        functools.partial(shards, mesh.shape["dp"], mesh.shape["tensor"]),
        mesh=mesh,
        in_specs=(both, P("dp"), both, weight, P("tensor"), weight, P(), weight, P("tensor"), weight, P(), P(), P(), P(), P()),
        out_specs=(both, both, weight, P("tensor"), weight, P(), weight, P("tensor"), weight, P(), P(), P(), P(), P()),
        check_vma=False,
    )
```

```python
import functools

import jax
import jax.numpy as jnp
from jax import lax
from jax.experimental import pallas as pl
from jax.experimental.pallas import tpu as pltpu
from jax.sharding import PartitionSpec as P

HEAD = 64
ROT = 16
SEQ_LEN = 1024
EPSILON = 1e-05
LANES = 128
BF = jnp.bfloat16
F32 = jnp.float32
NN = (((1,), (0,)), ((), ()))
NT = (((1,), (1,)), ((), ()))
TN = (((0,), (0,)), ((), ()))


def dot(first_op, second_op, dims=NN):
    return lax.dot_general(first_op, second_op, dims, preferred_element_type=F32)


class Order:
    def __init__(self, index, marks=()):
        self.index, self.marks = index, list(marks)
        self.shape = index.shape


def call(kernel, grid, in_specs, out_specs, out_shape, operands, flops, scratch=(), index=None, vmem=28):
    moved = sum(x.size * x.dtype.itemsize for x in operands)
    moved += sum(s.size * jnp.dtype(s.dtype).itemsize for s in out_shape)
    marks = []
    if isinstance(index, Order):
        index, marks = index.index, index.marks
    first, count = (0 if index is None else 1) + len(operands), len(marks)

    def body(*refs):
        kernel(*refs[:first], *refs[first + count :])

    return pl.pallas_call(
        body,
        grid_spec=pltpu.PrefetchScalarGridSpec(
            num_scalar_prefetch=0 if index is None else 1,
            grid=grid,
            in_specs=[*in_specs, *[pl.BlockSpec(memory_space=pl.ANY)] * count],
            out_specs=out_specs,
            scratch_shapes=list(scratch),
        ),
        out_shape=out_shape,
        compiler_params=pltpu.CompilerParams(vmem_limit_bytes=vmem * 2**20),
        cost_estimate=pl.CostEstimate(flops=flops, bytes_accessed=moved, transcendentals=0),
    )(*(() if index is None else (index,)), *operands, *marks)


def shape_of(rows, cols, kind=BF):
    return jax.ShapeDtypeStruct((rows, cols), kind)


def row_kernel(body, rows, block, row_ins, full_ins, row_outs, sum_outs, flops, index):
    steps = rows // block
    n_index = 1

    def at_row(first):
        return lambda step, *_: (step + first // block, 0)

    def at_zero(step, *_):
        return (0, 0)

    in_specs = [pl.BlockSpec((block, x.shape[1]), at_row(first)) for x, first in row_ins]
    in_specs += [pl.BlockSpec(x.shape, at_zero, pipeline_mode=pl.Buffered(1)) for x in full_ins]
    def out_spec(cols):
        if isinstance(cols, tuple):
            return pl.BlockSpec((cols[0], block, cols[1]), lambda step, *_: (0, step, 0))
        return pl.BlockSpec((block, cols), at_row(0))

    out_specs = [out_spec(cols) for cols, _ in row_outs]
    out_specs += [pl.BlockSpec((1, width), at_zero) for width in sum_outs]
    out_shape = [
        jax.ShapeDtypeStruct((cols[0], rows, cols[1]), kind) if isinstance(cols, tuple) else shape_of(rows, cols, kind)
        for cols, kind in row_outs
    ]
    out_shape += [shape_of(1, width, F32) for width in sum_outs]
    n_in, n_out = len(in_specs), len(row_outs)

    def kernel(*refs):
        ins = refs[: n_index + n_in]
        outs = refs[n_index + n_in : n_index + n_in + n_out]
        sums = refs[n_index + n_in + n_out :]
        if sums:

            @pl.when(pl.program_id(0) == 0)
            def _():
                for ref in sums:
                    ref[...] = jnp.zeros_like(ref)

        body(ins, outs, sums)

    operands = [x for x, _ in row_ins] + list(full_ins)
    return call(kernel, (steps,), in_specs, out_specs, out_shape, operands, flops, index=index)


def moments(vectors):
    row_mean = jnp.mean(vectors, axis=-1, keepdims=True)
    centered = vectors - row_mean
    spread = jnp.mean(centered * centered, axis=-1, keepdims=True)
    return centered, lax.rsqrt(spread + EPSILON)


def pieces_kernel(body, pieces, index, full_ins, row_outs, block):
    count = len(pieces)
    width = pieces[0][0].shape[1]
    rows = sum(x.shape[0] for x, _, _ in pieces)
    core_at = index.shape[0] - 1

    def slot(side, first, core):
        return (jnp.bitwise_xor(side, core) * (rows // 2) + first) // block

    def at_piece(x, side, first):
        return lambda step, idx: (jnp.clip(step - slot(side, first, idx[core_at]), 0, x.shape[0] // block - 1), 0)

    def kernel(idx, *refs):
        ins, fulls = refs[:count], refs[count : count + len(full_ins)]
        outs = refs[count + len(full_ins) : count + len(full_ins) + len(row_outs)]
        mark, scratch = refs[-2:]
        mark[...] = jnp.zeros_like(mark)
        step = pl.program_id(0)
        for ref, (x, side, first) in zip(ins, pieces):
            start = slot(side, first, idx[core_at])

            @pl.when((step >= start) & (step < start + x.shape[0] // block))
            def _(ref=ref):
                scratch[...] = ref[...].astype(F32)

        body(idx, fulls, outs, scratch)

    return call(
        kernel,
        (rows // block,),
        [pl.BlockSpec((block, width), at_piece(*p)) for p in pieces]
        + [pl.BlockSpec(x.shape, lambda step, _: (0, 0)) for x in full_ins],
        [pl.BlockSpec((block, width), lambda step, _: (step, 0)) for _ in row_outs]
        + [pl.BlockSpec((1, LANES), lambda step, _: (0, 0))],
        [*[shape_of(rows, width, kind) for kind in row_outs], shape_of(1, LANES, F32)],
        [*[x for x, _, _ in pieces], *full_ins],
        30 * rows * width,
        scratch=[pltpu.VMEM((block, width), F32)],
        index=index,
    )


def block_at(perm, place, width, count):
    if count == 1:
        return pl.ds(0, width)
    return pl.ds(pl.multiple_of(perm[place] * width, width), width)


def norm_body(count, perm, fulls, outs, scratch):
    gain_one, shift_one, gain_two, shift_two = fulls
    normed1, normed2, standard = outs
    centered, inverse = moments(scratch[...])
    scratch[...] = centered * inverse
    width = scratch.shape[1] // count
    for p in range(count):
        here = slice(p * width, (p + 1) * width)
        there = block_at(perm, p, width, count)
        part = scratch[:, there]
        normed1[:, here] = (part * gain_one[:, there] + shift_one[:, there]).astype(BF)
        normed2[:, here] = (part * gain_two[:, there] + shift_two[:, there]).astype(BF)
        standard[:, here] = part.astype(BF)


def turn_body(count, perm, fulls, outs, scratch):
    width = scratch.shape[1] // count
    for p in range(count):
        outs[0][:, p * width : (p + 1) * width] = scratch[:, block_at(perm, p, width, count)].astype(BF)


def lane_roll(x, shift):
    if x.shape[1] == LANES:
        return pltpu.roll(x, shift % LANES, 1)
    return jnp.roll(x, shift, axis=1)


def turned(x, table, sign):
    back = ROT // 2
    lane = lax.broadcasted_iota(jnp.int32, x.shape, 1) % HEAD
    sine = lane_roll(table, -ROT)
    moved = jnp.where(lane < back, -lane_roll(x, -back), lane_roll(x, back)) * sine
    total = x * table + moved if sign > 0 else x * table - moved
    return jnp.where(lane < ROT, total, x)


def by_kind(parts):
    if parts[0].shape[1] < LANES:
        return parts
    first, second, third = parts
    low = lax.broadcasted_iota(jnp.int32, first.shape, 1) < HEAD
    return (
        jnp.where(low, first, second),
        jnp.where(low, lane_roll(first, HEAD), lane_roll(third, HEAD)),
        jnp.where(low, second, third),
    )


def by_head(query, key, value):
    if query.shape[1] < LANES:
        return query, key, value
    low = lax.broadcasted_iota(jnp.int32, query.shape, 1) < HEAD
    swapped = lane_roll(key, HEAD)
    return jnp.where(low, query, swapped), jnp.where(low, value, query), jnp.where(low, swapped, value)


def qkv_body(groups, ins, outs, sums):
    _, normed, table, weight, bias = ins
    width = table.shape[1]
    for h in range(groups):
        cols = slice(3 * h * width, 3 * (h + 1) * width)
        mixed = dot(normed[...], weight[:, cols]) + bias[:, cols]
        query, key, value = by_kind([mixed[:, i * width : (i + 1) * width] for i in range(3)])
        outs[0][h] = turned(query, table[...], 1).astype(BF)
        outs[0][groups + h] = turned(key, table[...], 1).astype(BF)
        outs[0][2 * groups + h] = value.astype(BF)


def fc1_body(ins, outs, sums):
    _, normed, weight, bias = ins
    cols = weight.shape[1]
    step = min(256, cols)
    for j in range(cols // step):
        here = slice(j * step, (j + 1) * step)
        pre = dot(normed[...], weight[:, here]) + bias[:, here]
        phi = 0.5 * (1.0 + lax.erf(pre * 0.7071067811865476))
        outs[0][:, here] = (pre * phi).astype(BF)
        outs[1][:, here] = (phi + pre * jnp.exp(-0.5 * pre * pre) * 0.3989422804014327).astype(BF)


def pre_grad_body(ins, outs, sums):
    _, cot, slope, weight = ins
    grad = (dot(cot[...], weight[...]) * slope[...].astype(F32)).astype(BF)
    outs[0][...] = grad
    sums[0][...] += jnp.sum(grad.astype(F32), axis=0, keepdims=True)


def att_grad_body(cols, ins, outs, sums):
    _, cot, w_att = ins
    grad = dot(cot[...], w_att[:, cols:]).astype(BF)
    groups, _, width = outs[0].shape
    for h in range(groups):
        outs[0][h] = grad[:, h * width : (h + 1) * width]


def tail_body(groups, count, ins, outs, sums):
    perm, hidden, pre_grad, standard = ins[:4]
    attended, grads = ins[4 : 4 + groups], ins[4 + groups : 4 + 2 * groups]
    w1, w2, wa, gain_one, gain_two = ins[4 + 2 * groups :]
    dense = groups * grads[0].shape[1]
    att = jnp.concatenate([x[...] for x in attended], axis=1)
    grad = jnp.concatenate([x[...] for x in grads], axis=1)
    width = standard.shape[1] // count
    step = min(256, standard.shape[1])
    for j in range(standard.shape[1] // step):
        cols = slice(j * step, (j + 1) * step)
        total = dot(hidden[...], w2[cols, :], NT) + dot(att, wa[cols, dense:], NT)
        outs[0][0, :, cols] = total.astype(BF)
        two = dot(pre_grad[...], w1[cols, :], NT)
        one = dot(grad, wa[cols, :dense], NT)
        std = standard[:, cols].astype(F32)
        values = (one * std, one, two * std, two)
        values = [jnp.sum(v, axis=0, keepdims=True) for v in values]
        if count == 1:
            for ref, value in zip(sums, values):
                ref[:, cols] += value
            outs[0][1, :, cols] = (one * gain_one[:, cols] + two * gain_two[:, cols]).astype(BF)
            continue
        for k in range(step // width):
            there = block_at(perm, j * (step // width) + k, width, count)
            part = slice(k * width, (k + 1) * width)
            for ref, value in zip(sums, values):
                ref[:, there] += value[:, part]
            scaled = one[:, part] * gain_one[:, there] + two[:, part] * gain_two[:, there]
            outs[0][1, :, j * step + k * width : j * step + (k + 1) * width] = scaled.astype(BF)


def att_weight_body(groups, rows, _, *refs):
    normed, cot = refs[:2]
    attended, grads = refs[2 : 2 + 2 * groups], refs[2 + 2 * groups : 2 + 4 * groups]
    out, mark, joined = refs[-3:]
    mark[...] = jnp.zeros_like(mark)
    width, wide = attended[0].shape[1], grads[0].shape[1]
    dense = groups * wide

    @pl.when(pl.program_id(0) == 0)
    def _():
        for which in range(2):
            here = slice(which * rows, (which + 1) * rows)
            for h in range(groups):
                joined[here, h * wide : (h + 1) * wide] = grads[which * groups + h][...]
                joined[here, dense + h * width : dense + (h + 1) * width] = attended[which * groups + h][...]

    out[:, :dense] = dot(normed[...], joined[:, :dense], TN).astype(BF)
    out[:, dense:] = dot(cot[...], joined[:, dense:], TN).astype(BF)


def att_weight_kernel(index, normed, cot, attended, grads):
    groups = len(attended) // 2
    rows, depth = normed.shape
    cols = sum(x.shape[1] for x in (*attended[:groups], *grads[:groups]))
    step = min(256, depth)

    def whole(x):
        return pl.BlockSpec(x.shape, lambda i, _: (0, 0), pipeline_mode=pl.Buffered(1))

    return call(
        functools.partial(att_weight_body, groups, rows // 2),
        (depth // step,),
        [pl.BlockSpec((rows, step), lambda i, _: (0, i))] * 2 + [whole(x) for x in (*attended, *grads)],
        [pl.BlockSpec((step, cols), lambda i, _: (i, 0)), pl.BlockSpec((1, LANES), lambda i, _: (0, 0))],
        [shape_of(depth, cols), shape_of(1, LANES, F32)],
        [normed, cot, *attended, *grads],
        2 * rows * depth * cols,
        scratch=[pltpu.VMEM((rows, cols), BF)],
        index=index,
        vmem=56,
    )


def attention_kernel(flip, q_ref, k_ref, v_ref, g_ref, table_ref, att_ref, out_ref, sum_ref, keys, values, q_acc, key_acc, value_acc):
    _, _, halves, length, width = q_ref.shape
    per = width // HEAD
    block = min(256, length)

    def place(half):
        return half if halves == 1 else jnp.bitwise_xor(half, flip[0])

    @pl.when(pl.program_id(0) == 0)
    def _():
        sum_ref[...] = jnp.zeros_like(sum_ref)

    for half in range(halves):
        rows = slice(half * length, (half + 1) * length)
        keys[rows, :] = k_ref[0, 0, place(half)]
        values[rows, :] = v_ref[0, 0, place(half)]
    key_acc[...] = jnp.zeros_like(key_acc)
    value_acc[...] = jnp.zeros_like(value_acc)
    lane = lax.broadcasted_iota(jnp.int32, (block, width), 1)
    scale = HEAD ** (-0.5)

    for i in range(halves * length // block):
        half, offset = i * block // length, i * block % length
        here = pl.ds(offset, block)
        extent = (i + 1) * block
        q_all = q_ref[0, 0, place(half), here, :]
        g_all = g_ref[0, 0, place(half), here, :]
        key_rows = keys[:extent, :]
        value_rows = values[:extent, :]
        causal = (
            lax.broadcasted_iota(jnp.int32, (block, extent), 0) + i * block
            >= lax.broadcasted_iota(jnp.int32, (block, extent), 1)
        )
        att_total = jnp.zeros((block, width), F32)
        query_total = jnp.zeros((block, width), F32)
        for h in range(per):
            mine = (lane >= h * HEAD) & (lane < (h + 1) * HEAD)
            q = jnp.where(mine, q_all.astype(F32) * scale, 0.0).astype(BF)
            g = jnp.where(mine, g_all.astype(F32), 0.0).astype(BF)
            scores = jnp.where(causal, dot(q, key_rows, NT), -1e30)
            expon = jnp.exp(scores - jnp.max(scores, axis=-1, keepdims=True))
            probs = expon * (1.0 / jnp.sum(expon, axis=-1, keepdims=True))
            low = probs.astype(BF)
            result = jnp.where(mine, dot(low, value_rows), 0.0)
            prob_grad = dot(g, value_rows, NT)
            row_dot = jnp.sum(result * g.astype(F32), axis=-1, keepdims=True)
            score_grad = (probs * (prob_grad - row_dot)).astype(BF)
            att_total += result
            query_total += jnp.where(mine, dot(score_grad, key_rows), 0.0)
            key_acc[:extent, :] += dot(score_grad, q, TN)
            value_acc[:extent, :] += dot(low, g, TN)
        att_ref[0, place(half), here, :] = att_total.astype(BF)
        q_acc[i * block : (i + 1) * block, :] = query_total
    for half in range(halves):
        rows = slice(half * length, (half + 1) * length)
        table = table_ref[0, place(half)]
        query = turned(q_acc[rows, :] * scale, table, -1)
        key = turned(key_acc[rows, :], table, -1)
        for j, part in enumerate(by_head(query, key, value_acc[rows, :])):
            part = part.astype(BF)
            out_ref[0, place(half), :, j * width : (j + 1) * width] = part
            sum_ref[:, j * width : (j + 1) * width] += jnp.sum(part.astype(F32), axis=0, keepdims=True)


def attention(qkv, grad, table, flip, halves, which, group):
    groups, total, width = grad.shape
    length = SEQ_LEN // halves
    seqs = total // SEQ_LEN
    own = seqs // 2

    def split(x):
        return x.reshape(*x.shape[:-2], seqs, halves, length, width)

    def spec(at):
        return pl.BlockSpec((1, 1, halves, length, width), lambda s, _: (at, which * own + s, 0, 0, 0))

    def out_spec(cols):
        return pl.BlockSpec((1, halves, length, cols), lambda s, _: (s, 0, 0, 0))

    acc = pltpu.VMEM((SEQ_LEN, width), F32)
    low = pltpu.VMEM((SEQ_LEN, width), BF)
    att, out, sums = call(
        attention_kernel,
        (own,),
        [*[spec(base * groups + group) for base in range(3)], spec(group)]
        + [pl.BlockSpec((1, halves, length, width), lambda s, _: (which * own + s, 0, 0, 0))],
        [out_spec(width), out_spec(3 * width), pl.BlockSpec((1, 3 * width), lambda s, _: (0, 0))],
        [
            jax.ShapeDtypeStruct((own, halves, length, width), BF),
            jax.ShapeDtypeStruct((own, halves, length, 3 * width), BF),
            shape_of(1, 3 * width, F32),
        ],
        [split(qkv)] * 3 + [split(grad), split(table)],
        own * (width // HEAD) * 12 * SEQ_LEN * SEQ_LEN * 256 * 5 // 8,
        scratch=[low, low, acc, acc, acc],
        index=flip,
    )
    return att.reshape(-1, width), out.reshape(-1, 3 * width), sums


def table_kernel(positions, flip, halves, repeat):
    rows = positions.shape[1]
    width, half_rot = repeat * HEAD, ROT // 2
    length = SEQ_LEN // halves

    def kernel(flip_ref, pos_ref, out):
        index = lax.broadcasted_iota(jnp.int32, (half_rot, 1), 0).astype(F32)
        frequencies = jnp.exp(index * (-9.210340371976184 / half_rot))
        frequencies = jnp.where(index == 0.0, 1.0, frequencies)
        angles = frequencies * pos_ref[...].astype(F32)
        lane = lax.broadcasted_iota(jnp.int32, (half_rot, width), 1) % HEAD
        place = lax.broadcasted_iota(jnp.int32, (half_rot, width), 0)
        first = ((lane == place) | (lane == place + half_rot)).astype(F32)
        second = ((lane == place + ROT) | (lane == place + ROT + half_rot)).astype(F32)

        def spread(x, y):
            return lax.dot_general(x, y, TN, precision=lax.Precision.HIGHEST, preferred_element_type=F32)

        table = spread(jnp.cos(angles), first) + spread(jnp.sin(angles), second)
        for f in range(halves):

            @pl.when(flip_ref[0] == f)
            def _(f=f):
                for start in range(0, rows, SEQ_LEN):
                    for half in range(halves):
                        there = start + (half ^ f) * length
                        here = start + half * length
                        out[there : there + length, :] = table[here : here + length, :]

    return one_step(kernel, [positions], [shape_of(rows, width, F32)], index=flip)[0]


def final_body(count, n_parts, ins, outs, sums):
    perm, tokens, cot = ins[:3]
    parts, bias = ins[3:-1], ins[-1]
    width = tokens.shape[1] // count

    def total(refs):
        value = refs[0][...].astype(F32)
        for ref in refs[1:]:
            value = value + ref[...].astype(F32)
        return value

    out_total, grad_total = total(parts[:n_parts]), total(parts[n_parts:])
    scratch = outs[2]
    for p in range(count):
        there = block_at(perm, p, width, count)
        here = slice(p * width, (p + 1) * width)
        scratch[:, there] = grad_total[:, here]
        outs[0][:, there] = (tokens[:, there].astype(F32) + out_total[:, here] + bias[:, there]).astype(BF)
    grad = scratch[...]
    centered, inverse = moments(tokens[...].astype(F32))
    standard = centered * inverse
    through = inverse * (
        grad
        - jnp.mean(grad, axis=-1, keepdims=True)
        - standard * jnp.mean(grad * standard, axis=-1, keepdims=True)
    )
    outs[1][...] = (cot[...].astype(F32) + through).astype(BF)


def pair_add_kernel(index, part, got):
    _, rows, width = part.shape
    rows //= 2
    block = min(256, rows)
    per = rows // block

    def kernel(_, part_ref, got_ref, *outs):
        for k in range(2):
            outs[k][...] = (part_ref[k].astype(F32) + got_ref[k].astype(F32)).astype(BF)

    high = pl.BlockSpec((2, block, width), lambda i, _: (0, i + per, 0))
    other = pl.BlockSpec((block, width), lambda i, _: (i, 0))
    return call(
        kernel, (per,), [high, high], [other, other], [shape_of(rows, width)] * 2, [part, got], 2 * rows * width,
        index=index,
    )


def own_kernel(index, pairs):
    _, rows, width = pairs[0][0].shape
    rows //= 2
    block = min(256, rows)

    def kernel(idx, *refs):
        zero, one = (refs[2 * i][...].astype(F32) + refs[2 * i + 1][...].astype(F32) for i in range(2))
        total = jnp.where(idx[idx.shape[0] - 1] == 0, zero, one).astype(BF)
        refs[-2][...], refs[-1][...] = total[0], total[1]

    low = pl.BlockSpec((2, block, width), lambda i, _: (0, i, 0))
    own = pl.BlockSpec((block, width), lambda i, _: (i, 0))
    operands = [x for pair in pairs for x in pair]
    return call(
        kernel, (rows // block,), [low] * 4, [own] * 2, [shape_of(rows, width)] * 2, operands, 6 * rows * width,
        index=index,
    )


def one_step(kernel, operands, shapes, index=None):
    def whole(shape):
        return pl.BlockSpec(shape, lambda i, *_: (0,) * len(shape))

    return call(
        kernel, (1,), [whole(x.shape) for x in operands], [whole(s.shape) for s in shapes], shapes, operands, 0,
        index=index, vmem=40,
    )


def split_kernel(core, weights):
    w_qkv, w_dense, w_fc1, w_fc2 = weights
    rows = w_qkv.shape[0]
    cols = [w.shape[1] // 2 for w in weights]

    def kernel(core_ref, qkv, dense, fc1, fc2, *outs):
        for c in range(2):

            @pl.when(core_ref[0] == c)
            def _(c=c):
                for out, k in zip(outs, (c, 1 - c)):
                    out[:rows, : cols[0]] = qkv[:, k * cols[0] : (k + 1) * cols[0]]
                    out[:rows, cols[0] :] = dense[:, k * cols[1] : (k + 1) * cols[1]]
                    out[rows : 2 * rows, :] = fc1[:, k * cols[2] : (k + 1) * cols[2]]
                    out[2 * rows :, :] = fc2[:, k * cols[3] : (k + 1) * cols[3]]

    return one_step(kernel, list(weights), [shape_of(3 * rows, cols[2])] * 2, index=core)


def place_kernel(core, mine, other):
    rows = mine.shape[0] // 3

    def kernel(core_ref, a, b, first, second):
        for c in range(2):

            @pl.when(core_ref[0] == c)
            def _(c=c):
                for ref, k in ((a, c), (b, 1 - c)):
                    first[k * rows : (k + 1) * rows, :] = ref[:rows, :]
                    first[(2 + k) * rows : (3 + k) * rows, :] = ref[rows : 2 * rows, :]
                    second[k * rows : (k + 1) * rows, :] = ref[2 * rows :, :]

    cols = mine.shape[1]
    return one_step(kernel, [mine, other], [shape_of(4 * rows, cols), shape_of(2 * rows, cols)], index=core)


def join_kernel(blocks, stack):
    rows = blocks[0].shape[0] // stack
    whole = sum(b.shape[0] for b in blocks) // stack

    def kernel(*refs):
        outs = refs[-stack:]
        first, filled = 0, 0
        for ref in refs[:-stack]:
            if ref.shape[0] == stack * rows:
                for k in range(stack):
                    outs[k][first : first + rows, :] = ref[k * rows : (k + 1) * rows, :]
                first += rows
                continue
            got = ref.shape[0]
            place = first + (filled % rows)
            outs[filled // rows][place : place + got, :] = ref[...]
            filled += got
            if filled == stack * rows:
                first += rows

    return one_step(kernel, blocks, [shape_of(whole, blocks[0].shape[1])] * stack)


def reorder_kernel(arrays, perm, count, gather):
    rows, cols = arrays[0].shape
    block = rows // count
    wide = cols * len(arrays)

    def kernel(_, *refs):
        for i, ref in enumerate(refs[:-1]):
            refs[-1][:, i * cols : (i + 1) * cols] = ref[...]

    def moved(p, perm_ref):
        return (perm_ref[p], 0)

    def plain(p, _):
        return (p, 0)

    return call(
        kernel,
        (count,),
        [pl.BlockSpec((block, cols), moved if gather else plain)] * len(arrays),
        [pl.BlockSpec((block, wide), plain if gather else moved)],
        [shape_of(rows, wide)],
        arrays,
        0,
        index=perm,
    )[0]


def share_kernel(core, parts):
    rows = parts[0].shape[0] // 2

    def kernel(core_ref, *refs):
        for c in range(2):

            @pl.when(core_ref[0] == c)
            def _(c=c):
                for out, k in zip(refs[-2:], (c, 1 - c)):
                    here = slice(k * rows, (k + 1) * rows)
                    total = refs[0][here, :].astype(F32)
                    for ref in refs[1:-2]:
                        total = total + ref[here, :].astype(F32)
                    out[...] = total

    return one_step(kernel, list(parts), [shape_of(rows, parts[0].shape[1], F32)] * 2, index=core)


def columns_kernel(core, mine, other, cuts):
    rows = mine.shape[0]

    def kernel(core_ref, a, b, *outs):
        for c in range(2):

            @pl.when(core_ref[0] == c)
            def _(c=c):
                for out, low, high in zip(outs, cuts, cuts[1:]):
                    cols = high - low
                    out[:, c * cols : (c + 1) * cols] = a[:, low:high]
                    out[:, (1 - c) * cols : (2 - c) * cols] = b[:, low:high]

    shapes = [shape_of(rows, 2 * (high - low), F32) for low, high in zip(cuts, cuts[1:])]
    return one_step(kernel, [mine, other], shapes, index=core)


def add_kernel(grads, chips, places, received, spans):
    block = grads[0].shape[0] // chips
    cols = grads[0].shape[1]
    count = len(grads)

    def whole(shape):
        return pl.BlockSpec(shape, lambda i: (0, 0))

    def kernel(*refs):
        for way in range(2):
            ins = refs[way * count : (way + 1) * count]
            out = refs[-2 + way]
            low, high = spans[way]
            for i in range(count):
                if received is None:
                    size = high - low
                    out[i * size : (i + 1) * size, :] = ins[i][low:high, :]
                    continue
                got = refs[2 * count + way]
                size = high - low
                first = i * block
                if low:
                    out[first : first + low, :] = ins[i][:low, :]
                if high < block:
                    out[first + high : first + block, :] = ins[i][high:, :]
                total = ins[i][low:high, :].astype(F32) + got[i * size : (i + 1) * size, :].astype(F32)
                out[first + low : first + high, :] = total.astype(BF)

    specs = [
        pl.BlockSpec((block, cols), functools.partial(lambda place, i: (place, 0), places[way]))
        for way in range(2)
        for _ in range(count)
    ]
    operands = [*grads, *grads]
    out_rows = [count * block] * 2
    if received is None:
        out_rows = [count * (high - low) for low, high in spans]
    else:
        specs += [whole(x.shape) for x in received]
        operands += list(received)
    return call(
        kernel, (1,), specs, [whole((r, cols)) for r in out_rows], [shape_of(r, cols) for r in out_rows], operands, 0
    )


def swap_core(x, size):
    return lax.ppermute(x, "dp", [(i, i ^ 1) for i in range(size)])


def tie(*trees):
    return lax.optimization_barrier(trees)


def sum_step(x, axis, size, step):
    return x + lax.ppermute(x, axis, [(i, i ^ step) for i in range(size)])


def sum_over(x, axis, size):
    if size & (size - 1):
        return lax.psum(x, axis)
    step = 1
    while step < size:
        x = sum_step(x, axis, size, step)
        step *= 2
    return x


class Ring:
    def __init__(self, chips):
        self.chips = chips
        order = [2 * i for i in range(chips // 2)] + [2 * i + 1 for i in reversed(range(chips // 2))]
        self.order = order
        places = [0] * chips
        for place, chip in enumerate(order):
            places[chip] = place
        mine = jnp.asarray(places, jnp.int32)[lax.axis_index("dp") // 2]
        self.perm = jnp.asarray(order, jnp.int32)[(mine + jnp.arange(chips)) % chips]
        self.inverse = (jnp.asarray(places, jnp.int32) - mine) % chips

    def send(self, x, step):
        pairs = []
        for place, chip in enumerate(self.order):
            other = self.order[(place + step) % self.chips]
            pairs += [(2 * chip + c, 2 * other + c) for c in range(2)]
        return lax.ppermute(x, "dp", pairs)


class Gather:
    def __init__(self, ring, x, stack):
        self.ring, self.step, self.last, self.stack = ring, 0, (x, x), stack
        self.blocks = [x] + [None] * (ring.chips - 1)

    def run(self):
        self.step += 1
        up, down = self.last
        if self.step == self.ring.chips // 2:
            half = up.shape[0] // 2
            up, down = up[:half], down[half:]
        self.last = (self.ring.send(up, 1), self.ring.send(down, -1))

    def keep(self):
        up, down = self.last
        if self.step == self.ring.chips // 2:
            self.middle = [up, down]
        else:
            self.blocks[self.ring.chips - self.step], self.blocks[self.step] = up, down

    def result(self):
        middle = self.ring.chips // 2
        return join_kernel([*self.blocks[:middle], *self.middle, *self.blocks[middle + 1 :]], self.stack)


class Scatter:
    def __init__(self, ring, grads):
        self.ring, self.grads, self.step, self.last = ring, grads, 0, None

    def run(self):
        chips = self.ring.chips
        middle, block = chips // 2, self.grads[0].shape[0] // chips
        places = (middle - self.step, middle + self.step)
        if self.step < 2:
            spans = ((0, block // 2), (block // 2, block))
        else:
            spans = ((0, block), (0, block))
        up, down = add_kernel(self.grads, chips, places, self.last, spans)
        self.step += 1
        self.last = (self.ring.send(up, 1), self.ring.send(down, -1))

    def result(self):
        rows = self.grads[0].shape[0] // self.ring.chips
        return [self.grads[0][:rows], *self.last]


def shards(dp, tensor, *arrays):
    tokens, positions, cotangent, w_qkv, b_qkv, w_dense, b_dense, w_fc1, b_fc1, w_fc2, b_fc2 = arrays[:11]
    norm1_gain, norm1_shift, norm2_gain, norm2_shift = arrays[11:]
    core = lax.axis_index("dp") % 2
    own_rows, width = tokens.shape
    row_share = w_qkv.shape[0]
    heads = w_qkv.shape[1] // (3 * HEAD) // 2
    qkv_cols, dense_cols = 3 * heads * HEAD, heads * HEAD
    groups = heads // 2 if heads % 2 == 0 else heads
    chips = dp // 2
    ringed = chips % 2 == 0 and chips >= 4 and (2 * row_share) % LANES == 0 and chips * 2 * row_share == width
    halves = 2 if tensor == 2 and 2 * own_rows == SEQ_LEN else 1
    core_index = core.astype(jnp.int32).reshape(1)
    block, row_block = 256, 512

    if ringed:
        ring = Ring(chips)
        count = chips
        perm = jnp.concatenate([ring.perm, core_index])
    else:
        count = 1
        perm = jnp.concatenate([jnp.zeros((1,), jnp.int32), core_index])

    def over_x(x):
        return lax.ppermute(x, "tensor", [(0, 1), (1, 0)])

    flip = (lax.axis_index("tensor") if halves == 2 else jnp.int32(0)).astype(jnp.int32).reshape(1)

    def make_tables(both):
        repeat = 2 if heads % 2 == 0 else 1
        return table_kernel(both, flip, halves, repeat)

    gains = tuple(v.reshape(1, width) for v in (norm1_gain, norm1_shift, norm2_gain, norm2_shift))
    gain_one, _, gain_two, _ = gains
    hidden_cols = w_fc1.shape[1] // 2
    b1 = lax.dynamic_slice(b_fc1, (core * hidden_cols,), (hidden_cols,)).reshape(1, hidden_cols)
    bq = lax.dynamic_slice(b_qkv, (core * qkv_cols,), (qkv_cols,)).reshape(1, qkv_cols)
    rows = 2 * own_rows * tensor
    group_rows = rows // 2
    work = 2 * rows * width * hidden_cols

    mine, other = split_kernel(core_index, (w_qkv, w_dense, w_fc1, w_fc2))
    in_rows, fc2_rows = place_kernel(core_index, mine, swap_core(other, dp))
    pos = positions.reshape(1, -1)
    other = swap_core(pos, dp)
    positions_two = jnp.where(
        core == 0, jnp.concatenate([pos, other], axis=1), jnp.concatenate([other, pos], axis=1)
    )

    def run_norm(pieces, order=perm):
        return pieces_kernel(functools.partial(norm_body, count), pieces, order, gains, (BF, BF, BF), block)

    def run_turn(pieces, order=perm):
        return pieces_kernel(functools.partial(turn_body, count), pieces, order, (), (BF,), block)

    def run_qkv(normed1, table, wa, order=perm):
        return row_kernel(
            functools.partial(qkv_body, groups), rows, row_block, [(normed1, 0), (table, 0)], (wa, bq),
            (((3 * groups, dense_cols // groups), BF),), (LANES,), 2 * rows * width * qkv_cols, order,
        )

    def run_fc1(normed2, w1, order=perm):
        return row_kernel(
            fc1_body, rows, row_block, [(normed2, 0)], (w1, b1), ((hidden_cols, BF), (hidden_cols, BF)), (LANES,), work, order
        )

    def run_att_grad(cot, wa, order=perm):
        return row_kernel(
            functools.partial(att_grad_body, qkv_cols), rows, row_block, [(cot, 0)], (wa,), (((groups, dense_cols // groups), BF),), (LANES,),
            2 * rows * width * dense_cols, order,
        )

    def run_pre_grad(cot, slope, w2, order=perm):
        return row_kernel(
            pre_grad_body, rows, row_block, [(cot, 0), (slope, 0)], (w2,), ((hidden_cols, BF),), (hidden_cols,), work, order
        )

    def run_tail(which, hidden, pre_grad, standard, attended, grads, w1, w2, wa, order=perm):
        first = which * group_rows
        return row_kernel(
            functools.partial(tail_body, groups, count), group_rows, row_block,
            [(hidden, first), (pre_grad, first), (standard, first), *[(x, 0) for x in (*attended, *grads)]],
            (w1, w2, wa, gain_one, gain_two), (((2, width), BF),), (width,) * 4,
            work + group_rows * width * (qkv_cols + dense_cols) * 2, order,
        )

    def run_attention(qkv, att_grad, table, which, group, order=flip):
        return attention(qkv, att_grad, table, order, halves, which, group)

    def to_owner(which, part):
        return lax.ppermute(part, "dp", [(2 * k + 1 - which, 2 * k + which) for k in range(chips)])

    out_bias = jnp.sum(cotangent.astype(F32), axis=0, keepdims=True)

    def small_sums(sums, bias_qkv, bias_fc1):
        wide = jnp.concatenate([*sums, out_bias], axis=1)
        wide = sum_over(wide, "tensor", tensor)
        narrow = jnp.concatenate([bias_qkv, bias_fc1], axis=1)
        zero = jnp.zeros_like(narrow)
        return jnp.concatenate([wide, jnp.where(core == 0, narrow, zero), jnp.where(core == 0, zero, narrow)], axis=1)

    def reduce_x(which, other):
        pairs = [(2 * i + x, 2 * i + 1 - x) for i in range(which, dp, 2) for x in range(2)]
        return lax.ppermute(other, ("dp", "tensor"), pairs)

    if ringed and halves == 2:
        flow = ring_flow
    else:
        flow = plain_flow
    env = dict(locals())
    results = flow(env)
    final_block = min(256, own_rows)
    parts = results["parts"]
    output, grad_tokens, _ = row_kernel(
        functools.partial(final_body, count, len(parts) // 2), own_rows, final_block,
        [(tokens, 0), (cotangent, 0), *parts],
        ((b_dense + b_fc2).reshape(1, width),), ((width, BF), (width, BF), (width, F32)), (), 0, perm,
    )

    small = results["small"]
    wide, first, second = jnp.split(small[0], [5 * width, 5 * width + qkv_cols + hidden_cols])
    wide = wide.reshape(5, width)
    bias_qkv = jnp.concatenate([first[:qkv_cols], second[:qkv_cols]])
    bias_fc1 = jnp.concatenate([first[qkv_cols:], second[qkv_cols:]])
    grad_w_qkv, grad_w_dense, grad_w_fc1, grad_w_fc2 = results["weights"]
    return (
        output, grad_tokens, grad_w_qkv, bias_qkv, grad_w_dense, wide[4], grad_w_fc1, bias_fc1, grad_w_fc2, wide[4],
        wide[0], wide[1], wide[2], wide[3],
    )


def plain_flow(env):
    dp, chips, groups = env["dp"], env["chips"], env["groups"]
    core, perm = env["core"], env["perm"]
    sets = [[2 * k + c for k in range(chips)] for c in range(2)]

    def gather(x):
        return lax.all_gather(x, "dp", axis=0, tiled=True, axis_index_groups=sets)

    def scatter(x):
        return lax.psum_scatter(x, "dp", scatter_dimension=0, tiled=True, axis_index_groups=sets)

    def pieces(x):
        x = lax.all_gather(x, "tensor", axis=0, tiled=True)
        return [(x, 0, 0), (swap_core(x, dp), 1, 0)]

    half = env["in_rows"].shape[0] // 2
    wa, w1, w2 = gather(env["in_rows"][:half]), gather(env["in_rows"][half:]), gather(env["fc2_rows"])
    table = env["make_tables"](env["positions_two"])
    normed1, normed2, standard, _ = env["run_norm"](pieces(env["tokens"]))
    cot, _ = env["run_turn"](pieces(env["cotangent"]))
    hidden, slope, _ = env["run_fc1"](normed2, w1)
    pre_grad, bias_fc1 = env["run_pre_grad"](cot, slope, w2)
    qkv, _ = env["run_qkv"](normed1, table, wa)
    att_grad, _ = env["run_att_grad"](cot, wa)
    attended, grads, sums, totals, biases = [], [], [0.0] * 4, [], []
    for which in range(2):
        got = [env["run_attention"](qkv, att_grad, table, which, h) for h in range(groups)]
        attended += [x[0] for x in got]
        grads += [x[1] for x in got]
        biases.append(jnp.concatenate([x[2] for x in got], axis=1))
        part, *some = env["run_tail"](
            which, hidden, pre_grad, standard, attended[-groups:], grads[-groups:], w1, w2, wa
        )
        sums = [a + b for a, b in zip(sums, some)]
        part = part + env["to_owner"](which, part)
        totals.append([lax.psum_scatter(part[k], "tensor", scatter_dimension=0, tiled=True) for k in range(2)])
    cols = env["qkv_cols"]
    ff = [scatter(x) for x in (dot(normed2, pre_grad, TN).astype(BF), dot(cot, hidden, TN).astype(BF))]
    grad_att = att_weight_kernel(perm, normed1, cot, attended, grads)[0]
    weights = share_weights(env, [scatter(grad_att)], (0, cols, ff[0].shape[1]))
    weights += share_weights(env, [jnp.concatenate(ff, axis=1)], (0, ff[0].shape[1], 2 * ff[0].shape[1]))
    small = env["small_sums"](sums, biases[0] + biases[1], bias_fc1)
    parts = [(jnp.where(core == 0, totals[0][k], totals[1][k]), 0) for k in range(2)]
    return dict(parts=parts, small=sum_over(small, "dp", dp), weights=weights)


def share_weights(env, parts, cuts):
    mine, other = share_kernel(env["core_index"], parts)
    return list(columns_kernel(env["core_index"], mine, swap_core(other, env["dp"]), cuts))


def ring_flow(env):
    dp, ring, groups, chips = env["dp"], env["ring"], env["groups"], env["chips"]
    over_x, own_rows = env["over_x"], env["own_rows"]
    tokens, cotangent, pos = env["tokens"], env["cotangent"], env["positions_two"]
    sets = [[2 * k + c for k in range(chips)] for c in range(2)]
    half = own_rows // 2
    order = [Order(env["perm"]), Order(env["flip"])]

    def settle(rings, *values):
        lasts, values = tie([r.last for r in rings], list(values))
        marks = [x for x in jax.tree.leaves(values) if x.size <= 8 * LANES]
        order[:] = [Order(o.index, marks) for o in order]
        for r, last in zip(rings, lasts):
            r.last = last
            if isinstance(r, Gather):
                r.keep()
        return values

    weights_in = Gather(ring, env["in_rows"], 2)
    weights_out = Gather(ring, env["fc2_rows"], 1)

    tok_a = over_x(tokens[:half])
    tok_sib = swap_core(tokens, dp)
    weights_in.run()
    tok_a, tok_rest, pos = settle([weights_in], tok_a, tokens[half:], pos)
    tok_b = over_x(tok_rest)
    tok_a_sib = swap_core(tok_a, dp)
    weights_in.run()
    table = env["make_tables"](pos)
    tok_b, cot_first, _ = settle([weights_in], tok_b, cotangent[:half], table[:8])
    cot_a = over_x(cot_first)
    tok_b_sib = swap_core(tok_b, dp)
    weights_in.run()
    normed1, normed2, standard, mark = env["run_norm"](
        [(tokens, 0, 0), (tok_sib, 1, 0), (tok_a, 0, own_rows), (tok_b, 0, own_rows + half),
         (tok_a_sib, 1, own_rows), (tok_b_sib, 1, own_rows + half)], order[0],
    )
    cot_a, cot_rest, mark = settle([weights_in], cot_a, cotangent[half:], mark)
    cot_b = over_x(cot_rest)
    cot_a_sib = swap_core(cot_a, dp)
    cot_sib = swap_core(cotangent, dp)
    weights_in.run()
    cot_b, cot_a_sib, cot_sib = settle([weights_in], cot_b, cot_a_sib, cot_sib)
    wa, w1 = weights_in.result()
    cot_b_sib = swap_core(cot_b, dp)
    weights_out.run()
    qkv, mark = env["run_qkv"](normed1, table, wa, order[0])
    settle([weights_out], mark)
    weights_out.run()
    hidden, slope, mark = env["run_fc1"](normed2, w1, order[0])
    cot_b_sib, mark = settle([weights_out], cot_b_sib, mark)
    weights_out.run()
    cot, mark = env["run_turn"](
        [(cotangent, 0, 0), (cot_sib, 1, 0), (cot_a, 0, own_rows), (cot_b, 0, own_rows + half),
         (cot_a_sib, 1, own_rows), (cot_b_sib, 1, own_rows + half)], order[0],
    )
    settle([weights_out], mark)
    weights_out.run()
    att_grad, mark = env["run_att_grad"](cot, wa, order[0])

    def run_att(which, h):
        return env["run_attention"](qkv, att_grad, table, which, h, order[1])

    def run_tail(which, got):
        return env["run_tail"](
            which, hidden, pre_grad, standard, [x[0] for x in got], [x[1] for x in got], w1, w2, wa, order[0]
        )

    settle([weights_out], mark)
    (w2,) = weights_out.result()
    pre_grad, bias_fc1 = env["run_pre_grad"](cot, slope, w2, order[0])
    grad_fc2 = dot(cot, hidden, TN).astype(BF)
    grad_fc1 = dot(normed2, pre_grad, TN).astype(BF)
    grad_ff = reorder_kernel([grad_fc1, grad_fc2], order[0], chips, False)
    grad_ff, mark = settle([], grad_ff, bias_fc1)
    own_ff = lax.psum_scatter(grad_ff, "dp", scatter_dimension=0, tiled=True, axis_index_groups=sets)
    first = [run_att(0, h) for h in range(groups)]
    part0, *sums0 = run_tail(0, first)
    part0, mark = settle([], part0, sums0[0])
    sent0 = env["to_owner"](0, part0)
    second = [run_att(1, 0)]
    sent0, _ = settle([], sent0, second[0][2])
    out0, grad0 = pair_add_kernel(order[0], part0, sent0)
    out0 = env["reduce_x"](0, out0)
    second += [run_att(1, h) for h in range(1, groups)]
    grad0, mark = settle([], grad0, second[-1][2])
    grad0 = env["reduce_x"](0, grad0)
    part1, *sums1 = run_tail(1, second)
    out0, grad0, part1, own_ff, mark = settle([], out0, grad0, part1, own_ff, sums1[0])
    sent1 = env["to_owner"](1, part1)
    bias_qkv = jnp.concatenate([a[2] + b[2] for a, b in zip(first, second)], axis=1)
    small = env["small_sums"]([a + b for a, b in zip(sums0, sums1)], bias_qkv, bias_fc1)
    grad_att, mark = att_weight_kernel(
        order[0], normed1, cot, [x[0] for x in (*first, *second)], [x[1] for x in (*first, *second)]
    )
    sent1, mark, small = settle([], sent1, mark, small)
    scattered = Scatter(ring, [grad_att])
    scattered.run()
    steps = [1 << k for k in range(dp.bit_length() - 1)]
    if steps:
        small = sum_step(small, "dp", dp, steps.pop(0))
    out1, grad1 = pair_add_kernel(order[0], part1, sent1)
    out1, grad1, mark, small = settle([scattered], out1, grad1, mark, small)
    out1 = env["reduce_x"](1, out1)
    middle = chips // 2 - 2
    for i in range(middle):
        scattered.run()
        if steps:
            small = sum_step(small, "dp", dp, steps.pop(0))
        if i == 0:
            own = own_kernel(order[0], [(part0, sent0), (part1, sent1)])
        values = [small, own] + ([out1] if i == middle - 1 else [])
        small, own, *out1_now = settle([scattered], *values)
    (out1,) = out1_now
    grad1 = env["reduce_x"](1, grad1)
    scattered.run()
    if steps:
        small = sum_step(small, "dp", dp, steps.pop(0))
    (small,) = settle([scattered], small)
    wide, cols = env["hidden_cols"], env["qkv_cols"]
    for step in steps:
        small = sum_step(small, "dp", dp, step)
    weights = share_weights(env, scattered.result(), (0, cols, wide))
    weights += share_weights(env, [own_ff], (0, wide, 2 * wide))
    parts = [(x, 0) for x in (own[0], out0, out1, own[1], grad0, grad1)]
    return dict(parts=parts, small=small, weights=weights)


def solution(mesh):
    both, weight = P(("dp", "tensor"), None), P("dp", "tensor")
    return jax.shard_map(
        functools.partial(shards, mesh.shape["dp"], mesh.shape["tensor"]),
        mesh=mesh,
        in_specs=(both, P("dp"), both, weight, P("tensor"), weight, P(), weight, P("tensor"), weight, P(), P(), P(), P(), P()),
        out_specs=(both, both, weight, P("tensor"), weight, P(), weight, P("tensor"), weight, P(), P(), P(), P(), P()),
        check_vma=False,
    )
```
